32 devices in a mesh: tp: 4 (over x, core), dp: 8 (over z, y).
Axes of the slice: x: 2, y: 2, z: 4, core: 2. Of those that a mesh axis runs over, the one named last changes fastest.
Arguments:
- block_input: bfloat16 [12288, 768], P('dp'), may hold values from -6 to 6
- pieces: int32 [48, 6], P('dp'), may hold values from 1 to 64, 256 in all within a row
- gain_one: float32 [768], replicated, may hold values from 0.1 to 1.9
- shift_one: float32 [768], replicated, may hold values from -1.8 to 1.8
- query_weight: bfloat16 [768, 768], P(None, 'tp'), may hold values from -0.4375 to 0.4375
- query_bias: float32 [768], P('tp'), may hold values from -3 to 3
- key_weight: bfloat16 [768, 768], P(None, 'tp'), may hold values from -0.21875 to 0.21875
- value_weight: bfloat16 [768, 768], P(None, 'tp'), may hold values from -0.21875 to 0.21875
- value_bias: float32 [768], P('tp'), may hold values from -3 to 3
- out_weight: bfloat16 [768, 768], P('tp'), may hold values from -0.875 to 0.875
- out_bias: float32 [768], replicated, may hold values from -1.8 to 1.8
- gain_two: float32 [768], replicated, may hold values from 0.1 to 1.9
- shift_two: float32 [768], replicated, may hold values from -1.8 to 1.8
- up_weight: bfloat16 [768, 3072], P(None, 'tp'), may hold values from -0.21875 to 0.21875
- up_bias: float32 [3072], P('tp'), may hold values from -3 to 3
- down_weight: bfloat16 [3072, 768], P('tp'), may hold values from -0.15625 to 0.15625
- down_bias: float32 [768], replicated, may hold values from -1.8 to 1.8
- cotangent: bfloat16 [12288, 768], P('dp'), may hold values from -6 to 6
Outputs:
- block_output: bfloat16 [12288, 768], P('dp')
- input_grad: float32 [12288, 768], P('dp')
- gain_one_grad: float32 [768], replicated
- shift_one_grad: float32 [768], replicated
- query_weight_grad: float32 [768, 768], P(None, 'tp')
- query_bias_grad: float32 [768], P('tp')
- key_weight_grad: float32 [768, 768], P(None, 'tp')
- value_weight_grad: float32 [768, 768], P(None, 'tp')
- value_bias_grad: float32 [768], P('tp')
- out_weight_grad: float32 [768, 768], P('tp')
- out_bias_grad: float32 [768], replicated
- gain_two_grad: float32 [768], replicated
- shift_two_grad: float32 [768], replicated
- up_weight_grad: float32 [768, 3072], P(None, 'tp')
- up_bias_grad: float32 [3072], P('tp')
- down_weight_grad: float32 [3072, 768], P('tp')
- down_bias_grad: float32 [768], replicated
The draws below stay inside these ranges and needn't reach their ends.
Inputs may be any that keep to these rules, and one draw needn't show every extreme that they name: `pieces`: row s lists, in order, the rows of each image packed into sequence s and, as its last entry, the rows of padding at the sequence's end; each row sums to 256, and its largest entry is 64.
All inputs are finite; a program needn't handle non-finite values.
Results may differ from the reference program's by a relative error of at most 0.012.
The reference program's roundings to bfloat16 on the way count: a program that leaves them out, or rounds other values in their place, can miss the bound.
Values may be sent and summed in bfloat16 or wider, within the bound.
No kernel may reach another device: no remote copies, remote signals or barrier semaphores. Data moves between devices by JAX's collectives and lax.ppermute only.
A program may use at most 128 MiB of HBM per device.

```python
import math
import jax
import jax.numpy as jnp
import numpy as np
from jax import lax

D = 768
HEADS = 12
HEAD = 64
FF = 3072
SEQ_LEN = 256
PIECES = 6
MOST = 64
SEQ_DEV = 6
SEQS = 48
TOKENS = 12288


def levels(rng, extent, split, low, high):
    loudness, own = 1.0, jax.random.fold_in(rng, 6)
    for axis_at, blocks in split:
        draws = jnp.exp(jax.random.uniform(jax.random.fold_in(own, axis_at), (blocks,), jnp.float32, low / len(split), high / len(split)))
        loudness = loudness * jnp.repeat(draws, extent[axis_at] // blocks).reshape([-1 if axis == axis_at else 1 for axis in range(len(extent))])
    return loudness


def profile(number_of, total, bound, skew):
    weights = [(1 << 20) // math.isqrt(grade ** skew) + 1 for grade in range(2, number_of + 1)]
    rest, holding = total - bound - (number_of - 1), [1] * (number_of - 1)
    while rest > 0:
        free = [i for i in range(number_of - 1) if holding[i] < bound]
        pool, budget = sum([weights[i] for i in free]), rest
        for i in free:
            extra = min(bound - holding[i], max(1, budget * weights[i] // pool), rest)
            holding[i] = holding[i] + extra
            rest = rest - extra
    return np.array([bound] + holding)


def ragged(stream_key, amount, total, most, lean):
    if amount == 2:
        one = jax.random.randint(stream_key, (), max(1, total - most), min(most, total - 1) + 1)
        return jnp.stack([one, total - one])
    sizes = jnp.asarray(profile(amount, total, most, lean), jnp.int32)
    pairs = (amount - 1) // 2
    donor, taker = sizes[1:1 + 2 * pairs:2], sizes[2:2 + 2 * pairs:2]
    margin = jnp.minimum(donor - 1, most - taker)
    shifted = jax.random.randint(jax.random.fold_in(stream_key, 1), (pairs,), 0, 1 << 20) % (margin + 1)
    sizes = sizes.at[1:1 + 2 * pairs:2].set(donor - shifted).at[2:2 + 2 * pairs:2].set(taker + shifted)
    return sizes[jax.random.permutation(jax.random.fold_in(stream_key, 2), amount)]


def gaussian(rng, dims, deviation, most, split=(), held_as=jnp.bfloat16):
    level = levels(rng, dims, split, -0.22, 0.18) if split else 1.0
    values = jax.random.normal(rng, dims, jnp.float32) * deviation * level
    return jnp.minimum(jnp.maximum(values, -most), most).astype(held_as)


def setup_inputs(seed: int = 0) -> dict:
    keys = jax.random.split(jax.random.key(seed), 19)
    return {
        "block_input": gaussian(keys[0], (TOKENS, D), 1.0, 6.0, ((0, 8),)),
        "pieces": jax.vmap(lambda own: ragged(own, PIECES, SEQ_LEN, MOST, 1))(jax.random.split(keys[1], SEQS)).reshape((SEQS, PIECES)).astype(jnp.int32),
        "gain_one": jnp.clip(1.0 + 0.18 * jax.random.normal(keys[2], (D,), jnp.float32), 0.1, 1.9),
        "shift_one": gaussian(keys[3], (D,), 0.3, 1.8, (), jnp.float32),
        "query_weight": gaussian(keys[4], (D, D), (D // 4) ** -0.5, 0.4375, ((1, 4),)),
        "query_bias": gaussian(keys[5], (D,), 0.5, 3.0, ((0, 4),), jnp.float32),
        "key_weight": gaussian(keys[6], (D, D), D ** -0.5, 0.21875, ((1, 4),)),
        "value_weight": gaussian(keys[7], (D, D), D ** -0.5, 0.21875, ((1, 4),)),
        "value_bias": gaussian(keys[8], (D,), 0.5, 3.0, ((0, 4),), jnp.float32),
        "out_weight": gaussian(keys[9], (D, D), (D // 16) ** -0.5, 0.875, ((0, 4),)),
        "out_bias": gaussian(keys[10], (D,), 0.3, 1.8, (), jnp.float32),
        "gain_two": jnp.clip(1.0 + 0.18 * jax.random.normal(keys[11], (D,), jnp.float32), 0.1, 1.9),
        "shift_two": gaussian(keys[12], (D,), 0.3, 1.8, (), jnp.float32),
        "up_weight": gaussian(keys[13], (D, FF), D ** -0.5, 0.21875, ((1, 4),)),
        "up_bias": gaussian(keys[14], (FF,), 0.5, 3.0, ((0, 4),), jnp.float32),
        "down_weight": gaussian(keys[15], (FF, D), (FF // 2) ** -0.5, 0.15625, ((0, 4),)),
        "down_bias": gaussian(keys[16], (D,), 0.3, 1.8, (), jnp.float32),
        "cotangent": gaussian(keys[17], (TOKENS, D), 1.0, 6.0, ((0, 8),)),
    }


EPS = 1e-06
SCALE = 0.125
NEG = -1000000000.0
ROOT_HALF = 0.7071067811865476

@jax.custom_vjp
def low(v):
    return lax.optimization_barrier(v.astype(jnp.bfloat16)).astype(jnp.float32)

@jax.custom_vjp
def low_back(v):
    return v

def low_keep(v):
    return (low(v), None)

def low_pass(kept, grad):
    return (grad,)

def back_keep(v):
    return (v, None)

def back_low(kept, grad):
    return (low(grad),)
low.defvjp(low_keep, low_pass)
low_back.defvjp(back_keep, back_low)

def segments_of(pieces):
    ends = jnp.cumsum(pieces, axis=-1).astype(jnp.int32)
    places = jnp.arange(SEQ_LEN, dtype=jnp.int32)
    segment = lax.optimization_barrier(jnp.sum((places[None, :, None] >= ends[:, None, :]).astype(jnp.int32), axis=-1)).astype(jnp.int32)
    return (segment, segment < PIECES - 1)

def layer_norm(values, gain, shift):
    centred = values - lax.optimization_barrier(jnp.mean(values, axis=-1, keepdims=True))
    spread = lax.optimization_barrier(jnp.mean(centred * centred, axis=-1, keepdims=True))
    return centred * lax.rsqrt(spread + EPS) * gain + shift

def product(left, right):
    return jnp.dot(left, right, precision=lax.Precision.HIGHEST)

def attend_group(items):
    query, key, value, segment, valid = items
    group = query.shape[0]
    query_heads = query.reshape(group, SEQ_LEN, HEADS, HEAD)
    key_heads = key.reshape(group, SEQ_LEN, HEADS, HEAD)
    value_heads = value.reshape(group, SEQ_LEN, HEADS, HEAD)
    scores = jnp.einsum('sqhd,skhd->shqk', query_heads, key_heads, precision=lax.Precision.HIGHEST) * SCALE
    scores = low_back(scores)
    allowed = (segment[:, :, None] == segment[:, None, :]) & valid[:, None, :] | jnp.eye(SEQ_LEN, dtype=jnp.bool_)[None]
    scores = jnp.where(allowed[:, None], scores, NEG)
    largest = lax.optimization_barrier(jnp.max(scores, axis=-1, keepdims=True))
    weights = jnp.exp(scores - largest)
    probs = weights / lax.optimization_barrier(jnp.sum(weights, axis=-1, keepdims=True))
    mixed = jnp.einsum('shqk,skhd->sqhd', low(probs), value_heads, precision=lax.Precision.HIGHEST)
    return mixed.reshape(group, SEQ_LEN, HEADS * HEAD)

def reference(block_input, pieces, gain_one, shift_one, query_weight, query_bias, key_weight, value_weight, value_bias, out_weight, out_bias, gain_two, shift_two, up_weight, up_bias, down_weight, down_bias, cotangent):
    segment, valid = segments_of(pieces)
    keep = valid.reshape(-1, 1).astype(jnp.float32)
    group_seqs = SEQ_DEV * 8

    def grouped(values):
        return values.reshape(-1, group_seqs, SEQ_LEN, D)

    def forward(inputs, g_one, s_one, w_query, b_query, w_key, w_value, b_value, w_out, b_out, g_two, s_two, w_up, b_up, w_down, b_down):
        normed = low(layer_norm(inputs, g_one, s_one))
        query = low(low_back(product(normed, w_query) + b_query))
        key = low(low_back(product(normed, w_key)))
        value = low(low_back(product(normed, w_value) + b_value))
        mixed = lax.map(jax.checkpoint(attend_group), (grouped(query), grouped(key), grouped(value), segment.reshape(-1, group_seqs, SEQ_LEN), valid.reshape(-1, group_seqs, SEQ_LEN)))
        mixed = low(low_back(mixed.reshape(-1, D)))
        branch = low_back(product(mixed, w_out) + b_out)
        middle = inputs + keep * branch
        normed_two = low(layer_norm(middle, g_two, s_two))
        hidden = low_back(product(normed_two, w_up) + b_up)
        active = low(0.5 * hidden * (1.0 + jax.scipy.special.erf(hidden * ROOT_HALF)))
        branch_two = low_back(product(active, w_down) + b_down)
        return middle + keep * branch_two
    floats = (block_input.astype(jnp.float32), gain_one, shift_one, query_weight.astype(jnp.float32), query_bias, key_weight.astype(jnp.float32), value_weight.astype(jnp.float32), value_bias, out_weight.astype(jnp.float32), out_bias, gain_two, shift_two, up_weight.astype(jnp.float32), up_bias, down_weight.astype(jnp.float32), down_bias)
    result, pullback = jax.vjp(forward, *floats)
    grads = pullback(cotangent.astype(jnp.float32))
    return (result.astype(jnp.bfloat16), grads[0], grads[1], grads[2], grads[3], grads[4], grads[5], grads[6], grads[7], grads[8], grads[9], grads[10], grads[11], grads[12], grads[13], grads[14], grads[15])
```

```python
import functools

import jax
import jax.numpy as jnp
from jax import lax
from jax.experimental import pallas as pl
from jax.experimental.pallas import tpu as pltpu
from jax.sharding import PartitionSpec as P

HEAD = 64
SEQ_LEN = 256
EPS = 1e-06
SCALE = 0.125
NEG = -1000000000.0
ROOT_HALF = 0.7071067811865476
INV_ROOT_TAU = 0.3989422804014327
F32 = jnp.float32
BF16 = jnp.bfloat16
VMEM_LIMIT = 48 * 1024 * 1024


def dot_nn(a, b):
    return lax.dot_general(a, b, (((1,), (0,)), ((), ())), preferred_element_type=F32)


def dot_nt(a, b):
    return lax.dot_general(a, b, (((1,), (1,)), ((), ())), preferred_element_type=F32)


def dot_tn(a, b):
    return lax.dot_general(a, b, (((0,), (0,)), ((), ())), preferred_element_type=F32)


def standardize(values):
    centred = values - jnp.mean(values, axis=-1, keepdims=True)
    spread = jnp.mean(centred * centred, axis=-1, keepdims=True)
    scaler = lax.rsqrt(spread + EPS)
    return centred * scaler, scaler


def norm_back(grad_normed, gain, normed, scaler):
    scaled = grad_normed * gain
    centred = scaled - jnp.mean(scaled, axis=-1, keepdims=True)
    return scaler * (centred - normed * jnp.mean(scaled * normed, axis=-1, keepdims=True))


def gelu_parts(hidden):
    cumul = 0.5 * (1.0 + lax.erf(hidden * ROOT_HALF))
    return hidden * cumul, cumul + hidden * (jnp.exp(-0.5 * hidden * hidden) * INV_ROOT_TAU)


def segment_at(pieces_ref, row, amount, shape, axis):
    place = lax.broadcasted_iota(jnp.int32, shape, axis)
    end = jnp.int32(0)
    segment = jnp.zeros(shape, jnp.int32)
    for k in range(amount):
        end = end + pieces_ref[row, k]
        segment = segment + (place >= end).astype(jnp.int32)
    return segment


def mask_bias(pieces_ref, row, amount):
    shape = (SEQ_LEN, SEQ_LEN)
    down = segment_at(pieces_ref, row, amount, shape, 0)
    across = segment_at(pieces_ref, row, amount, shape, 1)
    same = (down == across) & (across < amount - 1)
    diagonal = lax.broadcasted_iota(jnp.int32, shape, 0) == lax.broadcasted_iota(jnp.int32, shape, 1)
    return jnp.where(same | diagonal, 0.0, NEG).astype(F32)


def keep_rows(pieces_ref, row, amount):
    segment = segment_at(pieces_ref, row, amount, (SEQ_LEN, 1), 0)
    return (segment < amount - 1).astype(F32)


def head_lanes(shape):
    return lax.broadcasted_iota(jnp.int32, shape, 1) < HEAD


def attend(qkv_ref, bias, width):
    low_lanes = head_lanes((SEQ_LEN, 2 * HEAD))
    lane = lax.broadcasted_iota(jnp.int32, (SEQ_LEN, 2 * HEAD), 1)
    logs = jnp.zeros((SEQ_LEN, 2 * HEAD), F32)
    mixed = []
    for pair in range(width // (2 * HEAD)):
        at = pair * 2 * HEAD
        query = qkv_ref[:, at : at + 2 * HEAD]
        key = qkv_ref[:, width + at : width + at + 2 * HEAD]
        value = qkv_ref[:, 2 * width + at : 2 * width + at + 2 * HEAD]
        parts = []
        for side in range(2):
            mine = low_lanes if side == 0 else ~low_lanes
            scores = dot_nt(jnp.where(mine, query, jnp.zeros_like(query)), key) + bias
            largest = jnp.max(scores, axis=-1, keepdims=True)
            weights = jnp.exp(scores - largest)
            totals = jnp.sum(weights, axis=-1, keepdims=True)
            probs = (weights * (1.0 / totals)).astype(BF16)
            parts.append(dot_nn(probs, value))
            logs = jnp.where(lane == 2 * pair + side, largest + jnp.log(totals), logs)
        mixed.append(jnp.where(low_lanes, parts[0], parts[1]).astype(BF16))
    return jnp.concatenate(mixed, axis=1), logs


def forward_kernel(
    first, amount, shard, *refs
):
    if first:
        (base_ref, pieces_ref, x_ref, gain_ref, shift_ref, wa_ref, wb_ref, bias_ref,
         w_ref, normed_ref, qkv_ref, mixed_ref, logs_ref, part_ref) = refs
    else:
        (base_ref, pieces_ref, x_ref, normed_in_ref, part_in_ref, out_bias_ref, gain_ref, shift_ref,
         wa_ref, wb_ref, bias_ref, w_ref, qkv_ref, logs_ref, middle_ref, normed_ref) = refs
    step = pl.program_id(0)
    width = 2 * shard

    @pl.when(step == 0)
    def _():
        for k in range(4):
            w_ref[k * width : k * width + shard, :] = wa_ref[k * shard : (k + 1) * shard, :]
            w_ref[k * width + shard : (k + 1) * width, :] = wb_ref[k * shard : (k + 1) * shard, :]

    row = base_ref[0] + step
    if first:
        normed, _ = standardize(x_ref[...].astype(F32))
        lowered = (normed * gain_ref[...] + shift_ref[...]).astype(BF16)
        normed_ref[...] = lowered
    else:
        lowered = normed_in_ref[...]
    for k in range(3):
        proj = dot_nt(lowered, w_ref[k * width : (k + 1) * width, :]) + bias_ref[:, k * width : (k + 1) * width]
        proj = proj.astype(BF16)
        if k == 0:
            proj = proj * jnp.asarray(SCALE, BF16)
        qkv_ref[:, k * width : (k + 1) * width] = proj
    mixed, logs = attend(qkv_ref, mask_bias(pieces_ref, row, amount), width)
    logs_ref[...] = logs.T[: logs_ref.shape[0], :]
    part = dot_nn(mixed, w_ref[3 * width : 4 * width, :])
    if first:
        mixed_ref[...] = mixed
        part_ref[...] = part
    else:
        keep = keep_rows(pieces_ref, row, amount)
        middle = x_ref[...].astype(F32) + keep * ((part_in_ref[...] + part) + out_bias_ref[...])
        middle_ref[...] = middle
        normed, _ = standardize(middle)
        normed_ref[...] = (normed * gain_ref[...] + shift_ref[...]).astype(BF16)


def whole(shape):
    return pl.BlockSpec(shape, lambda *_: (0,) * len(shape))


def by_seq(cols):
    return pl.BlockSpec((SEQ_LEN, cols), lambda i, *_: (i, 0))


def from_base(cols):
    return pl.BlockSpec((SEQ_LEN, cols), lambda i, base, *_: (base[0] + i, 0))


def params():
    return pltpu.CompilerParams(vmem_limit_bytes=VMEM_LIMIT)


def cost(flops, moved, exps=0):
    return pl.CostEstimate(flops=int(flops), bytes_accessed=int(moved), transcendentals=int(exps))


def forward_half(first, base, pieces, x, gain, shift, wa, wb, bias, normed=None, part=None, out_bias=None):
    seqs, amount = pieces.shape[0] // 2, pieces.shape[1]
    d = x.shape[1]
    shard = wa.shape[0] // 4
    width = 2 * shard
    rows = seqs * SEQ_LEN
    if first:
        operands = (x, gain, shift, wa, wb, bias)
        in_specs = [from_base(d), whole((1, d)), whole((1, d)), whole(wa.shape), whole(wb.shape), whole(bias.shape)]
        outs = [((8 * shard, d), BF16), ((rows, d), BF16), ((rows, 3 * width), BF16), ((rows, width), BF16), ((seqs * 8, SEQ_LEN), F32), ((rows, d), F32)]
        out_specs = [whole((8 * shard, d)), by_seq(d), by_seq(3 * width), by_seq(width), pl.BlockSpec((8, SEQ_LEN), lambda i, *_: (i, 0)), by_seq(d)]
    else:
        operands = (x, normed, part, out_bias, gain, shift, wa, wb, bias)
        in_specs = [from_base(d), by_seq(d), by_seq(d), whole((1, d)), whole((1, d)), whole((1, d)), whole(wa.shape), whole(wb.shape), whole(bias.shape)]
        outs = [((8 * shard, d), BF16), ((rows, 3 * width), BF16), ((seqs * 8, SEQ_LEN), F32), ((rows, d), F32), ((rows, d), BF16)]
        out_specs = [whole((8 * shard, d)), by_seq(3 * width), pl.BlockSpec((8, SEQ_LEN), lambda i, *_: (i, 0)), by_seq(d), by_seq(d)]
    return pl.pallas_call(
        functools.partial(forward_kernel, first, amount, shard),
        grid_spec=pltpu.PrefetchScalarGridSpec(num_scalar_prefetch=2, grid=(seqs,), in_specs=in_specs, out_specs=out_specs),
        out_shape=[jax.ShapeDtypeStruct(s, t) for s, t in outs],
        compiler_params=params(),
        cost_estimate=cost(2 * rows * d * 4 * width + 4 * rows * SEQ_LEN * width, 4 * rows * d * 4, rows * SEQ_LEN * 6),
        name="forward_own" if first else "forward_other",
    )(base, pieces, *operands)


def mlp_kernel(amount, seq, base_ref, pieces_ref, n2_ref, cot_ref, upa_ref, upb_ref, bias_ref, dna_ref, dnb_ref,
               active_ref, gh_ref, gn2_ref, down_ref, gb_ref, sums_ref):
    keep = keep_rows(pieces_ref, base_ref[0] + seq, amount)
    branch = (keep * cot_ref[...].astype(F32)).astype(BF16)
    gb_ref[...] = branch
    n2 = n2_ref[...]
    ff = upa_ref.shape[1]
    block = 256 if ff % 256 == 0 else ff
    for side, (up_ref, dn_ref) in enumerate(((upa_ref, dna_ref), (upb_ref, dnb_ref))):
        for j in range(0, ff, block):
            at = slice(side * ff + j, side * ff + j + block)
            hidden = dot_nn(n2, up_ref[:, j : j + block]) + bias_ref[:, at]
            active, slope = gelu_parts(hidden)
            active_ref[:, at] = active.astype(BF16)
            grad_active = dot_nt(branch, dn_ref[j : j + block, :])
            grad_hidden = (grad_active * slope).astype(BF16)
            gh_ref[:, at] = grad_hidden
            sums_ref[:, at] = jnp.sum(grad_hidden.astype(F32), axis=0, keepdims=True)
    gn2_ref[...] = (dot_nt(gh_ref[:, :ff], upa_ref[...]) + dot_nt(gh_ref[:, ff:], upb_ref[...])).astype(BF16)
    down_ref[...] = (dot_nn(active_ref[:, :ff], dna_ref[...]) + dot_nn(active_ref[:, ff:], dnb_ref[...])).astype(BF16)


def mlp_chunk(seq, base, pieces, n2, cot, upa, upb, bias, dna, dnb):
    amount = pieces.shape[1]
    d, ff = upa.shape
    at_base = pl.BlockSpec((SEQ_LEN, d), lambda i, base, *_: (base[0] + seq, 0))
    fixed = pl.BlockSpec((SEQ_LEN, d), lambda i, *_: (seq, 0))
    outs = [((SEQ_LEN, 2 * ff), BF16), ((SEQ_LEN, 2 * ff), BF16), ((SEQ_LEN, d), BF16), ((SEQ_LEN, d), BF16), ((SEQ_LEN, d), BF16), ((1, 2 * ff), F32)]
    return pl.pallas_call(
        functools.partial(mlp_kernel, amount, seq),
        grid_spec=pltpu.PrefetchScalarGridSpec(
            num_scalar_prefetch=2, grid=(1,),
            in_specs=[fixed, at_base, whole(upa.shape), whole(upb.shape), whole(bias.shape), whole(dna.shape), whole(dnb.shape)],
            out_specs=[whole(s) for s, _ in outs]),
        out_shape=[jax.ShapeDtypeStruct(s, t) for s, t in outs],
        compiler_params=params(),
        cost_estimate=cost(16 * SEQ_LEN * d * ff, 10 * d * ff, SEQ_LEN * ff * 2),
        name="mlp",
    )(base, pieces, n2, cot, upa, upb, bias, dna, dnb)


def tn_kernel(count, add, *refs):
    out_ref = refs[-1]
    total = dot_tn(refs[0][...], refs[count][...])
    for k in range(1, count):
        total = total + dot_tn(refs[k][...], refs[count + k][...])
    if add:
        total = total + refs[2 * count][...].astype(F32)
    out_ref[...] = total.astype(out_ref.dtype)


def weight_grad(lefts, start, size, rights, add=None):
    count, d = len(lefts), rights[0][0].shape[1]
    block = 256 if size % 256 == 0 and start % 256 == 0 else size
    first = start // block
    in_specs = [pl.BlockSpec((SEQ_LEN, block), lambda j: (0, first + j))] * count
    in_specs += [pl.BlockSpec((SEQ_LEN, d), functools.partial(lambda at, j: (at, 0), at)) for _, at in rights]
    operands = list(lefts) + [array for array, _ in rights]
    if add is not None:
        in_specs.append(pl.BlockSpec((block, d), lambda j: (j, 0)))
        operands.append(add)
    return pl.pallas_call(
        functools.partial(tn_kernel, count, add is not None),
        grid=(size // block,),
        in_specs=in_specs,
        out_specs=pl.BlockSpec((block, d), lambda j: (j, 0)),
        out_shape=jax.ShapeDtypeStruct((size, d), BF16),
        compiler_params=params(),
        cost_estimate=cost(2 * count * SEQ_LEN * size * d, 2 * (count * SEQ_LEN * (size + d) + size * d)),
        name="weight_grad",
    )(*operands)


def attend_back(qkv_ref, gm_ref, logs_ref, bias, width, grads_ref):
    low_lanes = head_lanes((SEQ_LEN, 2 * HEAD))
    for pair in range(width // (2 * HEAD)):
        at = pair * 2 * HEAD
        here = [slice(k * width + at, k * width + at + 2 * HEAD) for k in range(3)]
        query, key, value = (qkv_ref[:, h] for h in here)
        grad_mixed = gm_ref[:, here[0]]
        pieces = []
        for side in range(2):
            mine = low_lanes if side == 0 else ~low_lanes
            zero = jnp.zeros_like(key)
            head = 2 * pair + side
            scores = dot_nt(jnp.where(mine, key, zero), query) + bias
            probs = jnp.exp(scores - logs_ref[head : head + 1, :])
            grad_probs = dot_nt(jnp.where(mine, value, zero), grad_mixed)
            inner = jnp.sum(grad_probs * probs, axis=0, keepdims=True)
            grad_scores = (probs * (grad_probs - inner)).astype(BF16)
            pieces.append((dot_tn(grad_scores, key) * SCALE, dot_nn(grad_scores, query), dot_nn(probs.astype(BF16), grad_mixed)))
        for k in range(3):
            grads_ref[:, here[k]] = jnp.where(low_lanes, pieces[0][k], pieces[1][k]).astype(BF16)


def backward_kernel(amount, seq, base_ref, pieces_ref, x_ref, cot_ref, middle_ref, own_ref, got_ref, gain_one_ref, gain_two_ref,
                    w_own_ref, w_oth_ref, qkv_own_ref, qkv_oth_ref, logs_own_ref, logs_oth_ref, mixed_ref,
                    grad_ref, all_ref, attn_ref, sums_ref, gm_ref, other_ref):
    row = base_ref[0] + seq
    width = mixed_ref.shape[1]
    keep = keep_rows(pieces_ref, row, amount)
    bias = mask_bias(pieces_ref, row, amount)
    cot = cot_ref[...].astype(F32)
    gn2 = own_ref[...].astype(F32) + got_ref[...].astype(F32)
    normed, scaler = standardize(middle_ref[...])
    sums_ref[3:4, :] = jnp.sum(gn2 * normed, axis=0, keepdims=True)
    sums_ref[4:5, :] = jnp.sum(gn2, axis=0, keepdims=True)
    sums_ref[5:6, :] = jnp.sum((keep * cot).astype(BF16).astype(F32), axis=0, keepdims=True)
    grad_middle = cot + norm_back(gn2, gain_two_ref[...], normed, scaler)
    attn = (keep * grad_middle).astype(BF16)
    attn_ref[...] = attn
    grad_ref[...] = grad_middle
    sums_ref[2:3, :] = jnp.sum(attn.astype(F32), axis=0, keepdims=True)
    gn1 = []
    for w_ref, qkv_ref, logs_ref, grads_ref in ((w_own_ref, qkv_own_ref, logs_own_ref, all_ref), (w_oth_ref, qkv_oth_ref, logs_oth_ref, other_ref)):
        gm_ref[...] = dot_nt(attn, w_ref[3 * width : 4 * width, :]).astype(BF16)
        attend_back(qkv_ref, gm_ref, logs_ref, bias, width, grads_ref)
        gn1.append(dot_nn(grads_ref[:, : 3 * width], w_ref[: 3 * width, :]))
    all_ref[:, 3 * width :] = mixed_ref[...]
    gn1 = gn1[0] + gn1[1]
    normed, scaler = standardize(x_ref[...].astype(F32))
    sums_ref[0:1, :] = jnp.sum(gn1 * normed, axis=0, keepdims=True)
    sums_ref[1:2, :] = jnp.sum(gn1, axis=0, keepdims=True)
    sums_ref[6:8, :] = jnp.zeros_like(sums_ref[6:8, :])
    sums_ref[6:7, :width] = jnp.sum(all_ref[:, :width].astype(F32), axis=0, keepdims=True)
    sums_ref[7:8, :width] = jnp.sum(all_ref[:, 2 * width : 3 * width].astype(F32), axis=0, keepdims=True)
    grad_ref[...] = grad_ref[...] + norm_back(gn1, gain_one_ref[...], normed, scaler)


def backward_chunk(seq, base, pieces, x, cot, middle, own, got, gain_one, gain_two, w_own, w_oth, qkv_own, qkv_oth, logs_own, logs_oth, mixed):
    amount, d = pieces.shape[1], x.shape[1]
    width = mixed.shape[1]
    at_base = pl.BlockSpec((SEQ_LEN, d), lambda i, base, *_: (base[0] + seq, 0))

    def fixed(cols, rows=SEQ_LEN):
        return pl.BlockSpec((rows, cols), lambda i, *_: (seq, 0))

    outs = [((SEQ_LEN, d), F32), ((SEQ_LEN, 4 * width), BF16), ((SEQ_LEN, d), BF16), ((8, d), F32)]
    return pl.pallas_call(
        functools.partial(backward_kernel, amount, seq),
        grid_spec=pltpu.PrefetchScalarGridSpec(
            num_scalar_prefetch=2, grid=(1,),
            in_specs=[at_base, at_base, fixed(d), whole((SEQ_LEN, d)), whole((SEQ_LEN, d)), whole((1, d)), whole((1, d)),
                      whole(w_own.shape), whole(w_oth.shape), fixed(3 * width), fixed(3 * width),
                      fixed(SEQ_LEN, 8), fixed(SEQ_LEN, 8), fixed(width)],
            out_specs=[whole(s) for s, _ in outs],
            scratch_shapes=[pltpu.VMEM((SEQ_LEN, width), BF16), pltpu.VMEM((SEQ_LEN, 3 * width), BF16)]),
        out_shape=[jax.ShapeDtypeStruct(s, t) for s, t in outs],
        compiler_params=params(),
        cost_estimate=cost(2 * SEQ_LEN * d * 8 * width + 20 * SEQ_LEN * SEQ_LEN * width, 20 * SEQ_LEN * d, SEQ_LEN * SEQ_LEN * 12),
        name="backward",
    )(base, pieces, x, cot, middle, own, got, gain_one, gain_two, w_own, w_oth, qkv_own, qkv_oth, logs_own, logs_oth, mixed)


def attn_grad_kernel(seqs, shard, *refs):
    lefts, attns, n1_ref, own_ref, oth_ref = refs[:seqs], refs[seqs : 2 * seqs], refs[2 * seqs], refs[-2], refs[-1]
    kind = pl.program_id(0)

    def put(total):
        own_ref[...] = total[:shard].astype(BF16)
        oth_ref[...] = total[shard:].astype(BF16)

    @pl.when(kind < 3)
    def _():
        put(sum(dot_tn(lefts[s][...], n1_ref[s * SEQ_LEN : (s + 1) * SEQ_LEN, :]) for s in range(seqs)))

    @pl.when(kind == 3)
    def _():
        put(sum(dot_tn(lefts[s][...], attns[s][...]) for s in range(seqs)))


def attn_grad(lefts, attns, n1):
    seqs = len(lefts)
    width, d = lefts[0].shape[1] // 4, n1.shape[1]
    shard = width // 2
    return pl.pallas_call(
        functools.partial(attn_grad_kernel, seqs, shard),
        grid=(4,),
        in_specs=[pl.BlockSpec((SEQ_LEN, width), lambda k: (0, k))] * seqs + [whole((SEQ_LEN, d))] * seqs + [whole(n1.shape)],
        out_specs=[pl.BlockSpec((shard, d), lambda k: (k, 0))] * 2,
        out_shape=[jax.ShapeDtypeStruct((4 * shard, d), BF16)] * 2,
        compiler_params=params(),
        cost_estimate=cost(8 * seqs * SEQ_LEN * width * d, 4 * seqs * SEQ_LEN * (4 * width + 2 * d)),
        name="attn_grad",
    )(*lefts, *attns, n1)


def output_kernel(amount, seq, base_ref, pieces_ref, middle_ref, own_ref, got_ref, bias_ref, out_ref):
    keep = keep_rows(pieces_ref, base_ref[0] + seq, amount)
    total = own_ref[...].astype(F32) + got_ref[...].astype(F32) + bias_ref[...]
    out_ref[...] = (middle_ref[...] + keep * total).astype(BF16)


def output_chunk(seq, base, pieces, middle, own, got, bias):
    d = middle.shape[1]
    return pl.pallas_call(
        functools.partial(output_kernel, pieces.shape[1], seq),
        grid_spec=pltpu.PrefetchScalarGridSpec(
            num_scalar_prefetch=2, grid=(1,),
            in_specs=[pl.BlockSpec((SEQ_LEN, d), lambda i, *_: (seq, 0)), whole((SEQ_LEN, d)), whole((SEQ_LEN, d)), whole((1, d))],
            out_specs=whole((SEQ_LEN, d))),
        out_shape=jax.ShapeDtypeStruct((SEQ_LEN, d), BF16),
        compiler_params=params(),
        cost_estimate=cost(4 * SEQ_LEN * d, 10 * SEQ_LEN * d),
        name="block_output",
    )(base, pieces, middle, own, got, bias)


def swap(size, bit):
    return [(i, i ^ bit) for i in range(size)]


def halving_sum(unit, groups):
    me = lax.axis_index("dp")
    bits = [1 << k for k in range(groups.bit_length() - 1)]
    for bit in bits:
        low = (me & bit) == 0
        half = unit.shape[0] // 2
        first, second = unit[:half], unit[half:]
        got = lax.ppermute(jnp.where(low, second, first), "dp", swap(groups, bit))
        unit = (jnp.where(low, first, second).astype(F32) + got.astype(F32)).astype(BF16)
    for bit in reversed(bits):
        low = (me & bit) == 0
        got = lax.ppermute(unit, "dp", swap(groups, bit))
        unit = jnp.where(low, jnp.concatenate([unit, got]), jnp.concatenate([got, unit]))
    return unit


def doubling_sum(values, groups):
    for k in range(groups.bit_length() - 1):
        values = values + lax.ppermute(values, "dp", swap(groups, 1 << k))
    return values


def in_three(values):
    high = lax.reduce_precision(values, 8, 7)
    rest = values - high
    mid = lax.reduce_precision(rest, 8, 7)
    return jnp.stack([high, mid, rest - mid]).astype(BF16)


def on_device(groups, tp, block_input, pieces, gain_one, shift_one, query_weight, query_bias, key_weight, value_weight, value_bias,
              out_weight, out_bias, gain_two, shift_two, up_weight, up_bias, down_weight, down_bias, cotangent):
    d = block_input.shape[1]
    shard = query_weight.shape[1]
    ff = up_weight.shape[1]
    seqs = pieces.shape[0] // 2
    core = lax.axis_index("tp") & 1
    base = (core * seqs).astype(jnp.int32).reshape(1)

    def other_core(values):
        return lax.ppermute(values, "tp", swap(tp, 1))

    def other_chip(values):
        return lax.ppermute(values, "tp", swap(tp, 2))

    def row(values):
        return values.reshape(1, -1)

    biases = jnp.pad(in_three(jnp.concatenate([query_bias, value_bias])), ((0, 13), (0, d - 2 * shard)))
    pack = jnp.concatenate([query_weight.T, key_weight.T, value_weight.T, out_weight, biases], axis=0)
    pack_b = other_core(pack)
    pack_x = other_chip(pack)
    pack_xb = other_core(pack_x)
    up_b = other_core(up_weight)
    down_b = other_core(down_weight)
    up_bias_b = other_core(up_bias)

    def half_bias(a, b):
        a = jnp.sum(a[4 * shard : 4 * shard + 3].astype(F32), axis=0)
        b = jnp.sum(b[4 * shard : 4 * shard + 3].astype(F32), axis=0)
        return row(jnp.concatenate([a[:shard], b[:shard], jnp.zeros((2 * shard,), F32), a[shard : 2 * shard], b[shard : 2 * shard]]))

    w_own, n1, qkv_own, mixed, logs_own, part = forward_half(
        True, base, pieces, block_input, row(gain_one), row(shift_one), pack[: 4 * shard], pack_b[: 4 * shard], half_bias(pack, pack_b))
    w_oth, qkv_oth, logs_oth, middle, n2 = forward_half(
        False, base, pieces, block_input, row(gain_two), row(shift_two), pack_x[: 4 * shard], pack_xb[: 4 * shard], half_bias(pack_x, pack_xb),
        normed=n1, part=part, out_bias=row(out_bias))

    bias_up = row(jnp.concatenate([up_bias, up_bias_b]))
    chunks = [mlp_chunk(s, base, pieces, n2, cotangent, up_weight, up_b, bias_up, down_weight, down_b) for s in range(seqs)]
    got_gn2 = [other_chip(c[2]) for c in chunks]
    got_down = [other_chip(c[3]) for c in chunks]
    actives, hiddens = [c[0] for c in chunks], [c[1] for c in chunks]
    n2_rows = [(n2, s) for s in range(seqs)]
    branch_rows = [(c[4], 0) for c in chunks]
    up_grad = other_core(weight_grad(hiddens, ff, ff, n2_rows))
    down_grad = other_core(weight_grad(actives, ff, ff, branch_rows))
    up_grad = halving_sum(weight_grad(hiddens, 0, ff, n2_rows, up_grad), groups)
    down_grad = halving_sum(weight_grad(actives, 0, ff, branch_rows, down_grad), groups)

    backs = [
        backward_chunk(s, base, pieces, block_input, cotangent, middle, chunks[s][2], got_gn2[s], row(gain_one), row(gain_two),
                       w_own, w_oth, qkv_own, qkv_oth, logs_own, logs_oth, mixed)
        for s in range(seqs)
    ]
    own, oth = attn_grad([b[1] for b in backs], [b[2] for b in backs], n1)
    attn = (own.astype(F32) + other_core(oth).astype(F32)).astype(BF16)
    attn = halving_sum(attn, groups)

    sums = sum(b[3] for b in backs)
    up_sums = sum(c[5] for c in chunks)

    def small(side):
        at = slice(side * shard, (side + 1) * shard)
        tail = jnp.concatenate([sums[6:7, at], sums[7:8, at], jnp.zeros((1, d - 2 * shard), F32)], axis=1)
        ups = up_sums[:, side * ff : (side + 1) * ff].reshape(-1, d)
        return jnp.concatenate([sums[:6], tail, ups], axis=0)

    totals = doubling_sum(small(0) + other_core(small(1)), groups)

    def both_cores(mine):
        theirs = other_core(mine)
        return jnp.where(core == 0, jnp.concatenate([mine, theirs]), jnp.concatenate([theirs, mine]))

    outputs = [output_chunk(s, base, pieces, middle, chunks[s][3], got_down[s], row(down_bias)) for s in range(seqs)]
    block_output = both_cores(jnp.concatenate(outputs))
    input_grad = both_cores(jnp.concatenate([b[0] for b in backs]))

    attn = attn.astype(F32)
    return (
        block_output,
        input_grad,
        totals[0],
        totals[1],
        attn[:shard].T,
        totals[6, :shard],
        attn[shard : 2 * shard].T,
        attn[2 * shard : 3 * shard].T,
        totals[6, shard : 2 * shard],
        attn[3 * shard :],
        totals[2],
        totals[3],
        totals[4],
        up_grad.astype(F32).T,
        totals[7:].reshape(-1),
        down_grad.astype(F32),
        totals[5],
    )


def solution(mesh):
    rows, cols, col, copied = P("dp", None), P(None, "tp"), P("tp"), P()
    return jax.shard_map(
        functools.partial(on_device, mesh.shape["dp"], mesh.shape["tp"]),
        mesh=mesh,
        in_specs=(rows, rows, copied, copied, cols, col, cols, cols, col, P("tp", None), copied, copied, copied, cols, col, P("tp", None), copied, rows),
        out_specs=(rows, rows, copied, copied, cols, col, cols, cols, col, P("tp", None), copied, copied, copied, cols, col, P("tp", None), copied),
        check_vma=False,
    )
```

```python
import functools

import jax
import jax.numpy as jnp
from jax import lax
from jax.experimental import pallas as pl
from jax.experimental.pallas import tpu as pltpu
from jax.sharding import PartitionSpec as P

HEAD = 64
SEQ_LEN = 256
EPS = 1e-06
SCALE = 0.125
NEG = -1000000000.0
ROOT_HALF = 0.7071067811865476
INV_ROOT_TAU = 0.3989422804014327
F32 = jnp.float32
BF16 = jnp.bfloat16
VMEM_LIMIT = 14 * 1024 * 1024


def dot_nn(a, b):
    return lax.dot_general(a, b, (((1,), (0,)), ((), ())), preferred_element_type=F32)


def dot_nt(a, b):
    return lax.dot_general(a, b, (((1,), (1,)), ((), ())), preferred_element_type=F32)


def dot_tn(a, b):
    return lax.dot_general(a, b, (((0,), (0,)), ((), ())), preferred_element_type=F32)


def standardize(values):
    centred = values - jnp.mean(values, axis=-1, keepdims=True)
    spread = jnp.mean(centred * centred, axis=-1, keepdims=True)
    scaler = lax.rsqrt(spread + EPS)
    return centred * scaler, scaler


def norm_back(grad_normed, gain, normed, scaler):
    scaled = grad_normed * gain
    centred = scaled - jnp.mean(scaled, axis=-1, keepdims=True)
    return scaler * (centred - normed * jnp.mean(scaled * normed, axis=-1, keepdims=True))


def gelu_parts(hidden):
    cumul = 0.5 * (1.0 + lax.erf(hidden * ROOT_HALF))
    return hidden * cumul, cumul + hidden * (jnp.exp(-0.5 * hidden * hidden) * INV_ROOT_TAU)


def segment_at(pieces_ref, row, amount, shape, axis):
    place = lax.broadcasted_iota(jnp.int32, shape, axis)
    end = jnp.int32(0)
    segment = jnp.zeros(shape, jnp.int32)
    for k in range(amount):
        end = end + pieces_ref[row, k]
        segment = segment + (place >= end).astype(jnp.int32)
    return segment


def mask_bias(pieces_ref, row, amount):
    shape = (SEQ_LEN, SEQ_LEN)
    down = segment_at(pieces_ref, row, amount, shape, 0)
    across = segment_at(pieces_ref, row, amount, shape, 1)
    same = (down == across) & (across < amount - 1)
    diagonal = lax.broadcasted_iota(jnp.int32, shape, 0) == lax.broadcasted_iota(jnp.int32, shape, 1)
    return jnp.where(same | diagonal, 0.0, NEG).astype(F32)


def keep_rows(pieces_ref, row, amount):
    segment = segment_at(pieces_ref, row, amount, (SEQ_LEN, 1), 0)
    return (segment < amount - 1).astype(F32)


def head_lanes(shape):
    return lax.broadcasted_iota(jnp.int32, shape, 1) < HEAD


def attend(qkv_ref, rows, bias, width):
    low_lanes = head_lanes((SEQ_LEN, 2 * HEAD))
    lane = lax.broadcasted_iota(jnp.int32, (SEQ_LEN, 2 * HEAD), 1)
    logs = jnp.zeros((SEQ_LEN, 2 * HEAD), F32)
    mixed = []
    for pair in range(width // (2 * HEAD)):
        at = pair * 2 * HEAD
        query = qkv_ref[rows, at : at + 2 * HEAD]
        key = qkv_ref[rows, width + at : width + at + 2 * HEAD]
        value = qkv_ref[rows, 2 * width + at : 2 * width + at + 2 * HEAD]
        parts = []
        for side in range(2):
            mine = low_lanes if side == 0 else ~low_lanes
            scores = dot_nt(jnp.where(mine, query, jnp.zeros_like(query)), key) + bias
            largest = jnp.max(scores, axis=-1, keepdims=True)
            weights = jnp.exp(scores - largest)
            totals = jnp.sum(weights, axis=-1, keepdims=True)
            probs = (weights * (1.0 / totals)).astype(BF16)
            parts.append(dot_nn(probs, value))
            logs = jnp.where(lane == 2 * pair + side, largest + jnp.log(totals), logs)
        mixed.append(jnp.where(low_lanes, parts[0], parts[1]).astype(BF16))
    return jnp.concatenate(mixed, axis=1), logs


def held(*_):
    return pl.BlockSpec(memory_space=pltpu.VMEM)


def seq_rows(seq):
    return pl.ds(pl.multiple_of(seq * SEQ_LEN, SEQ_LEN), SEQ_LEN)


def call(kernel, name, scalars, operands, outs, grid=(1,), scratch=()):
    return pl.pallas_call(
        kernel,
        grid_spec=pltpu.PrefetchScalarGridSpec(
            num_scalar_prefetch=len(scalars), grid=grid, in_specs=[held()] * len(operands), out_specs=[held()] * len(outs), scratch_shapes=list(scratch)),
        out_shape=[jax.ShapeDtypeStruct(shape, dtype) for shape, dtype in outs],
        compiler_params=pltpu.CompilerParams(vmem_limit_bytes=VMEM_LIMIT),
        cost_estimate=pl.CostEstimate(flops=1, bytes_accessed=1, transcendentals=0),
        name=name,
    )(*scalars, *operands)


def column_sum(values):
    return jnp.sum(values.reshape(values.shape[0] // 8, 8, values.shape[1]), axis=0)


VECTORS = 6
BITS = 2


def pack_kernel(shard, place_ref, wq_ref, wk_ref, wv_ref, wo_ref, qb_ref, vb_ref, up_bias_ref, *refs):
    vector_refs, (pack_ref, first_ref, last_ref, vectors_ref, up_ref) = refs[:VECTORS], refs[VECTORS:]
    d = pack_ref.shape[1]
    third = first_ref.shape[0]
    for k, ref in enumerate((wq_ref, wk_ref, wv_ref, wo_ref)):
        pack_ref[k * shard : (k + 1) * shard, :] = ref[...]
    zero = jnp.zeros((1, shard), F32)
    rest = jnp.concatenate([qb_ref[...].reshape(1, shard), zero, vb_ref[...].reshape(1, shard), zero], axis=1)
    rows = []
    for _ in range(3):
        part = rest.astype(BF16).astype(F32)
        rows.append(part)
        rest = rest - part
    rows.append(jnp.zeros((13, d), F32))
    pack_ref[4 * shard :, :] = jnp.concatenate(rows, axis=0).astype(BF16)
    first_ref[...] = pack_ref[pl.ds(pl.multiple_of(place_ref[BITS] * third, third), third), :]
    last_ref[...] = pack_ref[2 * third :, :]
    vectors_ref[...] = jnp.zeros_like(vectors_ref)
    for k, ref in enumerate(vector_refs):
        vectors_ref[k : k + 1, :] = ref[...].reshape(1, d)
    up_ref[...] = up_bias_ref[...].reshape(1, up_bias_ref.shape[0])


def pack_weights(place, wq, wk, wv, wo, qb, vb, up_bias, *vectors):
    shard, d = wo.shape
    third = 4 * shard // 3
    outs = [((4 * shard + 16, d), BF16), ((third, d), BF16), ((third + 16, d), BF16), ((8, d), F32), ((1, up_bias.shape[0]), F32)]
    return call(functools.partial(pack_kernel, shard), "pack_weights", (place,), (wq, wk, wv, wo, qb, vb, up_bias, *vectors), outs)


def spread_bias(a_ref, b_ref, shard):
    a = jnp.sum(a_ref[4 * shard :, :].astype(F32), axis=0, keepdims=True)
    b = jnp.sum(b_ref[4 * shard :, :].astype(F32), axis=0, keepdims=True)
    return a + jnp.concatenate([jnp.zeros((1, shard), F32), b[:, : 3 * shard]], axis=1)


def join_shards(w_ref, a_ref, b_ref, shard):
    width = 2 * shard
    for k in range(4):
        w_ref[k * width : k * width + shard, :] = a_ref[k * shard : (k + 1) * shard, :]
        w_ref[k * width + shard : (k + 1) * width, :] = b_ref[k * shard : (k + 1) * shard, :]


def project(lowered, w_ref, bias, qkv_ref, at, width):
    for k in range(3):
        proj = dot_nt(lowered, w_ref[k * width : (k + 1) * width, :])
        if k == 0:
            proj = (proj + bias[:, :width]).astype(BF16) * jnp.asarray(SCALE, BF16)
        elif k == 2:
            proj = proj + bias[:, width:]
        qkv_ref[at, k * width : (k + 1) * width] = proj.astype(BF16)


def project_kernel(shard, place_ref, x_ref, vectors_ref, a_ref, b_ref, w_ref, normed_ref, qkv_ref):
    step = pl.program_id(0)

    @pl.when(step == 0)
    def _():
        join_shards(w_ref, a_ref, b_ref, shard)

    normed, _ = standardize(x_ref[seq_rows(place_ref[0] + step), :].astype(F32))
    lowered = (normed * vectors_ref[0:1, :] + vectors_ref[1:2, :]).astype(BF16)
    at = seq_rows(step)
    normed_ref[at, :] = lowered
    project(lowered, w_ref, spread_bias(a_ref, b_ref, shard), qkv_ref, at, 2 * shard)


def project_own(rows, place, x, vectors, a, b):
    d = x.shape[1]
    shard = (a.shape[0] - 16) // 4
    outs = [((8 * shard, d), BF16), ((rows, d), BF16), ((rows, 6 * shard), BF16)]
    return call(functools.partial(project_kernel, shard), "project_own", (place,), (x, vectors, a, b), outs, (rows // SEQ_LEN,))


def attend_kernel(amount, width, place_ref, pieces_ref, qkv_ref, w_ref, mixed_ref, logs_ref, part_ref):
    step = pl.program_id(0)
    at = seq_rows(step)
    mixed, logs = attend(qkv_ref, at, mask_bias(pieces_ref, place_ref[0] + step, amount), width)
    logs_ref[pl.ds(pl.multiple_of(step * 8, 8), 8), :] = logs.T[:8, :]
    mixed_ref[at, :] = mixed
    part_ref[at, :] = dot_nn(mixed, w_ref[3 * width : 4 * width, :])


def attend_own(place, pieces, qkv, w):
    seqs, amount = pieces.shape[0] // 2, pieces.shape[1]
    width, d = w.shape[0] // 4, w.shape[1]
    rows = seqs * SEQ_LEN
    outs = [((rows, width), BF16), ((seqs * 8, SEQ_LEN), F32), ((rows, d), F32)]
    return call(functools.partial(attend_kernel, amount, width), "attend_own", (place, pieces), (qkv, w), outs, (seqs,))


def other_kernel(amount, shard, place_ref, pieces_ref, x_ref, normed_in_ref, part_in_ref, vectors_ref,
                 af_ref, ao_ref, al_ref, bf_ref, bo_ref, bl_ref, w_ref, qkv_ref, logs_ref, middle_ref, normed_ref,
                 a_ref, b_ref, sum_ref):
    step = pl.program_id(0)
    width = 2 * shard
    third = af_ref.shape[0]

    @pl.when(step == 0)
    def _():
        for to_ref, first_ref, other_ref, last_ref in ((a_ref, af_ref, ao_ref, al_ref), (b_ref, bf_ref, bo_ref, bl_ref)):
            to_ref[pl.ds(pl.multiple_of(place_ref[BITS] * third, third), third), :] = first_ref[...]
            to_ref[pl.ds(pl.multiple_of((1 - place_ref[BITS]) * third, third), third), :] = other_ref[...]
            to_ref[2 * third :, :] = last_ref[...]
        join_shards(w_ref, a_ref, b_ref, shard)

    row = place_ref[0] + step
    at = seq_rows(step)
    project(normed_in_ref[at, :], w_ref, spread_bias(a_ref, b_ref, shard), qkv_ref, at, width)
    mixed, logs = attend(qkv_ref, at, mask_bias(pieces_ref, row, amount), width)
    logs_ref[pl.ds(pl.multiple_of(step * 8, 8), 8), :] = logs.T[:8, :]
    sum_ref[...] = dot_nn(mixed, w_ref[3 * width : 4 * width, :])
    keep_row = keep_rows(pieces_ref, row, amount)
    middle = x_ref[seq_rows(row), :].astype(F32) + keep_row * ((part_in_ref[at, :] + sum_ref[...]) + vectors_ref[2:3, :])
    middle_ref[at, :] = middle
    normed, _ = standardize(middle)
    normed_ref[at, :] = (normed * vectors_ref[3:4, :] + vectors_ref[4:5, :]).astype(BF16)


def forward_other(place, pieces, x, normed, part, vectors, a_pieces, b_pieces):
    seqs, amount = pieces.shape[0] // 2, pieces.shape[1]
    d = x.shape[1]
    third = a_pieces[0].shape[0]
    shard = 3 * third // 4
    rows = seqs * SEQ_LEN
    outs = [((8 * shard, d), BF16), ((rows, 6 * shard), BF16), ((seqs * 8, SEQ_LEN), F32), ((rows, d), F32), ((rows, d), BF16)]
    return call(functools.partial(other_kernel, amount, shard), "forward_other", (place, pieces),
                (x, normed, part, vectors, *a_pieces, *b_pieces), outs, (seqs,),
                [pltpu.VMEM((3 * third + 16, d), BF16)] * 2 + [pltpu.VMEM((SEQ_LEN, d), F32)])


def mlp_kernel(amount, seq, place_ref, pieces_ref, n2_ref, cot_ref, ba_ref, bb_ref, upa_ref, upb_ref, dna_ref, dnb_ref,
               active_ref, gh_ref, gn2_ref, down_ref, gb_ref, sums_ref, n2_out_ref):
    row = place_ref[0] + seq
    keep = keep_rows(pieces_ref, row, amount)
    branch = (keep * cot_ref[seq_rows(row), :].astype(F32)).astype(BF16)
    gb_ref[...] = branch
    n2 = n2_ref[seq * SEQ_LEN : (seq + 1) * SEQ_LEN, :]
    n2_out_ref[...] = n2
    ff = upa_ref.shape[1]
    block = 256 if ff % 256 == 0 else ff
    for side, (up_ref, dn_ref, bias_ref) in enumerate(((upa_ref, dna_ref, ba_ref), (upb_ref, dnb_ref, bb_ref))):
        for j in range(0, ff, block):
            at = slice(side * ff + j, side * ff + j + block)
            hidden = dot_nn(n2, up_ref[:, j : j + block]) + bias_ref[:, j : j + block]
            active, slope = gelu_parts(hidden)
            active_ref[:, at] = active.astype(BF16)
            grad_active = dot_nt(branch, dn_ref[j : j + block, :])
            grad_hidden = (grad_active * slope).astype(BF16)
            gh_ref[:, at] = grad_hidden
            sums_ref[:, at] = jnp.sum(grad_hidden.astype(F32), axis=0, keepdims=True)
    gn2_ref[...] = (dot_nt(gh_ref[:, :ff], upa_ref[...]) + dot_nt(gh_ref[:, ff:], upb_ref[...])).astype(BF16)
    down_ref[...] = (dot_nn(active_ref[:, :ff], dna_ref[...]) + dot_nn(active_ref[:, ff:], dnb_ref[...])).astype(BF16)


def mlp_chunk(seq, place, pieces, n2, cot, bias, bias_b, upa, upb, dna, dnb):
    d, ff = upa.shape
    outs = [((SEQ_LEN, 2 * ff), BF16), ((SEQ_LEN, 2 * ff), BF16), ((SEQ_LEN, d), BF16), ((SEQ_LEN, d), BF16), ((SEQ_LEN, d), BF16), ((1, 2 * ff), F32), ((SEQ_LEN, d), BF16)]
    return call(functools.partial(mlp_kernel, pieces.shape[1], seq), "mlp", (place, pieces), (n2, cot, bias, bias_b, upa, upb, dna, dnb), outs)


def sent_kernel(count, side, *refs):
    out_ref = refs[-1]
    size = out_ref.shape[0]
    block = 256 if size % 256 == 0 else size
    for j in range(0, size, block):
        at = slice(side * size + j, side * size + j + block)
        total = sum(dot_tn(refs[k][:, at], refs[count + k][...]) for k in range(count))
        out_ref[j : j + block, :] = total.astype(BF16)


def grad_sent(side, lefts, rights):
    size, d = lefts[0].shape[1] // 2, rights[0].shape[1]
    return call(functools.partial(sent_kernel, len(lefts), side), "grad_sent", (), (*lefts, *rights), [((size, d), BF16)])[0]


def kept_kernel(count, bit, place_ref, *refs):
    add_ref, send_ref, keep_ref = refs[-3:]
    half = keep_ref.shape[0]
    for which, out_ref in enumerate((send_ref, keep_ref)):
        mine = place_ref[BITS + bit] if which else 1 - place_ref[BITS + bit]
        at = pl.ds(pl.multiple_of(mine * half, half), half)
        total = sum(dot_tn(refs[k][:, at], refs[count + k][...]) for k in range(count))
        out_ref[...] = (total + add_ref[at, :].astype(F32)).astype(BF16)


def grad_kept(bit, place, lefts, rights, add):
    half, d = lefts[0].shape[1] // 4, rights[0].shape[1]
    return call(functools.partial(kept_kernel, len(lefts), bit), "grad_kept", (place,), (*lefts, *rights, add), [((half, d), BF16)] * 2)


def attn_grad_kernel(seqs, shard, *refs):
    lefts, attns, n1_ref, own_ref, oth_ref = refs[:seqs], refs[seqs : 2 * seqs], refs[2 * seqs], refs[-2], refs[-1]
    width = 2 * shard
    for kind in range(4):
        at = slice(kind * width, (kind + 1) * width)
        rights = [attns[s][...] if kind == 3 else n1_ref[s * SEQ_LEN : (s + 1) * SEQ_LEN, :] for s in range(seqs)]
        total = sum(dot_tn(lefts[s][:, at], rights[s]) for s in range(seqs))
        own_ref[kind * shard : (kind + 1) * shard, :] = total[:shard].astype(BF16)
        oth_ref[kind * shard : (kind + 1) * shard, :] = total[shard:].astype(BF16)


def attn_grad(lefts, attns, n1):
    shard, d = lefts[0].shape[1] // 8, n1.shape[1]
    return call(functools.partial(attn_grad_kernel, len(lefts), shard), "attn_grad", (), (*lefts, *attns, n1), [((4 * shard, d), BF16)] * 2)


def attend_back(qkv_ref, rows, gm_ref, logs_ref, first, bias, width, grads_ref):
    low_lanes = head_lanes((SEQ_LEN, 2 * HEAD))
    for pair in range(width // (2 * HEAD)):
        at = pair * 2 * HEAD
        here = [slice(k * width + at, k * width + at + 2 * HEAD) for k in range(3)]
        query, key, value = (qkv_ref[rows, h] for h in here)
        grad_mixed = gm_ref[:, here[0]]
        pieces = []
        for side in range(2):
            mine = low_lanes if side == 0 else ~low_lanes
            zero = jnp.zeros_like(key)
            head = 2 * pair + side
            scores = dot_nt(jnp.where(mine, key, zero), query) + bias
            probs = jnp.exp(scores - logs_ref[first + head : first + head + 1, :])
            grad_probs = dot_nt(jnp.where(mine, value, zero), grad_mixed)
            inner = jnp.sum(grad_probs * probs, axis=0, keepdims=True)
            grad_scores = (probs * (grad_probs - inner)).astype(BF16)
            pieces.append((dot_tn(grad_scores, key) * SCALE, dot_nn(grad_scores, query), dot_nn(probs.astype(BF16), grad_mixed)))
        for k in range(3):
            grads_ref[:, here[k]] = jnp.where(low_lanes, pieces[0][k], pieces[1][k]).astype(BF16)


def own_back_kernel(amount, seq, place_ref, pieces_ref, cot_ref, middle_ref, own_ref, got_ref, vectors_ref, qkv_ref, logs_ref, mixed_ref, w_ref,
                    grad_ref, all_ref, attn_ref, part_ref, sums_ref, gm_ref):
    row = place_ref[0] + seq
    width = mixed_ref.shape[1]
    d = cot_ref.shape[1]
    keep_all = keep_rows(pieces_ref, row, amount)
    sums = [jnp.zeros((8, d), F32)] * 4
    block = 32
    for r in range(0, SEQ_LEN, block):
        at = slice(r, r + block)
        keep = keep_all[at]
        cot = cot_ref[pl.ds(pl.multiple_of(row * SEQ_LEN + r, block), block), :].astype(F32)
        gn2 = own_ref[at, :].astype(F32) + got_ref[at, :].astype(F32)
        normed, scaler = standardize(middle_ref[seq * SEQ_LEN + r : seq * SEQ_LEN + r + block, :])
        grad_middle = cot + norm_back(gn2, vectors_ref[3:4, :], normed, scaler)
        attn = (keep * grad_middle).astype(BF16)
        attn_ref[at, :] = attn
        grad_ref[at, :] = grad_middle
        terms = (attn.astype(F32), gn2 * normed, gn2, (keep * cot).astype(BF16).astype(F32))
        sums = [s + column_sum(t) for s, t in zip(sums, terms)]
    sums_ref[...] = jnp.zeros_like(sums_ref)
    for k in range(4):
        sums_ref[2 + k : 3 + k, :] = jnp.sum(sums[k], axis=0, keepdims=True)
    gm_ref[...] = dot_nt(attn_ref[...], w_ref[3 * width : 4 * width, :]).astype(BF16)
    rows = slice(seq * SEQ_LEN, (seq + 1) * SEQ_LEN)
    attend_back(qkv_ref, rows, gm_ref, logs_ref, 8 * seq, mask_bias(pieces_ref, row, amount), width, all_ref)
    part_ref[...] = dot_nn(all_ref[:, : 3 * width], w_ref[: 3 * width, :])
    all_ref[:, 3 * width :] = mixed_ref[rows, :]
    sums_ref[6:7, :width] = jnp.sum(all_ref[:, :width].astype(F32), axis=0, keepdims=True)
    sums_ref[7:8, :width] = jnp.sum(all_ref[:, 2 * width : 3 * width].astype(F32), axis=0, keepdims=True)


def own_back(seq, place, pieces, cot, middle, own, got, vectors, qkv, logs, mixed, w):
    d, width = cot.shape[1], mixed.shape[1]
    outs = [((SEQ_LEN, d), F32), ((SEQ_LEN, 4 * width), BF16), ((SEQ_LEN, d), BF16), ((SEQ_LEN, d), F32), ((8, d), F32)]
    return call(functools.partial(own_back_kernel, pieces.shape[1], seq), "own_back", (place, pieces),
                (cot, middle, own, got, vectors, qkv, logs, mixed, w), outs, scratch=[pltpu.VMEM((SEQ_LEN, width), BF16)])


def other_back_kernel(amount, seq, place_ref, pieces_ref, x_ref, grad_in_ref, attn_ref, part_ref, vectors_ref, qkv_ref, logs_ref, w_ref,
                      grad_ref, sums_ref, gm_ref, all_ref, sum_ref):
    row = place_ref[0] + seq
    width = gm_ref.shape[1]
    d = x_ref.shape[1]
    bias = mask_bias(pieces_ref, row, amount)
    gm_ref[...] = dot_nt(attn_ref[...], w_ref[3 * width : 4 * width, :]).astype(BF16)
    rows = slice(seq * SEQ_LEN, (seq + 1) * SEQ_LEN)
    attend_back(qkv_ref, rows, gm_ref, logs_ref, 8 * seq, bias, width, all_ref)
    sum_ref[...] = dot_nn(all_ref[...], w_ref[: 3 * width, :])
    sums = [jnp.zeros((8, d), F32)] * 2
    block = 32
    for r in range(0, SEQ_LEN, block):
        at = slice(r, r + block)
        gn1 = part_ref[at, :] + sum_ref[at, :]
        normed, scaler = standardize(x_ref[pl.ds(pl.multiple_of(row * SEQ_LEN + r, block), block), :].astype(F32))
        grad_ref[at, :] = grad_in_ref[at, :] + norm_back(gn1, vectors_ref[0:1, :], normed, scaler)
        sums = [s + column_sum(t) for s, t in zip(sums, (gn1 * normed, gn1))]
    sums_ref[...] = jnp.zeros_like(sums_ref)
    for k in range(2):
        sums_ref[k : k + 1, :] = jnp.sum(sums[k], axis=0, keepdims=True)


def other_back(seq, place, pieces, x, grad_in, attn, part, vectors, qkv, logs, w):
    d, width = x.shape[1], w.shape[0] // 4
    outs = [((SEQ_LEN, d), F32), ((8, d), F32)]
    return call(functools.partial(other_back_kernel, pieces.shape[1], seq), "other_back", (place, pieces),
                (x, grad_in, attn, part, vectors, qkv, logs, w), outs,
                scratch=[pltpu.VMEM((SEQ_LEN, width), BF16), pltpu.VMEM((SEQ_LEN, 3 * width), BF16), pltpu.VMEM((SEQ_LEN, d), F32)])


def output_kernel(amount, seqs, place_ref, pieces_ref, middle_ref, vectors_ref, *refs):
    out_ref = refs[-1]
    for seq in range(seqs):
        keep_all = keep_rows(pieces_ref, place_ref[0] + seq, amount)
        block = 64
        for r in range(0, SEQ_LEN, block):
            at = slice(seq * SEQ_LEN + r, seq * SEQ_LEN + r + block)
            total = refs[seq][r : r + block, :].astype(F32) + refs[seqs + seq][r : r + block, :].astype(F32) + vectors_ref[5:6, :]
            out_ref[at, :] = (middle_ref[at, :] + keep_all[r : r + block] * total).astype(BF16)


def output_rows(place, pieces, middle, vectors, owns, gots):
    return call(functools.partial(output_kernel, pieces.shape[1], len(owns)), "block_output", (place, pieces),
                (middle, vectors, *owns, *gots), [(middle.shape, BF16)])[0]


def both_kernel(count, place_ref, *refs):
    out_ref, sems = refs[-2:]
    size = refs[0].shape[0]
    copies = []
    for k in range(2 * count):
        at = (place_ref[1] if k < count else 1 - place_ref[1]) * count + k % count
        copies.append(pltpu.make_async_copy(refs[k], out_ref.at[pl.ds(pl.multiple_of(at * size, size), size)], sems.at[k]))
        copies[-1].start()
    for copy in copies:
        copy.wait()


def both_cores(place, mine, theirs):
    count = len(mine)
    rows, d = mine[0].shape
    return pl.pallas_call(
        functools.partial(both_kernel, count),
        grid_spec=pltpu.PrefetchScalarGridSpec(
            num_scalar_prefetch=1, grid=(1,), in_specs=[held()] * (2 * count), out_specs=pl.BlockSpec(memory_space=pl.ANY),
            scratch_shapes=[pltpu.SemaphoreType.DMA((2 * count,))]),
        out_shape=jax.ShapeDtypeStruct((2 * count * rows, d), mine[0].dtype),
        compiler_params=pltpu.CompilerParams(vmem_limit_bytes=VMEM_LIMIT),
        cost_estimate=pl.CostEstimate(flops=1, bytes_accessed=1, transcendentals=0),
        name="both_cores",
    )(place, *mine, *theirs)


def swap(size, bit):
    return [(i, i ^ bit) for i in range(size)]


def tie(values, *after):
    return lax.optimization_barrier((values, after))[0]


def split_kernel(bits, place_ref, own_ref, got_ref, *out_refs):
    size = own_ref.shape[0] // 4
    for k in range(2):
        for which, out_ref in enumerate(out_refs[2 * k : 2 * k + 2]):
            bit = place_ref[BITS + bits[k]] if which else 1 - place_ref[BITS + bits[k]]
            at = pl.ds(pl.multiple_of(2 * k * size + bit * size, size), size)
            out_ref[...] = (own_ref[at, :].astype(F32) + got_ref[at, :].astype(F32)).astype(BF16)


def split_units(bits, place, own, got):
    rows, d = own.shape
    outs = [((rows // 4, d), BF16)] * 4
    return call(functools.partial(split_kernel, bits), "split_units", (place,), (own, got), outs)


def merge_kernel(at, place_ref, keep_ref, got_ref, send_ref, out_ref):
    size = out_ref.shape[0]
    for which, ref in enumerate((send_ref, out_ref)):
        bit = place_ref[BITS + at] if which else 1 - place_ref[BITS + at]
        rows = pl.ds(pl.multiple_of(bit * size, size), size)
        ref[...] = (keep_ref[rows, :].astype(F32) + got_ref[rows, :].astype(F32)).astype(BF16)


def merge(bit, place, keep, got):
    rows, d = keep.shape
    half = rows // 2
    if half % 16:
        total = (keep.astype(F32) + got.astype(F32)).astype(BF16)
        low = place[BITS + bit] == 0
        return jnp.where(low, total[half:], total[:half]), jnp.where(low, total[:half], total[half:])
    return call(functools.partial(merge_kernel, bit), "merge", (place,), (keep, got), [((half, d), BF16)] * 2)


def add_kernel(keep_ref, got_ref, out_ref):
    out_ref[...] = (keep_ref[...].astype(F32) + got_ref[...].astype(F32)).astype(out_ref.dtype)


def add(keep, got):
    return call(add_kernel, "add", (), (keep, got), [(keep.shape, keep.dtype)])[0]


def grow_kernel(at, place_ref, keep_ref, got_ref, out_ref):
    size = keep_ref.shape[0]
    out_ref[pl.ds(pl.multiple_of(place_ref[BITS + at] * size, size), size), :] = keep_ref[...]
    out_ref[pl.ds(pl.multiple_of((1 - place_ref[BITS + at]) * size, size), size), :] = got_ref[...]


def grow(bit, place, keep, got):
    rows, d = keep.shape
    if rows % 16:
        return jnp.where(place[BITS + bit] == 0, jnp.concatenate([keep, got]), jnp.concatenate([got, keep]))
    return call(functools.partial(grow_kernel, bit), "grow", (place,), (keep, got), [((2 * rows, d), BF16)])[0]


def up_kernel(at, place_ref, keep_ref, got_ref, out_ref):
    size = keep_ref.shape[0]
    out_ref[:, pl.ds(pl.multiple_of(place_ref[BITS + at] * size, 128), size)] = keep_ref[...].astype(F32).T
    out_ref[:, pl.ds(pl.multiple_of((1 - place_ref[BITS + at]) * size, 128), size)] = got_ref[...].astype(F32).T


def down_kernel(at, place_ref, keep_ref, got_ref, out_ref):
    size = keep_ref.shape[0]
    out_ref[pl.ds(pl.multiple_of(place_ref[BITS + at] * size, size), size), :] = keep_ref[...].astype(F32)
    out_ref[pl.ds(pl.multiple_of((1 - place_ref[BITS + at]) * size, size), size), :] = got_ref[...].astype(F32)


def finish(kernel, name, bit, shape, place, keep, got):
    return call(functools.partial(kernel, bit), name, (place,), (keep, got), [(shape, F32)])[0]


def attn_kernel(bits, place_ref, a_ref, a_got_ref, b_ref, b_got_ref, *out_refs):
    for k, (keep_ref, got_ref) in enumerate(((a_ref, a_got_ref), (b_ref, b_got_ref))):
        mine = place_ref[BITS + bits[k]] == 0
        keep, got = keep_ref[...].astype(F32), got_ref[...].astype(F32)
        out_refs[2 * k][...] = jnp.where(mine, keep, got)
        out_refs[2 * k + 1][...] = jnp.where(mine, got, keep)


def finish_attn(bits, place, a, a_got, b, b_got):
    outs = [(a.shape, F32)] * 4
    return call(functools.partial(attn_kernel, bits), "finish_attn", (place,), (a, a_got, b, b_got), outs)


class Unit:
    def __init__(self, groups, order, place, send, keep):
        self.groups, self.order, self.place = groups, order, place
        self.send, self.keep, self.step = send, keep, 0

    def start(self):
        count = len(self.order)
        at = self.step if self.step < count else 2 * count - 1 - self.step
        self.got = lax.ppermute(self.send, "dp", swap(self.groups, 1 << self.order[at]))

    def take(self):
        count = len(self.order)
        if self.step < count - 1:
            self.send, self.keep = merge(self.order[self.step + 1], self.place, self.keep, self.got)
        elif self.step == count - 1:
            self.keep = add(self.keep, self.got)
            self.send = self.keep
        elif self.step < 2 * count - 1:
            self.keep = grow(self.order[2 * count - 1 - self.step], self.place, self.keep, self.got)
            self.send = self.keep
        self.step += 1


class Chain:
    def __init__(self):
        self.last = ()

    def run(self, kernel, *args, need=()):
        args = tie(args, self.last, need)
        out = kernel(*args)
        self.last = out
        return out

    def after(self, values):
        return tie(values, self.last)

    def take(self, *units):
        for unit in units:
            unit.keep, unit.got = tie((unit.keep, unit.got), self.last)
            unit.take()
            self.last = unit.keep

    def start(self, *units):
        for unit in units:
            unit.send = tie(unit.send, self.last)
            unit.start()


def small_kernel(seqs, shard, *refs):
    own, oth, ups = refs[:seqs], refs[seqs : 2 * seqs], refs[2 * seqs : 3 * seqs]
    total = sum(r[...] for r in own) + sum(r[...] for r in oth)
    up = sum(r[...] for r in ups)
    d = total.shape[1]
    ff = up.shape[1] // 2
    for side, out_ref in enumerate(refs[3 * seqs :]):
        out_ref[0:6, :] = total[0:6]
        at = slice(side * shard, (side + 1) * shard)
        out_ref[6:7, :] = jnp.concatenate([total[6:7, at], total[7:8, at], jnp.zeros((1, d - 2 * shard), F32)], axis=1)
        for k in range(ff // d):
            out_ref[7 + k : 8 + k, :] = up[:, side * ff + k * d : side * ff + (k + 1) * d]


def small_sums(shard, own, oth, ups):
    seqs, d = len(own), own[0].shape[1]
    rows = 7 + ups[0].shape[1] // 2 // d
    operands = [*own, *oth, *ups]
    return call(functools.partial(small_kernel, seqs, shard), "small_sums", (), operands, [((rows, d), F32)] * 2)


def on_device(groups, tp, block_input, pieces, gain_one, shift_one, query_weight, query_bias, key_weight, value_weight, value_bias,
              out_weight, out_bias, gain_two, shift_two, up_weight, up_bias, down_weight, down_bias, cotangent):
    d = block_input.shape[1]
    shard = query_weight.shape[1]
    ff = up_weight.shape[1]
    seqs = pieces.shape[0] // 2
    core = lax.axis_index("tp") & 1
    group = lax.axis_index("dp")
    bits = list(range(groups.bit_length() - 1))
    place = jnp.stack([core * seqs, core] + [(group >> bit) & 1 for bit in bits]).astype(jnp.int32)
    orders = [bits, bits[1:] + bits[:1]]
    first_bits = [order[0] for order in orders]

    def other_core(values):
        return lax.ppermute(values, "tp", swap(tp, 1))

    def other_chip(values):
        return lax.ppermute(values, "tp", swap(tp, 2))

    def next_group(values):
        return lax.ppermute(values, "dp", swap(groups, 1))

    chain = Chain()
    pack, first, last, vectors, up_row = chain.run(
        pack_weights, place, query_weight.T, key_weight.T, value_weight.T, out_weight, query_bias, value_bias, up_bias,
        gain_one, shift_one, out_bias, gain_two, shift_two, down_bias)
    pack_b = other_core(pack)
    first = other_chip(first)
    last = other_chip(last)
    up_b = other_core(up_weight)
    down_b = other_core(down_weight)
    up_row_b = other_core(up_row)

    w_own, n1, qkv_own = chain.run(functools.partial(project_own, seqs * SEQ_LEN), place, block_input, vectors, pack, pack_b)
    second = next_group(chain.after(first))
    mixed, logs_own, part = chain.run(attend_own, place, pieces, qkv_own, w_own, need=(first,))
    got = chain.after((first, second, last))
    w_oth, qkv_oth, logs_oth, middle, n2 = chain.run(
        forward_other, place, pieces, block_input, n1, part, vectors, got, [other_core(g) for g in got])

    chunks, got_gn2 = [], []
    for s in range(seqs):
        chunks.append(chain.run(functools.partial(mlp_chunk, s), place, pieces, n2, cotangent, up_row, up_row_b, up_weight, up_b, down_weight, down_b))
        got_gn2.append(other_chip(chunks[-1][2]))
    actives, hiddens, branches = ([c[k] for c in chunks] for k in (0, 1, 4))

    n2s = [c[6] for c in chunks]
    up_sent = chain.run(functools.partial(grad_sent, 1), hiddens, n2s, need=got_gn2[:1])
    up_got = other_core(up_sent)
    down_sent = chain.run(functools.partial(grad_sent, 1), actives, branches)
    down_got = other_core(down_sent)
    up = chain.run(functools.partial(grad_kept, orders[0][0]), place, hiddens, n2s, up_got)
    up = Unit(groups, orders[0], place, *up)
    up.start()
    down = chain.run(functools.partial(grad_kept, orders[1][0]), place, actives, branches, down_got)
    down = Unit(groups, orders[1], place, *down)
    down.start()

    owns, downs = [], []
    for s in range(seqs):
        owns.append(chain.run(functools.partial(own_back, s), place, pieces, cotangent, middle, chunks[s][2], got_gn2[s], vectors,
                              qkv_own, logs_own, mixed, w_own))
    chain.take(up, down)
    chain.start(up, down)
    own, oth = chain.run(attn_grad, [o[1] for o in owns], [o[2] for o in owns], n1)
    theirs = other_core(oth)
    downs.append(other_chip(chain.after(chunks[0][3])))

    others = []

    def back(s, need=()):
        others.append(chain.run(functools.partial(other_back, s), place, pieces, block_input, owns[s][0], owns[s][2], owns[s][3], vectors,
                                qkv_oth, logs_oth, w_oth, need=need))

    back(0)
    halves = chain.run(functools.partial(split_units, first_bits), place, own, theirs)
    units = [Unit(groups, order, place, *halves[2 * k : 2 * k + 2]) for k, order in enumerate(orders)]
    chain.start(*units)
    chain.take(up)
    chain.start(up)
    downs.append(other_chip(chain.after(chunks[1][3])))
    back(1, need=downs[:1])
    chain.take(down)
    chain.start(down)
    chain.take(*units)
    chain.start(*units)
    chain.take(up)
    chain.start(up)
    downs.append(other_chip(chain.after(chunks[2][3])))
    back(2, need=downs[:2])
    more = chain.run(functools.partial(small_sums, shard), [o[4] for o in owns], [o[1] for o in others], [c[5] for c in chunks], need=downs)
    totals = more[0]
    small_got = other_core(more[1])
    grad_own = [o[0] for o in others]
    grad_got = [other_core(g) for g in grad_own]

    for step in range(2 * len(bits) - 1 - units[0].step):
        chain.take(*units)
        chain.start(*units)
        left = [u for u in (up, down) if u.step < 2 * len(bits) - 1]
        chain.take(*left)
        chain.start(*left)
        if step <= len(bits):
            totals = chain.run(add, totals, small_got)
            if step < len(bits):
                small_got = lax.ppermute(totals, "dp", swap(groups, 1 << bits[step]))
        if step == 0:
            out_own = chain.run(output_rows, place, pieces, middle, vectors, [c[3] for c in chunks], downs)
            out_got = other_core(out_own)
        elif step == 1:
            input_grad = chain.run(both_cores, place, grad_own, grad_got)
        elif step == 2:
            block_output = chain.run(both_cores, place, [out_own], [out_got])
    up_grad = chain.run(functools.partial(finish, up_kernel, "finish_up", up.order[0], (d, ff)), place, up.keep, up.got)
    down_grad = chain.run(functools.partial(finish, down_kernel, "finish_down", down.order[0], (ff, d)), place, down.keep, down.got)
    attn = chain.run(functools.partial(finish_attn, first_bits), place, units[0].keep, units[0].got, units[1].keep, units[1].got)
    return (
        block_output,
        input_grad,
        totals[0],
        totals[1],
        attn[0].T,
        totals[6, :shard],
        attn[1].T,
        attn[2].T,
        totals[6, shard : 2 * shard],
        attn[3],
        totals[2],
        totals[3],
        totals[4],
        up_grad,
        totals[7:].reshape(-1),
        down_grad,
        totals[5],
    )


def solution(mesh):
    rows, cols, col, copied = P("dp", None), P(None, "tp"), P("tp"), P()
    return jax.shard_map(
        functools.partial(on_device, mesh.shape["dp"], mesh.shape["tp"]),
        mesh=mesh,
        in_specs=(rows, rows, copied, copied, cols, col, cols, cols, col, P("tp", None), copied, copied, copied, cols, col, P("tp", None), copied, rows),
        out_specs=(rows, rows, copied, copied, cols, col, cols, cols, col, P("tp", None), copied, copied, copied, cols, col, P("tp", None), copied),
        check_vma=False,
    )
```

```python
import functools

import jax
import jax.numpy as jnp
from jax import lax
from jax.experimental import pallas as pl
from jax.experimental.pallas import tpu as pltpu
from jax.sharding import PartitionSpec as P

HEAD = 64
SEQ_LEN = 256
EPS = 1e-06
SCALE = 0.125
NEG = -1000000000.0
ROOT_HALF = 0.7071067811865476
INV_ROOT_TAU = 0.3989422804014327
F32 = jnp.float32
BF16 = jnp.bfloat16
VMEM_LIMIT = 14 * 1024 * 1024
FETCH_LIMIT = 60 * 1024 * 1024


def dot_nn(a, b):
    return lax.dot_general(a, b, (((1,), (0,)), ((), ())), preferred_element_type=F32)


def dot_nt(a, b):
    return lax.dot_general(a, b, (((1,), (1,)), ((), ())), preferred_element_type=F32)


def dot_tn(a, b):
    return lax.dot_general(a, b, (((0,), (0,)), ((), ())), preferred_element_type=F32)


def standardize(values):
    centred = values - jnp.mean(values, axis=-1, keepdims=True)
    spread = jnp.mean(centred * centred, axis=-1, keepdims=True)
    scaler = lax.rsqrt(spread + EPS)
    return centred * scaler, scaler


def norm_back(grad_normed, gain, normed, scaler):
    scaled = grad_normed * gain
    centred = scaled - jnp.mean(scaled, axis=-1, keepdims=True)
    return scaler * (centred - normed * jnp.mean(scaled * normed, axis=-1, keepdims=True))


def gelu_parts(hidden):
    cumul = 0.5 * (1.0 + lax.erf(hidden * ROOT_HALF))
    return hidden * cumul, cumul + hidden * (jnp.exp(-0.5 * hidden * hidden) * INV_ROOT_TAU)


def segment_at(pieces_ref, row, amount, shape, axis):
    place = lax.broadcasted_iota(jnp.int32, shape, axis)
    end = jnp.int32(0)
    segment = jnp.zeros(shape, jnp.int32)
    for k in range(amount):
        end = end + pieces_ref[row, k]
        segment = segment + (place >= end).astype(jnp.int32)
    return segment


def mask_bias(pieces_ref, row, amount):
    shape = (SEQ_LEN, SEQ_LEN)
    down = segment_at(pieces_ref, row, amount, shape, 0)
    across = segment_at(pieces_ref, row, amount, shape, 1)
    same = (down == across) & (across < amount - 1)
    diagonal = lax.broadcasted_iota(jnp.int32, shape, 0) == lax.broadcasted_iota(jnp.int32, shape, 1)
    return jnp.where(same | diagonal, 0.0, NEG).astype(F32)


def keep_rows(pieces_ref, row, amount):
    segment = segment_at(pieces_ref, row, amount, (SEQ_LEN, 1), 0)
    return (segment < amount - 1).astype(F32)


def head_lanes(shape):
    return lax.broadcasted_iota(jnp.int32, shape, 1) < HEAD


def attend(qkv_ref, rows, bias, width):
    low_lanes = head_lanes((SEQ_LEN, 2 * HEAD))
    lane = lax.broadcasted_iota(jnp.int32, (SEQ_LEN, 2 * HEAD), 1)
    logs = jnp.zeros((SEQ_LEN, 2 * HEAD), F32)
    mixed = []
    for pair in range(width // (2 * HEAD)):
        at = pair * 2 * HEAD
        query = qkv_ref[rows, at : at + 2 * HEAD]
        key = qkv_ref[rows, width + at : width + at + 2 * HEAD]
        value = qkv_ref[rows, 2 * width + at : 2 * width + at + 2 * HEAD]
        parts = []
        for side in range(2):
            mine = low_lanes if side == 0 else ~low_lanes
            scores = dot_nt(jnp.where(mine, query, jnp.zeros_like(query)), key) + bias
            largest = jnp.max(scores, axis=-1, keepdims=True)
            weights = jnp.exp(scores - largest)
            totals = jnp.sum(weights, axis=-1, keepdims=True)
            probs = (weights * (1.0 / totals)).astype(BF16)
            parts.append(dot_nn(probs, value))
            logs = jnp.where(lane == 2 * pair + side, largest + jnp.log(totals), logs)
        mixed.append(jnp.where(low_lanes, parts[0], parts[1]).astype(BF16))
    return jnp.concatenate(mixed, axis=1), logs


def held(*_):
    return pl.BlockSpec(memory_space=pltpu.VMEM)


def seq_rows(seq):
    return pl.ds(pl.multiple_of(seq * SEQ_LEN, SEQ_LEN), SEQ_LEN)


def anywhere(*_):
    return pl.BlockSpec(memory_space=pltpu.HBM)


def call(kernel, name, scalars, operands, outs, grid=(1,), scratch=(), loose=0, limit=VMEM_LIMIT):
    return pl.pallas_call(
        kernel,
        grid_spec=pltpu.PrefetchScalarGridSpec(
            num_scalar_prefetch=len(scalars), grid=grid, in_specs=[anywhere()] * loose + [held()] * (len(operands) - loose), out_specs=[held()] * len(outs), scratch_shapes=list(scratch)),
        out_shape=[jax.ShapeDtypeStruct(shape, dtype) for shape, dtype in outs],
        compiler_params=pltpu.CompilerParams(vmem_limit_bytes=limit),
        cost_estimate=pl.CostEstimate(flops=1, bytes_accessed=1, transcendentals=0),
        name=name,
    )(*scalars, *operands)


def copy_all(copies, sems):
    started = [pltpu.make_async_copy(source, target, sems.at[at]) for at, (source, target) in enumerate(copies)]
    for copy in started:
        copy.start()
    return started


def column_sum(values):
    return jnp.sum(values.reshape(values.shape[0] // 8, 8, values.shape[1]), axis=0)


VECTORS = 6
BITS = 2
TAIL = 16


def first_kernel(place_ref, wq_ref, wk_ref, out_ref, sems):
    for k, ref in enumerate((wq_ref, wk_ref)):
        @pl.when(place_ref[BITS] == k)
        def _():
            pltpu.make_async_copy(ref, out_ref, sems.at[0]).start()

    pltpu.make_async_copy(wq_ref, out_ref, sems.at[0]).wait()


def fetch_first(place, wq, wk):
    return call(first_kernel, "fetch_first", (place,), (wq, wk), [(wq.shape, BF16)], loose=2, limit=FETCH_LIMIT,
                scratch=[pltpu.SemaphoreType.DMA((1,))])[0]


def in_three(values):
    rows = []
    for _ in range(3):
        part = values.astype(BF16).astype(F32)
        rows.append(part)
        values = values - part
    return rows


def fetch_kernel(place_ref, wq_ref, wk_ref, wv_ref, wo_ref, x_ref, cot_ref, small_ref, pack_ref, v_ref, x_own_ref, cot_own_ref, vectors_ref, up_ref, sems):
    shard, d = wo_ref.shape
    mine = pl.ds(pl.multiple_of(place_ref[0] * SEQ_LEN, SEQ_LEN), x_own_ref.shape[0])
    copies = copy_all(
        [(ref, pack_ref.at[pl.ds(k * shard, shard)]) for k, ref in enumerate((wq_ref, wk_ref, wv_ref, wo_ref))]
        + [(wv_ref, v_ref.at[pl.ds(0, shard)]), (x_ref.at[mine], x_own_ref), (cot_ref.at[mine], cot_own_ref)], sems)

    def vector(at, size):
        return small_ref[pl.ds(at, size)].reshape(1, size)

    vectors_ref[...] = jnp.zeros_like(vectors_ref)
    for k in range(VECTORS):
        vectors_ref[k : k + 1, :] = vector(k * d, d)
    ff = up_ref.shape[1]
    up = vector(VECTORS * d, ff)
    up_ref[...] = up
    zero = jnp.zeros((1, shard), F32)
    at = VECTORS * d + ff
    rows = in_three(jnp.concatenate([vector(at, shard), zero, vector(at + shard, shard), zero], axis=1))
    for k in range(ff // d):
        rows += in_three(up[:, k * d : (k + 1) * d])
    rows.append(jnp.zeros((TAIL - len(rows), d), F32))
    tail = jnp.concatenate(rows, axis=0).astype(BF16)
    pack_ref[4 * shard :, :] = tail
    v_ref[shard:, :] = tail
    for copy in copies:
        copy.wait()


def fetch(place, wq, wk, wv, wo, x, cot, small, rows, ff):
    shard, d = wo.shape
    outs = [((4 * shard + TAIL, d), BF16), ((shard + TAIL, d), BF16), ((rows, d), BF16), ((rows, d), BF16), ((8, d), F32), ((1, ff), F32)]
    return call(fetch_kernel, "fetch", (place,), (wq, wk, wv, wo, x, cot, small), outs, loose=6, limit=FETCH_LIMIT,
                scratch=[pltpu.SemaphoreType.DMA((7,))])


def spread_bias(a_ref, b_ref, shard):
    a, b = (jnp.sum(ref[ref.shape[0] - TAIL : ref.shape[0] - TAIL + 3, :].astype(F32), axis=0, keepdims=True) for ref in (a_ref, b_ref))
    return a + jnp.concatenate([jnp.zeros((1, shard), F32), b[:, : 3 * shard]], axis=1)


def project(lowered, w_ref, bias, qkv_ref, at, width):
    for k in range(3):
        proj = dot_nt(lowered, w_ref[k * width : (k + 1) * width, :])
        if k == 0:
            proj = (proj + bias[:, :width]).astype(BF16) * jnp.asarray(SCALE, BF16)
        elif k == 2:
            proj = proj + bias[:, width:]
        qkv_ref[at, k * width : (k + 1) * width] = proj.astype(BF16)


def project_kernel(shard, x_ref, vectors_ref, a_ref, b_ref, w_ref, normed_ref, qkv_ref, up_ref):
    step = pl.program_id(0)
    width = 2 * shard
    d = x_ref.shape[1]

    @pl.when(step == 0)
    def _():
        for side, ref in enumerate((a_ref, b_ref)):
            for k in range(4):
                w_ref[k * width + side * shard : k * width + (side + 1) * shard, :] = ref[k * shard : (k + 1) * shard, :]
        tail = b_ref[4 * shard :, :].astype(F32)
        for k in range(up_ref.shape[1] // d):
            up_ref[:, k * d : (k + 1) * d] = jnp.sum(tail[3 + 3 * k : 6 + 3 * k], axis=0, keepdims=True)

    at = seq_rows(step)
    normed, _ = standardize(x_ref[at, :].astype(F32))
    lowered = (normed * vectors_ref[0:1, :] + vectors_ref[1:2, :]).astype(BF16)
    normed_ref[at, :] = lowered
    project(lowered, w_ref, spread_bias(a_ref, b_ref, shard), qkv_ref, at, width)


def project_own(x, vectors, a, b, ff):
    rows, d = x.shape
    shard = (a.shape[0] - TAIL) // 4
    outs = [((8 * shard, d), BF16), ((rows, d), BF16), ((rows, 6 * shard), BF16), ((1, ff), F32)]
    return call(functools.partial(project_kernel, shard), "project_own", (), (x, vectors, a, b), outs, (rows // SEQ_LEN,))


def attend_kernel(amount, width, place_ref, pieces_ref, qkv_ref, w_ref, mixed_ref, logs_ref, part_ref):
    step = pl.program_id(0)
    at = seq_rows(step)
    mixed, logs = attend(qkv_ref, at, mask_bias(pieces_ref, place_ref[0] + step, amount), width)
    logs_ref[pl.ds(pl.multiple_of(step * 8, 8), 8), :] = logs.T[:8, :]
    mixed_ref[at, :] = mixed
    part_ref[at, :] = dot_nn(mixed, w_ref[3 * width : 4 * width, :])


def attend_own(place, pieces, qkv, w):
    seqs, amount = pieces.shape[0] // 2, pieces.shape[1]
    width, d = w.shape[0] // 4, w.shape[1]
    rows = seqs * SEQ_LEN
    outs = [((rows, width), BF16), ((seqs * 8, SEQ_LEN), F32), ((rows, d), F32)]
    return call(functools.partial(attend_kernel, amount, width), "attend_own", (place, pieces), (qkv, w), outs, (seqs,))


def other_kernel(amount, shard, place_ref, pieces_ref, *refs):
    w_refs = refs[:6]
    normed_in_ref, w_ref, qkv_ref, logs_ref, mixed_ref = refs[6:]
    step = pl.program_id(0)
    width = 2 * shard
    kinds = (place_ref[BITS], 1 - place_ref[BITS], 2)

    @pl.when(step == 0)
    def _():
        for k, ref in enumerate(w_refs):
            to = kinds[k % 3] * width + (k // 3) * shard
            w_ref[pl.ds(to if k % 3 > 1 else pl.multiple_of(to, shard), shard), :] = ref[:shard, :]

    at = seq_rows(step)
    project(normed_in_ref[at, :], w_ref, spread_bias(w_refs[2], w_refs[5], shard), qkv_ref, at, width)
    mixed, logs = attend(qkv_ref, at, mask_bias(pieces_ref, place_ref[0] + step, amount), width)
    logs_ref[pl.ds(pl.multiple_of(step * 8, 8), 8), :] = logs.T[:8, :]
    mixed_ref[at, :] = mixed


def attend_other(place, pieces, weights, normed):
    seqs, amount = pieces.shape[0] // 2, pieces.shape[1]
    shard, d = weights[0].shape
    rows = seqs * SEQ_LEN
    outs = [((6 * shard, d), BF16), ((rows, 6 * shard), BF16), ((seqs * 8, SEQ_LEN), F32), ((rows, 2 * shard), BF16)]
    return call(functools.partial(other_kernel, amount, shard), "attend_other", (place, pieces), (*weights, normed), outs, (seqs,))


def middle_kernel(amount, place_ref, pieces_ref, wa_ref, wb_ref, x_ref, mixed_ref, part_in_ref, vectors_ref, w_ref, middle_ref, normed_ref, sum_ref):
    step = pl.program_id(0)
    shard = wa_ref.shape[0]

    @pl.when(step == 0)
    def _():
        w_ref[:shard, :] = wa_ref[...]
        w_ref[shard:, :] = wb_ref[...]

    at = seq_rows(step)
    sum_ref[...] = dot_nn(mixed_ref[at, :], w_ref[...])
    keep_all = keep_rows(pieces_ref, place_ref[0] + step, amount)
    block = 64
    for r in range(0, SEQ_LEN, block):
        here = pl.ds(pl.multiple_of(step * SEQ_LEN + r, block), block)
        added = part_in_ref[here, :] + sum_ref[r : r + block, :] + vectors_ref[2:3, :]
        middle = x_ref[here, :].astype(F32) + keep_all[r : r + block] * added
        middle_ref[here, :] = middle
        normed, _ = standardize(middle)
        normed_ref[here, :] = (normed * vectors_ref[3:4, :] + vectors_ref[4:5, :]).astype(BF16)


def middle_rows(place, pieces, wa, wb, x, mixed, part, vectors):
    rows, d = x.shape
    width = mixed.shape[1]
    outs = [((width, d), BF16), ((rows, d), F32), ((rows, d), BF16)]
    return call(functools.partial(middle_kernel, pieces.shape[1]), "middle", (place, pieces), (wa, wb, x, mixed, part, vectors), outs, (rows // SEQ_LEN,),
                [pltpu.VMEM((SEQ_LEN, d), F32)])


def mlp_kernel(amount, first, seqs, place_ref, pieces_ref, n2_ref, cot_ref, ba_ref, bb_ref, upa_ref, upb_ref, dna_ref, dnb_ref,
               active_ref, gh_ref, gb_ref, sums_ref, n2_out_ref, *gn2_refs):
    ff = upa_ref.shape[1]
    block = 256 if ff % 256 == 0 else ff
    total = [None] * (2 * ff // block)
    for s in range(seqs):
        rows = slice(s * SEQ_LEN, (s + 1) * SEQ_LEN)
        here = slice((first + s) * SEQ_LEN, (first + s + 1) * SEQ_LEN)
        keep = keep_rows(pieces_ref, place_ref[0] + first + s, amount)
        branch = (keep * cot_ref[here, :].astype(F32)).astype(BF16)
        gb_ref[rows, :] = branch
        n2 = n2_ref[here, :]
        n2_out_ref[rows, :] = n2
        for side, (up_ref, dn_ref, bias_ref) in enumerate(((upa_ref, dna_ref, ba_ref), (upb_ref, dnb_ref, bb_ref))):
            for j in range(0, ff, block):
                at = slice(side * ff + j, side * ff + j + block)
                hidden = dot_nn(n2, up_ref[:, j : j + block]) + bias_ref[:, j : j + block]
                active, slope = gelu_parts(hidden)
                active_ref[rows, at] = active.astype(BF16)
                grad_active = dot_nt(branch, dn_ref[j : j + block, :])
                grad_hidden = (grad_active * slope).astype(BF16)
                gh_ref[rows, at] = grad_hidden
                part = jnp.sum(grad_hidden.astype(F32), axis=0, keepdims=True)
                k = at.start // block
                total[k] = part if total[k] is None else total[k] + part
        gn2_refs[s][...] = (dot_nt(gh_ref[rows, :ff], upa_ref[...]) + dot_nt(gh_ref[rows, ff:], upb_ref[...])).astype(BF16)
    for k, part in enumerate(total):
        sums_ref[:, k * block : (k + 1) * block] = part


def mlp_rows(first, seqs, place, pieces, n2, cot, bias, bias_b, upa, upb, dna, dnb):
    d, ff = upa.shape
    rows = seqs * SEQ_LEN
    outs = [((rows, 2 * ff), BF16), ((rows, 2 * ff), BF16), ((rows, d), BF16), ((1, 2 * ff), F32), ((rows, d), BF16)] + [((SEQ_LEN, d), BF16)] * seqs
    return call(functools.partial(mlp_kernel, pieces.shape[1], first, seqs), "mlp", (place, pieces), (n2, cot, bias, bias_b, upa, upb, dna, dnb), outs)


def down_kernel(count, dna_ref, dnb_ref, *refs):
    ff = dna_ref.shape[0]
    at = 0
    for active_ref in refs[:count]:
        for r in range(0, active_ref.shape[0], SEQ_LEN):
            rows = slice(r, r + SEQ_LEN)
            refs[count + at][...] = (dot_nn(active_ref[rows, :ff], dna_ref[...]) + dot_nn(active_ref[rows, ff:], dnb_ref[...])).astype(BF16)
            at += 1


def down_rows(dna, dnb, actives):
    seqs, d = sum(a.shape[0] for a in actives) // SEQ_LEN, dna.shape[1]
    return call(functools.partial(down_kernel, len(actives)), "down", (), (dna, dnb, *actives), [((SEQ_LEN, d), BF16)] * seqs)


def sent_kernel(count, side, *refs):
    out_ref = refs[-1]
    size = out_ref.shape[0]
    block = 256 if size % 256 == 0 else size
    for j in range(0, size, block):
        at = slice(side * size + j, side * size + j + block)
        total = sum(dot_tn(refs[k][:, at], refs[count + k][...]) for k in range(count))
        out_ref[j : j + block, :] = total.astype(BF16)


def grad_sent(side, lefts, rights):
    size, d = lefts[0].shape[1] // 2, rights[0].shape[1]
    return call(functools.partial(sent_kernel, len(lefts), side), "grad_sent", (), (*lefts, *rights), [((size, d), BF16)])


def kept_kernel(count, bit, place_ref, *refs):
    add_ref, send_ref, keep_ref = refs[-3:]
    half = keep_ref.shape[0]
    for which, out_ref in enumerate((send_ref, keep_ref)):
        mine = place_ref[BITS + bit] if which else 1 - place_ref[BITS + bit]
        at = pl.ds(pl.multiple_of(mine * half, half), half)
        total = sum(dot_tn(refs[k][:, at], refs[count + k][...]) for k in range(count))
        out_ref[...] = (total + add_ref[at, :].astype(F32)).astype(BF16)


def grad_kept(bit, place, lefts, rights, add):
    half, d = lefts[0].shape[1] // 4, rights[0].shape[1]
    return call(functools.partial(kept_kernel, len(lefts), bit), "grad_kept", (place,), (*lefts, *rights, add), [((half, d), BF16)] * 2)


def attn_dots(refs, attns, n1_ref, seqs, shard, side, kind):
    width = 2 * shard
    at = slice(kind * width + side * shard, kind * width + (side + 1) * shard)
    rights = [attns[s][...] if kind == 3 else n1_ref[s * SEQ_LEN : (s + 1) * SEQ_LEN, :] for s in range(seqs)]
    return sum(dot_tn(refs[s][:, at], rights[s]) for s in range(seqs))


def attn_sent_kernel(seqs, kinds, *refs):
    out_ref = refs[-1]
    shard = out_ref.shape[0] // len(kinds)
    for k, kind in enumerate(kinds):
        out_ref[k * shard : (k + 1) * shard, :] = attn_dots(refs[:seqs], refs[seqs : 2 * seqs], refs[2 * seqs], seqs, shard, 1, kind).astype(BF16)


def attn_sent(kinds, lefts, attns, n1):
    shard, d = lefts[0].shape[1] // 8, n1.shape[1]
    return call(functools.partial(attn_sent_kernel, len(lefts), kinds), "attn_sent", (), (*lefts, *attns, n1), [((len(kinds) * shard, d), BF16)])


def attn_kept_kernel(seqs, kinds, bit, place_ref, *refs):
    add_ref, send_ref, keep_ref = refs[-3:]
    shard = keep_ref.shape[0]
    for which, kind in enumerate(kinds):
        total = attn_dots(refs[:seqs], refs[seqs : 2 * seqs], refs[2 * seqs], seqs, shard, 0, kind)
        total = (total + add_ref[which * shard : (which + 1) * shard, :].astype(F32)).astype(BF16)
        for out_ref, chosen in ((keep_ref, which), (send_ref, 1 - which)):
            @pl.when(place_ref[BITS + bit] == chosen)
            def _():
                out_ref[...] = total


def attn_kept(kinds, bit, place, lefts, attns, n1, add):
    shard, d = lefts[0].shape[1] // 8, n1.shape[1]
    return call(functools.partial(attn_kept_kernel, len(lefts), kinds, bit), "attn_kept", (place,), (*lefts, *attns, n1, add), [((shard, d), BF16)] * 2)


def attend_back(qkv_ref, rows, gm_ref, logs_ref, first, bias, width, grads_ref):
    low_lanes = head_lanes((SEQ_LEN, 2 * HEAD))
    for pair in range(width // (2 * HEAD)):
        at = pair * 2 * HEAD
        here = [slice(k * width + at, k * width + at + 2 * HEAD) for k in range(3)]
        query, key, value = (qkv_ref[rows, h] for h in here)
        grad_mixed = gm_ref[:, here[0]]
        pieces = []
        for side in range(2):
            mine = low_lanes if side == 0 else ~low_lanes
            zero = jnp.zeros_like(key)
            head = 2 * pair + side
            scores = dot_nt(jnp.where(mine, key, zero), query) + bias
            probs = jnp.exp(scores - logs_ref[first + head : first + head + 1, :])
            grad_probs = dot_nt(jnp.where(mine, value, zero), grad_mixed)
            inner = jnp.sum(grad_probs * probs, axis=0, keepdims=True)
            grad_scores = (probs * (grad_probs - inner)).astype(BF16)
            pieces.append((dot_tn(grad_scores, key) * SCALE, dot_nn(grad_scores, query), dot_nn(probs.astype(BF16), grad_mixed)))
        for k in range(3):
            grads_ref[:, here[k]] = jnp.where(low_lanes, pieces[0][k], pieces[1][k]).astype(BF16)


def own_back_kernel(amount, seq, place_ref, pieces_ref, cot_ref, middle_ref, own_ref, got_ref, vectors_ref, qkv_ref, logs_ref, mixed_ref, w_ref,
                    grad_ref, all_ref, attn_ref, part_ref, sums_ref, gm_ref):
    row = place_ref[0] + seq
    width = mixed_ref.shape[1]
    d = cot_ref.shape[1]
    keep_all = keep_rows(pieces_ref, row, amount)
    sums = [jnp.zeros((8, d), F32)] * 4
    block = 32
    for r in range(0, SEQ_LEN, block):
        at = slice(r, r + block)
        keep = keep_all[at]
        cot = cot_ref[seq * SEQ_LEN + r : seq * SEQ_LEN + r + block, :].astype(F32)
        gn2 = own_ref[at, :].astype(F32) + got_ref[at, :].astype(F32)
        normed, scaler = standardize(middle_ref[seq * SEQ_LEN + r : seq * SEQ_LEN + r + block, :])
        grad_middle = cot + norm_back(gn2, vectors_ref[3:4, :], normed, scaler)
        attn = (keep * grad_middle).astype(BF16)
        attn_ref[at, :] = attn
        grad_ref[at, :] = grad_middle
        terms = (attn.astype(F32), gn2 * normed, gn2, (keep * cot).astype(BF16).astype(F32))
        sums = [s + column_sum(t) for s, t in zip(sums, terms)]
    sums_ref[...] = jnp.zeros_like(sums_ref)
    for k in range(4):
        sums_ref[2 + k : 3 + k, :] = jnp.sum(sums[k], axis=0, keepdims=True)
    gm_ref[...] = dot_nt(attn_ref[...], w_ref[3 * width : 4 * width, :]).astype(BF16)
    rows = slice(seq * SEQ_LEN, (seq + 1) * SEQ_LEN)
    attend_back(qkv_ref, rows, gm_ref, logs_ref, 8 * seq, mask_bias(pieces_ref, row, amount), width, all_ref)
    part_ref[...] = dot_nn(all_ref[:, : 3 * width], w_ref[: 3 * width, :])
    all_ref[:, 3 * width :] = mixed_ref[rows, :]
    sums_ref[6:7, :width] = jnp.sum(all_ref[:, :width].astype(F32), axis=0, keepdims=True)
    sums_ref[7:8, :width] = jnp.sum(all_ref[:, 2 * width : 3 * width].astype(F32), axis=0, keepdims=True)


def own_back(seq, place, pieces, cot, middle, own, got, vectors, qkv, logs, mixed, w):
    d, width = cot.shape[1], mixed.shape[1]
    outs = [((SEQ_LEN, d), F32), ((SEQ_LEN, 4 * width), BF16), ((SEQ_LEN, d), BF16), ((SEQ_LEN, d), F32), ((8, d), F32)]
    return call(functools.partial(own_back_kernel, pieces.shape[1], seq), "own_back", (place, pieces),
                (cot, middle, own, got, vectors, qkv, logs, mixed, w), outs, scratch=[pltpu.VMEM((SEQ_LEN, width), BF16)])


def other_back_kernel(amount, seq, place_ref, pieces_ref, x_ref, grad_in_ref, attn_ref, part_ref, vectors_ref, qkv_ref, logs_ref, w_ref, wo_ref,
                      grad_ref, sums_ref, gm_ref, all_ref, sum_ref):
    row = place_ref[0] + seq
    width = gm_ref.shape[1]
    d = x_ref.shape[1]
    bias = mask_bias(pieces_ref, row, amount)
    gm_ref[...] = dot_nt(attn_ref[...], wo_ref[...]).astype(BF16)
    rows = slice(seq * SEQ_LEN, (seq + 1) * SEQ_LEN)
    attend_back(qkv_ref, rows, gm_ref, logs_ref, 8 * seq, bias, width, all_ref)
    sum_ref[...] = dot_nn(all_ref[...], w_ref[...])
    sums = [jnp.zeros((8, d), F32)] * 2
    block = 32
    for r in range(0, SEQ_LEN, block):
        at = slice(r, r + block)
        gn1 = part_ref[at, :] + sum_ref[at, :]
        normed, scaler = standardize(x_ref[seq * SEQ_LEN + r : seq * SEQ_LEN + r + block, :].astype(F32))
        grad_ref[at, :] = grad_in_ref[at, :] + norm_back(gn1, vectors_ref[0:1, :], normed, scaler)
        sums = [s + column_sum(t) for s, t in zip(sums, (gn1 * normed, gn1))]
    sums_ref[...] = jnp.zeros_like(sums_ref)
    for k in range(2):
        sums_ref[k : k + 1, :] = jnp.sum(sums[k], axis=0, keepdims=True)


def other_back(seq, place, pieces, x, grad_in, attn, part, vectors, qkv, logs, w, wo):
    d, width = wo.shape[1], wo.shape[0]
    outs = [((SEQ_LEN, d), F32), ((8, d), F32)]
    return call(functools.partial(other_back_kernel, pieces.shape[1], seq), "other_back", (place, pieces),
                (x, grad_in, attn, part, vectors, qkv, logs, w, wo), outs,
                scratch=[pltpu.VMEM((SEQ_LEN, width), BF16), pltpu.VMEM((SEQ_LEN, 3 * width), BF16), pltpu.VMEM((SEQ_LEN, d), F32)])


def output_kernel(amount, seqs, place_ref, pieces_ref, middle_ref, vectors_ref, *refs):
    out_refs = refs[2 * seqs :]
    size = out_refs[0].shape[0]
    block = 64
    for seq in range(seqs):
        keep_all = keep_rows(pieces_ref, place_ref[0] + seq, amount)
        for r in range(0, SEQ_LEN, block):
            at = seq * SEQ_LEN + r
            total = refs[seq][r : r + block, :].astype(F32) + refs[seqs + seq][r : r + block, :].astype(F32) + vectors_ref[5:6, :]
            out = (middle_ref[at : at + block, :] + keep_all[r : r + block] * total).astype(BF16)
            out_refs[at // size][at % size : at % size + block, :] = out


def output_rows(pieces_out, place, pieces, middle, vectors, owns, gots):
    rows, d = middle.shape
    return call(functools.partial(output_kernel, pieces.shape[1], len(owns)), "block_output", (place, pieces),
                (middle, vectors, *owns, *gots), [((rows // pieces_out, d), BF16)] * pieces_out)


def both_kernel(count, place_ref, *refs):
    out_ref, sems = refs[-2:]
    size = refs[0].shape[0]
    copies = []
    for k in range(2 * count):
        at = (place_ref[1] if k < count else 1 - place_ref[1]) * count + k % count
        copies.append(pltpu.make_async_copy(refs[k], out_ref.at[pl.ds(pl.multiple_of(at * size, size), size)], sems.at[k]))
        copies[-1].start()
    for copy in copies:
        copy.wait()


def both_cores(place, mine, theirs):
    count = len(mine)
    rows, d = mine[0].shape
    return pl.pallas_call(
        functools.partial(both_kernel, count),
        grid_spec=pltpu.PrefetchScalarGridSpec(
            num_scalar_prefetch=1, grid=(1,), in_specs=[held()] * (2 * count), out_specs=pl.BlockSpec(memory_space=pl.ANY),
            scratch_shapes=[pltpu.SemaphoreType.DMA((2 * count,))]),
        out_shape=jax.ShapeDtypeStruct((2 * count * rows, d), mine[0].dtype),
        compiler_params=pltpu.CompilerParams(vmem_limit_bytes=VMEM_LIMIT),
        cost_estimate=pl.CostEstimate(flops=1, bytes_accessed=1, transcendentals=0),
        name="both_cores",
    )(place, *mine, *theirs)


def swap(size, bit):
    return [(i, i ^ bit) for i in range(size)]


def tie(values, *after):
    return lax.optimization_barrier((values, after))[0]


def merge_kernel(at, place_ref, keep_ref, got_ref, send_ref, out_ref):
    size = out_ref.shape[0]
    for which, ref in enumerate((send_ref, out_ref)):
        bit = place_ref[BITS + at] if which else 1 - place_ref[BITS + at]
        rows = pl.ds(pl.multiple_of(bit * size, size), size)
        ref[...] = (keep_ref[rows, :].astype(F32) + got_ref[rows, :].astype(F32)).astype(BF16)


def merge(bit, place, keep, got):
    rows, d = keep.shape
    half = rows // 2
    if half % 16:
        total = (keep.astype(F32) + got.astype(F32)).astype(BF16)
        low = place[BITS + bit] == 0
        return jnp.where(low, total[half:], total[:half]), jnp.where(low, total[:half], total[half:])
    return call(functools.partial(merge_kernel, bit), "merge", (place,), (keep, got), [((half, d), BF16)] * 2)


def add_kernel(keep_ref, got_ref, out_ref):
    out_ref[...] = (keep_ref[...].astype(F32) + got_ref[...].astype(F32)).astype(out_ref.dtype)


def add(keep, got):
    return call(add_kernel, "add", (), (keep, got), [(keep.shape, keep.dtype)])[0]


def grow_kernel(at, place_ref, keep_ref, got_ref, out_ref):
    size = keep_ref.shape[0]
    out_ref[pl.ds(pl.multiple_of(place_ref[BITS + at] * size, size), size), :] = keep_ref[...]
    out_ref[pl.ds(pl.multiple_of((1 - place_ref[BITS + at]) * size, size), size), :] = got_ref[...]


def grow(bit, place, keep, got):
    rows, d = keep.shape
    if rows % 16:
        return jnp.where(place[BITS + bit] == 0, jnp.concatenate([keep, got]), jnp.concatenate([got, keep]))
    return call(functools.partial(grow_kernel, bit), "grow", (place,), (keep, got), [((2 * rows, d), BF16)])[0]


def finish_up_kernel(at, place_ref, keep_ref, got_ref, out_ref):
    size = keep_ref.shape[0]
    out_ref[:, pl.ds(pl.multiple_of(place_ref[BITS + at] * size, 128), size)] = keep_ref[...].astype(F32).T
    out_ref[:, pl.ds(pl.multiple_of((1 - place_ref[BITS + at]) * size, 128), size)] = got_ref[...].astype(F32).T


def finish_down_kernel(at, place_ref, keep_ref, got_ref, out_ref):
    size = keep_ref.shape[0]
    out_ref[pl.ds(pl.multiple_of(place_ref[BITS + at] * size, size), size), :] = keep_ref[...].astype(F32)
    out_ref[pl.ds(pl.multiple_of((1 - place_ref[BITS + at]) * size, size), size), :] = got_ref[...].astype(F32)


def finish(kernel, name, bit, shape, place, keep, got):
    return call(functools.partial(kernel, bit), name, (place,), (keep, got), [(shape, F32)])[0]


def rows_kernel(at, place_ref, keep_ref, got_ref, low_ref, high_ref):
    mine = place_ref[BITS + at] == 0
    keep, got = keep_ref[...].astype(F32), got_ref[...].astype(F32)
    low_ref[...] = jnp.where(mine, keep, got)
    high_ref[...] = jnp.where(mine, got, keep)


def finish_rows(bit, place, keep, got):
    return call(functools.partial(rows_kernel, bit), "finish_rows", (place,), (keep, got), [(keep.shape, F32)] * 2)


class Unit:
    def __init__(self, groups, order, place, send, keep):
        self.groups, self.order, self.place = groups, order, place
        self.send, self.keep, self.step = send, keep, 0
        self.last = 2 * len(order) - 1

    def start(self):
        count = len(self.order)
        at = self.step if self.step < count else 2 * count - 1 - self.step
        self.got = lax.ppermute(self.send, "dp", swap(self.groups, 1 << self.order[at]))

    def take(self):
        count = len(self.order)
        if self.step < count - 1:
            self.send, self.keep = merge(self.order[self.step + 1], self.place, self.keep, self.got)
        elif self.step == count - 1:
            self.keep = add(self.keep, self.got)
            self.send = self.keep
        elif self.step < 2 * count - 1:
            self.keep = grow(self.order[2 * count - 1 - self.step], self.place, self.keep, self.got)
            self.send = self.keep
        self.step += 1


class Chain:
    def __init__(self):
        self.last = ()

    def run(self, kernel, *args, need=()):
        args = tie(args, self.last, need)
        out = kernel(*args)
        self.last = out
        return out

    def after(self, values):
        return tie(values, self.last)

    def need(self, values):
        self.last = (self.last, values)


SCHEDULE = (
    "mlp0", "+G0", "mlp1", "gs0", "+G1", "+cb0", "gs1", "+cb1", "gk0", "+G2", "+u0", "gk1", "down", "ob0", "+u1", "+D0", "ob1", "u0",
    "xb1", "+u0", "ob2", "ao1", "-D0", "u1", "+gc1", "+ca1", "ao0", "+u1", "u0", "+ca0", "-cb1", "+D1", "+u0", "ak1", "ak0", "+u2", "u1",
    "+u1", "+u3", "xb0", "+D2", "+gc0", "u0", "+u0", "u2", "+u2", "u1", "u3", "u2", "+u1", "+u3", "u0", "+u2", "xb2", "-u1", "u1", "+u1",
    "sums", "+sc", "u3", "u2", "+u0", "+gc2", "+u3", "+u2", "out", "sa0", "u3", "+u3", "u2", "+s0", "+u2", "u1", "u0", "sa1", "u3", "+u1",
    "+u3", "+oc", "gin", "+s1", "u3", "u2", "sa2", "+u0", "+u3", "+s2", "-u3", "finish1", "bout", "+u2", "finish3", "finish0", "sa3",
    "finish2",
)
ORDERS = ((1, 0, 2), (0, 1, 2), (0, 1, 2), (0, 1, 2))


def small_kernel(seqs, shard, *refs):
    own, oth, ups, outs = refs[:seqs], refs[seqs : 2 * seqs], refs[2 * seqs : -2], refs[-2:]
    total = sum(r[...] for r in own) + sum(r[...] for r in oth)
    up = sum(r[...] for r in ups)
    d = total.shape[1]
    ff = up.shape[1] // 2
    for side, out_ref in enumerate(outs):
        out_ref[0:6, :] = total[0:6]
        at = slice(side * shard, (side + 1) * shard)
        out_ref[6:7, :] = jnp.concatenate([total[6:7, at], total[7:8, at], jnp.zeros((1, d - 2 * shard), F32)], axis=1)
        for k in range(ff // d):
            out_ref[7 + k : 8 + k, :] = up[:, side * ff + k * d : side * ff + (k + 1) * d]


def small_sums(shard, own, oth, ups):
    seqs, d = len(own), own[0].shape[1]
    rows = 7 + ups[0].shape[1] // 2 // d
    operands = [*own, *oth, *ups]
    return call(functools.partial(small_kernel, seqs, shard), "small_sums", (), operands, [((rows, d), F32)] * 2)


def on_device(groups, tp, block_input, pieces, gain_one, shift_one, query_weight, query_bias, key_weight, value_weight, value_bias,
              out_weight, out_bias, gain_two, shift_two, up_weight, up_bias, down_weight, down_bias, cotangent):
    d = block_input.shape[1]
    shard = query_weight.shape[1]
    ff = up_weight.shape[1]
    seqs = pieces.shape[0] // 2
    core = lax.axis_index("tp") & 1
    group = lax.axis_index("dp")
    bits = list(range(groups.bit_length() - 1))
    place = jnp.stack([core * seqs, core] + [(group >> bit) & 1 for bit in bits]).astype(jnp.int32)

    def other_core(values):
        return lax.ppermute(values, "tp", swap(tp, 1))

    def other_chip(values):
        return lax.ppermute(values, "tp", swap(tp, 2))

    def next_group(values):
        return lax.ppermute(values, "dp", swap(groups, 1))

    chain = Chain()
    wq, wk, wv, wo = query_weight.T, key_weight.T, value_weight.T, out_weight
    small = jnp.concatenate([gain_one, shift_one, out_bias, gain_two, shift_two, down_bias, up_bias, query_bias, value_bias])
    first = chain.run(fetch_first, place, wq, wk)
    first = other_chip(first)
    pack, last_v, x_own, cot_own, vectors, up_row = chain.run(
        functools.partial(fetch, rows=seqs * SEQ_LEN, ff=ff), place, wq, wk, wv, wo, block_input, cotangent, small)
    pack_b = other_core(pack)
    last_v, last_o = other_chip(last_v), other_chip(wo)
    up_b, down_b = other_core(up_weight), other_core(down_weight)
    w_own, n1, qkv_own, up_row_b = chain.run(functools.partial(project_own, ff=ff), x_own, vectors, pack, pack_b)
    second = next_group(chain.after(first))
    mixed, logs_own, part = chain.run(attend_own, place, pieces, qkv_own, w_own, need=(first, up_b, down_b))
    got = chain.after((first, second, last_v))
    w_oth, qkv_oth, logs_oth, mixed_oth = chain.run(attend_other, place, pieces, (*got, *[other_core(g) for g in got]), n1)
    last_o = chain.after(last_o)
    wo_oth, middle, n2 = chain.run(middle_rows, place, pieces, last_o, other_core(last_o), x_own, mixed_oth, part, vectors)

    sent, got, made = {}, {}, {}
    units = {}

    def unit(name, at, send, keep):
        order = [*ORDERS[at], *bits[len(ORDERS[at]) :]]
        units[name] = Unit(groups, order, place, send, keep)

    def take(name):
        u = units[name]
        u.keep, u.got = tie((u.keep, u.got), chain.last)
        u.take()
        chain.last = u.keep

    def begin(name):
        u = units[name]
        u.send = chain.after(u.send)
        with jax.named_scope(f"send_{name}_{u.step}"):
            u.start()

    def complete(name):
        u = units[name]
        while u.step < u.last:
            take(name)
            begin(name)

    def mlp(part):
        first, count = (0, 1) if part == 0 else (1, seqs - 1)
        out = chain.run(functools.partial(mlp_rows, first, count), place, pieces, n2, cot_own, up_row, up_row_b, up_weight, up_b, down_weight, down_b)
        for key, value in zip(("active", "hidden", "branch", "sums", "n2"), out):
            made.setdefault(key, []).append(value)
        made.setdefault("gn2", []).extend(out[5:])

    def sides(at):
        return (made["hidden"], made["n2"]) if at == 0 else (made["active"], made["branch"])

    def step(name):
        kind, at = name.rstrip("0123456789"), name[len(name.rstrip("0123456789")) :]
        at = int(at) if at else 0
        if kind == "mlp":
            mlp(at)
        elif kind == "down":
            made["down"] = chain.run(down_rows, down_weight, down_b, made["active"])
        elif kind == "gs":
            sent[f"cb{at}"] = chain.run(functools.partial(grad_sent, 1), *sides(at))
        elif kind == "gk":
            unit(f"u{at}", at, *chain.run(functools.partial(grad_kept, ORDERS[at][0]), place, *sides(at), got[f"cb{at}"][0]))
        elif kind == "ob":
            made[f"ob{at}"] = chain.run(functools.partial(own_back, at), place, pieces, cot_own, middle, made["gn2"][at], got[f"G{at}"][0], vectors,
                                        qkv_own, logs_own, mixed, w_own)
        elif kind in ("ao", "ak"):
            kinds = (0, 1) if at == 0 else (2, 3)
            owns = [made[f"ob{s}"] for s in range(seqs)]
            operands = ([o[1] for o in owns], [o[2] for o in owns], n1)
            if kind == "ao":
                sent[f"ca{at}"] = chain.run(functools.partial(attn_sent, kinds), *operands)
            else:
                unit(f"u{2 + at}", 2 + at, *chain.run(functools.partial(attn_kept, kinds, ORDERS[2 + at][0]), place, *operands, got[f"ca{at}"][0]))
        elif kind == "xb":
            own = made[f"ob{at}"]
            made[f"xb{at}"] = chain.run(functools.partial(other_back, at), place, pieces, x_own, own[0], own[2], own[3], vectors,
                                        qkv_oth, logs_oth, w_oth, wo_oth)
            sent[f"gc{at}"] = made[f"xb{at}"][:1]
        elif kind == "sums":
            made["small"], more = chain.run(functools.partial(small_sums, shard), [made[f"ob{s}"][4] for s in range(seqs)],
                                            [made[f"xb{s}"][1] for s in range(seqs)], made["sums"])
            sent["sc"] = [more]
        elif kind == "sa":
            made["small"] = chain.run(add, made["small"], got["sc" if at == 0 else f"s{at - 1}"][0])
            sent[f"s{at}"] = [made["small"]]
        elif kind == "out":
            sent["oc"] = chain.run(functools.partial(output_rows, 1), place, pieces, middle, vectors, made["down"], [got[f"D{s}"][0] for s in range(seqs)])
        elif kind == "gin":
            made["input_grad"] = chain.run(both_cores, place, sum((list(sent[f"gc{s}"]) for s in range(seqs)), []), sum((list(got[f"gc{s}"]) for s in range(seqs)), []))
        elif kind == "bout":
            made["block_output"] = chain.run(both_cores, place, sent["oc"], got["oc"])
        elif kind == "u":
            take(f"u{at}")
        elif kind == "finish":
            name = f"u{at}"
            complete(name)
            u = units[name]
            if at == 0:
                out = chain.run(functools.partial(finish, finish_up_kernel, "finish_up", u.order[0], (d, ff)), place, u.keep, u.got)
            elif at == 1:
                out = chain.run(functools.partial(finish, finish_down_kernel, "finish_down", u.order[0], (ff, d)), place, u.keep, u.got)
            else:
                out = chain.run(functools.partial(finish_rows, u.order[0]), place, u.keep, u.got)
            made[name] = out

    def start(name):
        if name[0] == "u":
            return begin(name)
        if name[0] == "G":
            sent[name] = [made["gn2"][int(name[1:])]]
        elif name[0] == "D":
            sent[name] = [made["down"][int(name[1:])]]
        if name[0] in "GD":
            move = other_chip
        elif name[0] == "s" and name != "sc":
            move = functools.partial(lax.ppermute, axis_name="dp", perm=swap(groups, 1 << int(name[1:])))
        else:
            move = other_core
        sent[name] = chain.after(sent[name])
        with jax.named_scope(f"send_{name}"):
            got[name] = [move(value) for value in sent[name]]

    for name in SCHEDULE:
        if name[0] == "+":
            start(name[1:])
        elif name[0] == "-":
            chain.need(units[name[1:]].got if name[1] == "u" else got[name[1:]])
        else:
            step(name)
    for at in range(3, len(bits)):
        start(f"s{at}")
        step(f"sa{at + 1}")
    totals, input_grad, block_output = made["small"], made["input_grad"], made["block_output"]
    up_grad, down_grad, attn = made["u0"], made["u1"], [*made["u2"], *made["u3"]]
    return (
        block_output,
        input_grad,
        totals[0],
        totals[1],
        attn[0].T,
        totals[6, :shard],
        attn[1].T,
        attn[2].T,
        totals[6, shard : 2 * shard],
        attn[3],
        totals[2],
        totals[3],
        totals[4],
        up_grad,
        totals[7:].reshape(-1),
        down_grad,
        totals[5],
    )


def solution(mesh):
    rows, cols, col, copied = P("dp", None), P(None, "tp"), P("tp"), P()
    return jax.shard_map(
        functools.partial(on_device, mesh.shape["dp"], mesh.shape["tp"]),
        mesh=mesh,
        in_specs=(rows, rows, copied, copied, cols, col, cols, cols, col, P("tp", None), copied, copied, copied, cols, col, P("tp", None), copied, rows),
        out_specs=(rows, rows, copied, copied, cols, col, cols, cols, col, P("tp", None), copied, copied, copied, cols, col, P("tp", None), copied),
        check_vma=False,
    )
```

```python
import functools

import jax
import jax.numpy as jnp
from jax import lax
from jax.experimental import pallas as pl
from jax.experimental.pallas import tpu as pltpu
from jax.sharding import PartitionSpec as P

HEAD = 64
SEQ_LEN = 256
EPS = 1e-06
SCALE = 0.125
NEG = -1000000000.0
ROOT_HALF = 0.7071067811865476
INV_ROOT_TAU = 0.3989422804014327
F32 = jnp.float32
BF16 = jnp.bfloat16
VMEM_LIMIT = 14 * 1024 * 1024


def dot_nn(a, b):
    return lax.dot_general(a, b, (((1,), (0,)), ((), ())), preferred_element_type=F32)


def dot_nt(a, b):
    return lax.dot_general(a, b, (((1,), (1,)), ((), ())), preferred_element_type=F32)


def dot_tn(a, b):
    return lax.dot_general(a, b, (((0,), (0,)), ((), ())), preferred_element_type=F32)


def standardize(values):
    centred = values - jnp.mean(values, axis=-1, keepdims=True)
    spread = jnp.mean(centred * centred, axis=-1, keepdims=True)
    scaler = lax.rsqrt(spread + EPS)
    return centred * scaler, scaler


def norm_back(grad_normed, gain, normed, scaler):
    scaled = grad_normed * gain
    centred = scaled - jnp.mean(scaled, axis=-1, keepdims=True)
    return scaler * (centred - normed * jnp.mean(scaled * normed, axis=-1, keepdims=True))


def gelu_parts(hidden):
    cumul = 0.5 * (1.0 + lax.erf(hidden * ROOT_HALF))
    return hidden * cumul, cumul + hidden * (jnp.exp(-0.5 * hidden * hidden) * INV_ROOT_TAU)


def segment_at(pieces_ref, row, amount, shape, axis):
    place = lax.broadcasted_iota(jnp.int32, shape, axis)
    end = jnp.int32(0)
    segment = jnp.zeros(shape, jnp.int32)
    for k in range(amount):
        end = end + pieces_ref[row, k]
        segment = segment + (place >= end).astype(jnp.int32)
    return segment


def mask_bias(pieces_ref, row, amount):
    shape = (SEQ_LEN, SEQ_LEN)
    down = segment_at(pieces_ref, row, amount, shape, 0)
    across = segment_at(pieces_ref, row, amount, shape, 1)
    same = (down == across) & (across < amount - 1)
    diagonal = lax.broadcasted_iota(jnp.int32, shape, 0) == lax.broadcasted_iota(jnp.int32, shape, 1)
    return jnp.where(same | diagonal, 0.0, NEG).astype(F32)


def keep_rows(pieces_ref, row, amount):
    segment = segment_at(pieces_ref, row, amount, (SEQ_LEN, 1), 0)
    return (segment < amount - 1).astype(F32)


def head_lanes(shape):
    return lax.broadcasted_iota(jnp.int32, shape, 1) < HEAD


def both_sides(values, low_lanes):
    zero = jnp.zeros_like(values)
    return jnp.concatenate([jnp.where(low_lanes, values, zero), jnp.where(low_lanes, zero, values)], axis=0)


def attend(qkv_ref, rows, bias, width):
    low_lanes = head_lanes((SEQ_LEN, 2 * HEAD))
    lane = lax.broadcasted_iota(jnp.int32, (SEQ_LEN, 2 * HEAD), 1)
    logs = jnp.zeros((SEQ_LEN, 2 * HEAD), F32)
    pairs = range(width // (2 * HEAD))
    where = [[slice(k * width + p * 2 * HEAD, k * width + (p + 1) * 2 * HEAD) for k in range(3)] for p in pairs]
    scores = [dot_nt(both_sides(qkv_ref[rows, where[p][0]], low_lanes), qkv_ref[rows, where[p][1]]) for p in pairs]
    mixed = []
    for p in pairs:
        probs = []
        for side in range(2):
            mine = scores[p][side * SEQ_LEN : (side + 1) * SEQ_LEN] + bias
            largest = jnp.max(mine, axis=-1, keepdims=True)
            weights = jnp.exp(mine - largest)
            totals = jnp.sum(weights, axis=-1, keepdims=True)
            probs.append((weights * (1.0 / totals)).astype(BF16))
            logs = jnp.where(lane == 2 * p + side, largest + jnp.log(totals), logs)
        out = dot_nn(jnp.concatenate(probs, axis=0), qkv_ref[rows, where[p][2]])
        mixed.append(jnp.where(low_lanes, out[:SEQ_LEN], out[SEQ_LEN:]).astype(BF16))
    return jnp.concatenate(mixed, axis=1), logs


def held(*_):
    return pl.BlockSpec(memory_space=pltpu.VMEM)


def seq_rows(seq):
    return pl.ds(pl.multiple_of(seq * SEQ_LEN, SEQ_LEN), SEQ_LEN)


def anywhere(*_):
    return pl.BlockSpec(memory_space=pltpu.HBM)


def call(kernel, name, scalars, operands, outs, grid=(1,), scratch=(), loose=0, limit=VMEM_LIMIT, us=1.0):
    return pl.pallas_call(
        kernel,
        grid_spec=pltpu.PrefetchScalarGridSpec(
            num_scalar_prefetch=len(scalars), grid=grid, in_specs=[anywhere()] * loose + [held()] * (len(operands) - loose), out_specs=[held()] * len(outs), scratch_shapes=list(scratch)),
        out_shape=[jax.ShapeDtypeStruct(shape, dtype) for shape, dtype in outs],
        compiler_params=pltpu.CompilerParams(vmem_limit_bytes=limit),
        cost_estimate=pl.CostEstimate(flops=int(us * 5e8), bytes_accessed=int(us * 1e6), transcendentals=0),
        name=name,
    )(*scalars, *operands)


def copy_all(copies, sems):
    started = [pltpu.make_async_copy(source, target, sems.at[at]) for at, (source, target) in enumerate(copies)]
    for copy in started:
        copy.start()
    return started


def column_sum(values):
    return jnp.sum(values.reshape(values.shape[0] // 8, 8, values.shape[1]), axis=0)


VECTORS = 6
BITS = 2
TAIL = 16


def vectors_kernel(shard, small_ref, vectors_ref, row_ref):
    d = vectors_ref.shape[1]

    def vector(at, size):
        return small_ref[pl.ds(at, size)].reshape(1, size)

    vectors_ref[...] = jnp.zeros_like(vectors_ref)
    for k in range(VECTORS):
        vectors_ref[k : k + 1, :] = vector(k * d, d)
    ff = row_ref.shape[1] - 4 * shard
    row_ref[:, 4 * shard :] = vector(VECTORS * d, ff)
    zero = jnp.zeros((1, shard), F32)
    at = VECTORS * d + ff
    row_ref[:, : 4 * shard] = jnp.concatenate([vector(at, shard), zero, vector(at + shard, shard), zero], axis=1)


def gather_vectors(small, shard, d, ff):
    return call(functools.partial(vectors_kernel, shard), "vectors", (), (small,), [((8, d), F32), ((1, 4 * shard + ff), F32)])


def join_kernel(place_ref, first_ref, second_ref, v_ref, row_ref, out_ref):
    shard, d = first_ref.shape
    out_ref[pl.ds(pl.multiple_of(place_ref[BITS] * shard, shard), shard), :] = first_ref[...]
    out_ref[pl.ds(pl.multiple_of((1 - place_ref[BITS]) * shard, shard), shard), :] = second_ref[...]
    out_ref[2 * shard : 3 * shard, :] = v_ref[...]
    rest = row_ref[:, : 4 * shard]
    rows = []
    for _ in range(3):
        part = rest.astype(BF16).astype(F32)
        rows.append(part)
        rest = rest - part
    rows.append(jnp.zeros((TAIL - 3, 4 * shard), F32))
    out_ref[3 * shard :, : 4 * shard] = jnp.concatenate(rows, axis=0).astype(BF16)


def join_weights(place, first, second, v, row):
    shard, d = first.shape
    return call(join_kernel, "join", (place,), (first, second, v, row), [((3 * shard + TAIL, d), BF16)])[0]


def spread_bias(a, b, shard):
    return a + jnp.concatenate([jnp.zeros((1, shard), F32), b[:, : 3 * shard]], axis=1)


def project(lowered, w_ref, bias, qkv_ref, at, width):
    for k in range(3):
        proj = dot_nt(lowered, w_ref[k * width : (k + 1) * width, :])
        if k == 0:
            proj = (proj + bias[:, :width]).astype(BF16) * jnp.asarray(SCALE, BF16)
        elif k == 2:
            proj = proj + bias[:, width:]
        qkv_ref[at, k * width : (k + 1) * width] = proj.astype(BF16)


def project_kernel(shard, place_ref, x_ref, vectors_ref, a_ref, b_ref, *refs):
    w_refs, (w_ref, normed_ref, qkv_ref) = refs[:6], refs[6:]
    step = pl.program_id(0)
    width = 2 * shard

    @pl.when(step == 0)
    def _():
        for k, ref in enumerate(w_refs):
            to = (k % 3) * width + (k // 3) * shard
            w_ref[to : to + shard, :] = ref[...]

    normed, _ = standardize(x_ref[seq_rows(place_ref[0] + step), :].astype(F32))
    lowered = (normed * vectors_ref[0:1, :] + vectors_ref[1:2, :]).astype(BF16)
    at = seq_rows(step)
    normed_ref[at, :] = lowered
    bias = spread_bias(a_ref[:, : 4 * shard], b_ref[:, : 4 * shard], shard)
    project(lowered, w_ref, bias, qkv_ref, at, width)


def project_own(rows, place, x, vectors, a, b, weights):
    shard, d = weights[0].shape
    outs = [((6 * shard, d), BF16), ((rows, d), BF16), ((rows, 6 * shard), BF16)]
    return call(functools.partial(project_kernel, shard), "project_own", (place,), (x, vectors, a, b, *weights), outs, (rows // SEQ_LEN,), us=3.5)


def attend_kernel(amount, width, place_ref, pieces_ref, qkv_ref, wa_ref, wb_ref, mixed_ref, logs_ref, part_ref, wo_ref):
    step = pl.program_id(0)

    @pl.when(step == 0)
    def _():
        wo_ref[: width // 2, :] = wa_ref[...]
        wo_ref[width // 2 :, :] = wb_ref[...]

    at = seq_rows(step)
    mixed, logs = attend(qkv_ref, at, mask_bias(pieces_ref, place_ref[0] + step, amount), width)
    logs_ref[pl.ds(pl.multiple_of(step * 8, 8), 8), :] = logs.T[:8, :]
    mixed_ref[at, :] = mixed
    part_ref[at, :] = dot_nn(mixed, wo_ref[...])


def attend_own(place, pieces, qkv, wa, wb):
    seqs, amount = pieces.shape[0] // 2, pieces.shape[1]
    width, d = 2 * wa.shape[0], wa.shape[1]
    rows = seqs * SEQ_LEN
    outs = [((rows, width), BF16), ((seqs * 8, SEQ_LEN), F32), ((rows, d), F32), ((width, d), BF16)]
    return call(functools.partial(attend_kernel, amount, width), "attend_own", (place, pieces), (qkv, wa, wb), outs, (seqs,), us=4.9)


def other_kernel(amount, shard, place_ref, pieces_ref, a_ref, b_ref, normed_in_ref, w_ref, qkv_ref, logs_ref, mixed_ref):
    step = pl.program_id(0)
    width = 2 * shard

    @pl.when(step == 0)
    def _():
        for side, ref in enumerate((a_ref, b_ref)):
            for k in range(3):
                to = k * width + side * shard
                w_ref[to : to + shard, :] = ref[k * shard : (k + 1) * shard, :]

    at = seq_rows(step)
    a, b = (jnp.sum(ref[3 * shard : 3 * shard + 3, : 4 * shard].astype(F32), axis=0, keepdims=True) for ref in (a_ref, b_ref))
    project(normed_in_ref[at, :], w_ref, spread_bias(a, b, shard), qkv_ref, at, width)
    mixed, logs = attend(qkv_ref, at, mask_bias(pieces_ref, place_ref[0] + step, amount), width)
    logs_ref[pl.ds(pl.multiple_of(step * 8, 8), 8), :] = logs.T[:8, :]
    mixed_ref[at, :] = mixed


def attend_other(place, pieces, a, b, normed):
    seqs, amount = pieces.shape[0] // 2, pieces.shape[1]
    shard, d = (a.shape[0] - TAIL) // 3, a.shape[1]
    rows = seqs * SEQ_LEN
    outs = [((6 * shard, d), BF16), ((rows, 6 * shard), BF16), ((seqs * 8, SEQ_LEN), F32), ((rows, 2 * shard), BF16)]
    return call(functools.partial(other_kernel, amount, shard), "attend_other", (place, pieces), (a, b, normed), outs, (seqs,), us=6.0)


def middle_kernel(amount, place_ref, pieces_ref, wa_ref, wb_ref, x_ref, mixed_ref, part_in_ref, vectors_ref, w_ref, middle_ref, normed_ref, sum_ref):
    step = pl.program_id(0)
    shard = wa_ref.shape[0]
    first = place_ref[0] * SEQ_LEN

    @pl.when(step == 0)
    def _():
        w_ref[:shard, :] = wa_ref[...]
        w_ref[shard:, :] = wb_ref[...]

    at = seq_rows(step)
    sum_ref[...] = dot_nn(mixed_ref[at, :], w_ref[...])
    keep_all = keep_rows(pieces_ref, place_ref[0] + step, amount)
    block = 64
    for r in range(0, SEQ_LEN, block):
        here = pl.ds(pl.multiple_of(step * SEQ_LEN + r, block), block)
        added = part_in_ref[here, :] + sum_ref[r : r + block, :] + vectors_ref[2:3, :]
        middle = x_ref[pl.ds(pl.multiple_of(first + step * SEQ_LEN + r, block), block), :].astype(F32) + keep_all[r : r + block] * added
        middle_ref[here, :] = middle
        normed, _ = standardize(middle)
        normed_ref[here, :] = (normed * vectors_ref[3:4, :] + vectors_ref[4:5, :]).astype(BF16)


def middle_rows(place, pieces, wa, wb, x, mixed, part, vectors):
    (rows, width), d = mixed.shape, x.shape[1]
    outs = [((width, d), BF16), ((rows, d), F32), ((rows, d), BF16)]
    return call(functools.partial(middle_kernel, pieces.shape[1]), "middle", (place, pieces), (wa, wb, x, mixed, part, vectors), outs, (rows // SEQ_LEN,),
                [pltpu.VMEM((SEQ_LEN, d), F32)], us=3.0)


def mlp_kernel(amount, first, seqs, place_ref, pieces_ref, n2_ref, cot_ref, ba_ref, bb_ref, upa_ref, upb_ref, dna_ref, dnb_ref,
               active_ref, gh_ref, gb_ref, sums_ref, n2_out_ref, *gn2_refs):
    ff = upa_ref.shape[1]
    skip = ba_ref.shape[1] - ff
    block = 256 if ff % 256 == 0 else ff
    total = [None] * (2 * ff // block)
    for s in range(seqs):
        rows = slice(s * SEQ_LEN, (s + 1) * SEQ_LEN)
        here = slice((first + s) * SEQ_LEN, (first + s + 1) * SEQ_LEN)
        keep = keep_rows(pieces_ref, place_ref[0] + first + s, amount)
        branch = (keep * cot_ref[seq_rows(place_ref[0] + first + s), :].astype(F32)).astype(BF16)
        gb_ref[rows, :] = branch
        n2 = n2_ref[here, :]
        n2_out_ref[rows, :] = n2
        for side, (up_ref, dn_ref, bias_ref) in enumerate(((upa_ref, dna_ref, ba_ref), (upb_ref, dnb_ref, bb_ref))):
            for j in range(0, ff, block):
                at = slice(side * ff + j, side * ff + j + block)
                hidden = dot_nn(n2, up_ref[:, j : j + block]) + bias_ref[:, skip + j : skip + j + block]
                active, slope = gelu_parts(hidden)
                active_ref[rows, at] = active.astype(BF16)
                grad_active = dot_nt(branch, dn_ref[j : j + block, :])
                grad_hidden = (grad_active * slope).astype(BF16)
                gh_ref[rows, at] = grad_hidden
                part = jnp.sum(grad_hidden.astype(F32), axis=0, keepdims=True)
                k = at.start // block
                total[k] = part if total[k] is None else total[k] + part
        gn2_refs[s][...] = (dot_nt(gh_ref[rows, :ff], upa_ref[...]) + dot_nt(gh_ref[rows, ff:], upb_ref[...])).astype(BF16)
    for k, part in enumerate(total):
        sums_ref[:, k * block : (k + 1) * block] = part


def mlp_rows(first, seqs, place, pieces, n2, cot, bias, bias_b, upa, upb, dna, dnb):
    d, ff = upa.shape
    rows = seqs * SEQ_LEN
    outs = [((rows, 2 * ff), BF16), ((rows, 2 * ff), BF16), ((rows, d), BF16), ((1, 2 * ff), F32), ((rows, d), BF16)] + [((SEQ_LEN, d), BF16)] * seqs
    return call(functools.partial(mlp_kernel, pieces.shape[1], first, seqs), "mlp", (place, pieces), (n2, cot, bias, bias_b, upa, upb, dna, dnb), outs, us=2.7 * seqs)


def down_kernel(count, dna_ref, dnb_ref, *refs):
    ff = dna_ref.shape[0]
    out_ref = refs[-1]
    at = 0
    for active_ref in refs[:count]:
        for r in range(0, active_ref.shape[0], SEQ_LEN):
            rows = slice(r, r + SEQ_LEN)
            out_ref[at : at + SEQ_LEN, :] = (dot_nn(active_ref[rows, :ff], dna_ref[...]) + dot_nn(active_ref[rows, ff:], dnb_ref[...])).astype(BF16)
            at += SEQ_LEN


def down_rows(dna, dnb, actives):
    rows, d = sum(a.shape[0] for a in actives), dna.shape[1]
    return call(functools.partial(down_kernel, len(actives)), "down", (), (dna, dnb, *actives), [((rows, d), BF16)], us=2.0)


def sent_kernel(count, side, *refs):
    out_ref = refs[-1]
    size = out_ref.shape[0]
    block = 256 if size % 256 == 0 else size
    for j in range(0, size, block):
        at = slice(side * size + j, side * size + j + block)
        total = sum(dot_tn(refs[k][:, at], refs[count + k][...]) for k in range(count))
        out_ref[j : j + block, :] = total.astype(BF16)


def grad_sent(side, lefts, rights):
    size, d = lefts[0].shape[1] // 2, rights[0].shape[1]
    return call(functools.partial(sent_kernel, len(lefts), side), "grad_sent", (), (*lefts, *rights), [((size, d), BF16)], us=1.1)


def kept_kernel(count, bit, place_ref, *refs):
    add_ref, send_ref, keep_ref = refs[-3:]
    half = keep_ref.shape[0]
    for which, out_ref in enumerate((send_ref, keep_ref)):
        mine = place_ref[BITS + bit] if which else 1 - place_ref[BITS + bit]
        at = pl.ds(pl.multiple_of(mine * half, half), half)
        total = sum(dot_tn(refs[k][:, at], refs[count + k][...]) for k in range(count))
        out_ref[...] = (total + add_ref[at, :].astype(F32)).astype(BF16)


def grad_kept(bit, place, lefts, rights, add):
    half, d = lefts[0].shape[1] // 4, rights[0].shape[1]
    return call(functools.partial(kept_kernel, len(lefts), bit), "grad_kept", (place,), (*lefts, *rights, add), [((half, d), BF16)] * 2, us=1.7)


def attn_dots(refs, attns, n1_ref, seqs, shard, side, kind):
    width = 2 * shard
    at = slice(kind * width + side * shard, kind * width + (side + 1) * shard)
    rights = [attns[s][...] if kind == 3 else n1_ref[s * SEQ_LEN : (s + 1) * SEQ_LEN, :] for s in range(seqs)]
    return sum(dot_tn(refs[s][:, at], rights[s]) for s in range(seqs))


def attn_sent_kernel(seqs, kinds, *refs):
    out_ref = refs[-1]
    shard = out_ref.shape[0] // len(kinds)
    for k, kind in enumerate(kinds):
        out_ref[k * shard : (k + 1) * shard, :] = attn_dots(refs[:seqs], refs[seqs : 2 * seqs], refs[2 * seqs], seqs, shard, 1, kind).astype(BF16)


def attn_sent(kinds, lefts, attns, n1):
    shard, d = lefts[0].shape[1] // 8, n1.shape[1]
    return call(functools.partial(attn_sent_kernel, len(lefts), kinds), "attn_sent", (), (*lefts, *attns, n1), [((len(kinds) * shard, d), BF16)], us=0.9)


def attn_kept_kernel(seqs, kinds, bit, place_ref, *refs):
    add_ref, send_ref, keep_ref, both_ref = refs[-4:]
    shard = keep_ref.shape[0]
    for which, kind in enumerate(kinds):
        total = attn_dots(refs[:seqs], refs[seqs : 2 * seqs], refs[2 * seqs], seqs, shard, 0, kind)
        at = slice(which * shard, (which + 1) * shard)
        both_ref[at, :] = (total + add_ref[at, :].astype(F32)).astype(BF16)
    mine = place_ref[BITS + bit]
    for out_ref, chosen in ((keep_ref, mine), (send_ref, 1 - mine)):
        out_ref[...] = both_ref[pl.ds(pl.multiple_of(chosen * shard, shard), shard), :]


def attn_kept(kinds, bit, place, lefts, attns, n1, add):
    shard, d = lefts[0].shape[1] // 8, n1.shape[1]
    return call(functools.partial(attn_kept_kernel, len(lefts), kinds, bit), "attn_kept", (place,), (*lefts, *attns, n1, add), [((shard, d), BF16)] * 2,
                scratch=[pltpu.VMEM((2 * shard, d), BF16)], us=1.2)


def attend_back(qkv_ref, rows, gm_ref, logs_ref, first, bias, width, grads_ref):
    low_lanes = head_lanes((SEQ_LEN, 2 * HEAD))
    pairs = range(width // (2 * HEAD))
    where = [[slice(k * width + p * 2 * HEAD, k * width + (p + 1) * 2 * HEAD) for k in range(3)] for p in pairs]
    scores = [dot_nt(both_sides(qkv_ref[rows, where[p][1]], low_lanes), qkv_ref[rows, where[p][0]]) for p in pairs]
    grad_probs = [dot_nt(both_sides(qkv_ref[rows, where[p][2]], low_lanes), gm_ref[:, where[p][0]]) for p in pairs]
    for p in pairs:
        probs, grad_scores = [], []
        for side in range(2):
            mine = slice(side * SEQ_LEN, (side + 1) * SEQ_LEN)
            head = first + 2 * p + side
            prob = jnp.exp(scores[p][mine] + bias - logs_ref[head : head + 1, :])
            inner = jnp.sum(grad_probs[p][mine] * prob, axis=0, keepdims=True)
            grad_scores.append((prob * (grad_probs[p][mine] - inner)).astype(BF16))
            probs.append(prob.astype(BF16))
        grad_key = dot_nn(jnp.concatenate(grad_scores, axis=0), qkv_ref[rows, where[p][0]])
        grad_value = dot_nn(jnp.concatenate(probs, axis=0), gm_ref[:, where[p][0]])
        grad_query = dot_tn(jnp.concatenate(grad_scores, axis=1), qkv_ref[rows, where[p][1]])
        grads_ref[:, where[p][0]] = (jnp.where(low_lanes, grad_query[:SEQ_LEN], grad_query[SEQ_LEN:]) * SCALE).astype(BF16)
        grads_ref[:, where[p][1]] = jnp.where(low_lanes, grad_key[:SEQ_LEN], grad_key[SEQ_LEN:]).astype(BF16)
        grads_ref[:, where[p][2]] = jnp.where(low_lanes, grad_value[:SEQ_LEN], grad_value[SEQ_LEN:]).astype(BF16)


def own_back_kernel(amount, seq, place_ref, pieces_ref, cot_ref, middle_ref, own_ref, got_ref, vectors_ref, qkv_ref, logs_ref, mixed_ref, w_ref, wo_ref,
                    grad_ref, all_ref, attn_ref, part_ref, sums_ref, gm_ref):
    row = place_ref[0] + seq
    width = mixed_ref.shape[1]
    d = cot_ref.shape[1]
    keep_all = keep_rows(pieces_ref, row, amount)
    sums = [jnp.zeros((8, d), F32)] * 4
    block = 32
    for r in range(0, SEQ_LEN, block):
        at = slice(r, r + block)
        keep = keep_all[at]
        cot = cot_ref[pl.ds(pl.multiple_of(row * SEQ_LEN + r, block), block), :].astype(F32)
        gn2 = own_ref[at, :].astype(F32) + got_ref[at, :].astype(F32)
        normed, scaler = standardize(middle_ref[seq * SEQ_LEN + r : seq * SEQ_LEN + r + block, :])
        grad_middle = cot + norm_back(gn2, vectors_ref[3:4, :], normed, scaler)
        attn = (keep * grad_middle).astype(BF16)
        attn_ref[at, :] = attn
        grad_ref[at, :] = grad_middle
        terms = (attn.astype(F32), gn2 * normed, gn2, (keep * cot).astype(BF16).astype(F32))
        sums = [s + column_sum(t) for s, t in zip(sums, terms)]
    sums_ref[...] = jnp.zeros_like(sums_ref)
    for k in range(4):
        sums_ref[2 + k : 3 + k, :] = jnp.sum(sums[k], axis=0, keepdims=True)
    gm_ref[...] = dot_nt(attn_ref[...], wo_ref[...]).astype(BF16)
    rows = slice(seq * SEQ_LEN, (seq + 1) * SEQ_LEN)
    attend_back(qkv_ref, rows, gm_ref, logs_ref, 8 * seq, mask_bias(pieces_ref, row, amount), width, all_ref)
    part_ref[...] = dot_nn(all_ref[:, : 3 * width], w_ref[...])
    all_ref[:, 3 * width :] = mixed_ref[rows, :]
    sums_ref[6:7, :width] = jnp.sum(all_ref[:, :width].astype(F32), axis=0, keepdims=True)
    sums_ref[7:8, :width] = jnp.sum(all_ref[:, 2 * width : 3 * width].astype(F32), axis=0, keepdims=True)


def own_back(seq, place, pieces, cot, middle, own, got, vectors, qkv, logs, mixed, w, wo):
    d, width = cot.shape[1], mixed.shape[1]
    outs = [((SEQ_LEN, d), F32), ((SEQ_LEN, 4 * width), BF16), ((SEQ_LEN, d), BF16), ((SEQ_LEN, d), F32), ((8, d), F32)]
    return call(functools.partial(own_back_kernel, pieces.shape[1], seq), "own_back", (place, pieces),
                (cot, middle, own, got, vectors, qkv, logs, mixed, w, wo), outs, scratch=[pltpu.VMEM((SEQ_LEN, width), BF16)], us=5.2)


def other_back_kernel(amount, seq, place_ref, pieces_ref, x_ref, grad_in_ref, attn_ref, part_ref, vectors_ref, qkv_ref, logs_ref, w_ref, wo_ref,
                      grad_ref, sums_ref, gm_ref, all_ref, sum_ref):
    row = place_ref[0] + seq
    width = gm_ref.shape[1]
    d = x_ref.shape[1]
    bias = mask_bias(pieces_ref, row, amount)
    gm_ref[...] = dot_nt(attn_ref[...], wo_ref[...]).astype(BF16)
    rows = slice(seq * SEQ_LEN, (seq + 1) * SEQ_LEN)
    attend_back(qkv_ref, rows, gm_ref, logs_ref, 8 * seq, bias, width, all_ref)
    sum_ref[...] = dot_nn(all_ref[...], w_ref[...])
    sums = [jnp.zeros((8, d), F32)] * 2
    block = 32
    for r in range(0, SEQ_LEN, block):
        at = slice(r, r + block)
        gn1 = part_ref[at, :] + sum_ref[at, :]
        normed, scaler = standardize(x_ref[pl.ds(pl.multiple_of(row * SEQ_LEN + r, block), block), :].astype(F32))
        grad_ref[at, :] = grad_in_ref[at, :] + norm_back(gn1, vectors_ref[0:1, :], normed, scaler)
        sums = [s + column_sum(t) for s, t in zip(sums, (gn1 * normed, gn1))]
    sums_ref[...] = jnp.zeros_like(sums_ref)
    for k in range(2):
        sums_ref[k : k + 1, :] = jnp.sum(sums[k], axis=0, keepdims=True)


def other_back(seq, place, pieces, x, grad_in, attn, part, vectors, qkv, logs, w, wo):
    d, width = wo.shape[1], wo.shape[0]
    outs = [((SEQ_LEN, d), F32), ((8, d), F32)]
    return call(functools.partial(other_back_kernel, pieces.shape[1], seq), "other_back", (place, pieces),
                (x, grad_in, attn, part, vectors, qkv, logs, w, wo), outs,
                scratch=[pltpu.VMEM((SEQ_LEN, width), BF16), pltpu.VMEM((SEQ_LEN, 3 * width), BF16), pltpu.VMEM((SEQ_LEN, d), F32)], us=4.5)


def output_kernel(amount, place_ref, pieces_ref, middle_ref, vectors_ref, own_ref, got_ref, out_ref):
    block = 64
    for seq in range(out_ref.shape[0] // SEQ_LEN):
        keep_all = keep_rows(pieces_ref, place_ref[0] + seq, amount)
        for r in range(0, SEQ_LEN, block):
            at = slice(seq * SEQ_LEN + r, seq * SEQ_LEN + r + block)
            total = own_ref[at, :].astype(F32) + got_ref[at, :].astype(F32) + vectors_ref[5:6, :]
            out_ref[at, :] = (middle_ref[at, :] + keep_all[r : r + block] * total).astype(BF16)


def output_rows(place, pieces, middle, vectors, own, got):
    return call(functools.partial(output_kernel, pieces.shape[1]), "block_output", (place, pieces),
                (middle, vectors, own, got), [(middle.shape, BF16)], us=1.4)


def both_kernel(count, place_ref, *refs):
    out_ref, sems = refs[-2:]
    size = refs[0].shape[0]
    copies = []
    for k in range(2 * count):
        at = (place_ref[1] if k < count else 1 - place_ref[1]) * count + k % count
        copies.append(pltpu.make_async_copy(refs[k], out_ref.at[pl.ds(pl.multiple_of(at * size, size), size)], sems.at[k]))
        copies[-1].start()
    for copy in copies:
        copy.wait()


def both_cores(place, mine, theirs):
    count = len(mine)
    rows, d = mine[0].shape
    return pl.pallas_call(
        functools.partial(both_kernel, count),
        grid_spec=pltpu.PrefetchScalarGridSpec(
            num_scalar_prefetch=1, grid=(1,), in_specs=[held()] * (2 * count), out_specs=pl.BlockSpec(memory_space=pl.ANY),
            scratch_shapes=[pltpu.SemaphoreType.DMA((2 * count,))]),
        out_shape=jax.ShapeDtypeStruct((2 * count * rows, d), mine[0].dtype),
        compiler_params=pltpu.CompilerParams(vmem_limit_bytes=VMEM_LIMIT),
        cost_estimate=pl.CostEstimate(flops=1, bytes_accessed=1, transcendentals=0),
        name="both_cores",
    )(place, *mine, *theirs)


def swap(size, bit):
    return [(i, i ^ bit) for i in range(size)]


def tie(values, *after):
    return lax.optimization_barrier((values, after))[0]


def merge_kernel(at, place_ref, keep_ref, got_ref, send_ref, out_ref):
    size = out_ref.shape[0]
    for which, ref in enumerate((send_ref, out_ref)):
        bit = place_ref[BITS + at] if which else 1 - place_ref[BITS + at]
        rows = pl.ds(pl.multiple_of(bit * size, size), size)
        ref[...] = (keep_ref[rows, :].astype(F32) + got_ref[rows, :].astype(F32)).astype(BF16)


def merge(bit, place, keep, got):
    rows, d = keep.shape
    half = rows // 2
    if half % 16:
        total = (keep.astype(F32) + got.astype(F32)).astype(BF16)
        low = place[BITS + bit] == 0
        return jnp.where(low, total[half:], total[:half]), jnp.where(low, total[:half], total[half:])
    return call(functools.partial(merge_kernel, bit), "merge", (place,), (keep, got), [((half, d), BF16)] * 2, us=0.6)


def add_kernel(keep_ref, got_ref, out_ref):
    out_ref[...] = (keep_ref[...].astype(F32) + got_ref[...].astype(F32)).astype(out_ref.dtype)


def add(keep, got):
    return call(add_kernel, "add", (), (keep, got), [(keep.shape, keep.dtype)])[0]


def grow_kernel(at, place_ref, keep_ref, got_ref, out_ref):
    size = keep_ref.shape[0]
    out_ref[pl.ds(pl.multiple_of(place_ref[BITS + at] * size, size), size), :] = keep_ref[...]
    out_ref[pl.ds(pl.multiple_of((1 - place_ref[BITS + at]) * size, size), size), :] = got_ref[...]


def grow(bit, place, keep, got):
    rows, d = keep.shape
    if rows % 16:
        return jnp.where(place[BITS + bit] == 0, jnp.concatenate([keep, got]), jnp.concatenate([got, keep]))
    return call(functools.partial(grow_kernel, bit), "grow", (place,), (keep, got), [((2 * rows, d), BF16)])[0]


def finish_up_kernel(at, place_ref, keep_ref, got_ref, out_ref):
    size = keep_ref.shape[0]
    out_ref[:, pl.ds(pl.multiple_of(place_ref[BITS + at] * size, 128), size)] = keep_ref[...].astype(F32).T
    out_ref[:, pl.ds(pl.multiple_of((1 - place_ref[BITS + at]) * size, 128), size)] = got_ref[...].astype(F32).T


def finish_down_kernel(at, place_ref, keep_ref, got_ref, out_ref):
    size = keep_ref.shape[0]
    out_ref[pl.ds(pl.multiple_of(place_ref[BITS + at] * size, size), size), :] = keep_ref[...].astype(F32)
    out_ref[pl.ds(pl.multiple_of((1 - place_ref[BITS + at]) * size, size), size), :] = got_ref[...].astype(F32)


def finish(kernel, name, bit, shape, place, keep, got):
    return call(functools.partial(kernel, bit), name, (place,), (keep, got), [(shape, F32)])[0]


def rows_kernel(at, place_ref, keep_ref, got_ref, low_ref, high_ref):
    mine = place_ref[BITS + at] == 0
    keep, got = keep_ref[...].astype(F32), got_ref[...].astype(F32)
    low_ref[...] = jnp.where(mine, keep, got)
    high_ref[...] = jnp.where(mine, got, keep)


def finish_rows(bit, place, keep, got):
    return call(functools.partial(rows_kernel, bit), "finish_rows", (place,), (keep, got), [(keep.shape, F32)] * 2, us=1.6)


class Unit:
    def __init__(self, groups, order, place, send, keep):
        self.groups, self.order, self.place = groups, order, place
        self.send, self.keep, self.step = send, keep, 0
        self.last = 2 * len(order) - 1

    def start(self):
        count = len(self.order)
        at = self.step if self.step < count else 2 * count - 1 - self.step
        self.got = lax.ppermute(self.send, "dp", swap(self.groups, 1 << self.order[at]))

    def take(self):
        count = len(self.order)
        if self.step < count - 1:
            self.send, self.keep = merge(self.order[self.step + 1], self.place, self.keep, self.got)
        elif self.step == count - 1:
            self.keep = add(self.keep, self.got)
            self.send = self.keep
        elif self.step < 2 * count - 1:
            self.keep = grow(self.order[2 * count - 1 - self.step], self.place, self.keep, self.got)
            self.send = self.keep
        self.step += 1


class Chain:
    def __init__(self):
        self.last = ()

    def run(self, kernel, *args, need=()):
        args = tie(args, self.last, need)
        out = kernel(*args)
        self.last = out
        return out

    def after(self, values):
        return tie(values, self.last)

    def need(self, values):
        self.last = (self.last, values)


SCHEDULE = (
    "mlp0", "mlp1", "+G2", "+G1", "gs0", "gs1", "+cb0", "+cb1", "down", "gk0", "+u0", "gk1", "+u1", "ob2", "+G0", "xb2", "u0", "+u0",
    "-cb1", "ob1", "u1", "+u1", "ob0", "ao0", "ao1", "+D0", "+ca0", "u0", "u1", "+u1", "+ca1", "+u0", "xb0", "u0", "+u0", "ak0", "+u2",
    "u1", "+u1", "ak1", "u0", "+u0", "+u3", "xb1", "sums", "u1", "+u1", "u2", "+u2", "u3", "out", "+u3", "+sc", "sa0", "+s0", "sa1", "u2",
    "+oc", "+s1", "u1", "+u1", "u3", "u0", "sa2", "+u3", "+u0", "+u2", "u3", "+u3", "u2", "+u2", "u3", "+u3", "+gc1", "u2", "+u2",
    "finish1", "+gc2", "finish0", "u3", "+u3", "u2", "+u2", "+gc0", "bout", "+s2", "gin", "finish2", "sa3", "finish3",
)
ORDERS = ((0, 2, 1), (1, 0, 2), (0, 1, 2), (1, 0, 2))


def small_kernel(seqs, shard, *refs):
    own, oth, ups, outs = refs[:seqs], refs[seqs : 2 * seqs], refs[2 * seqs : -2], refs[-2:]
    total = sum(r[...] for r in own) + sum(r[...] for r in oth)
    up = sum(r[...] for r in ups)
    d = total.shape[1]
    ff = up.shape[1] // 2
    for side, out_ref in enumerate(outs):
        out_ref[0:6, :] = total[0:6]
        at = slice(side * shard, (side + 1) * shard)
        out_ref[6:7, :] = jnp.concatenate([total[6:7, at], total[7:8, at], jnp.zeros((1, d - 2 * shard), F32)], axis=1)
        for k in range(ff // d):
            out_ref[7 + k : 8 + k, :] = up[:, side * ff + k * d : side * ff + (k + 1) * d]


def small_sums(shard, own, oth, ups):
    seqs, d = len(own), own[0].shape[1]
    rows = 7 + ups[0].shape[1] // 2 // d
    operands = [*own, *oth, *ups]
    return call(functools.partial(small_kernel, seqs, shard), "small_sums", (), operands, [((rows, d), F32)] * 2)


def on_device(groups, tp, block_input, pieces, gain_one, shift_one, query_weight, query_bias, key_weight, value_weight, value_bias,
              out_weight, out_bias, gain_two, shift_two, up_weight, up_bias, down_weight, down_bias, cotangent):
    d = block_input.shape[1]
    shard = query_weight.shape[1]
    ff = up_weight.shape[1]
    seqs = pieces.shape[0] // 2
    core = lax.axis_index("tp") & 1
    group = lax.axis_index("dp")
    bits = list(range(groups.bit_length() - 1))
    place = jnp.stack([core * seqs, core] + [(group >> bit) & 1 for bit in bits]).astype(jnp.int32)

    def other_core(values):
        return lax.ppermute(values, "tp", swap(tp, 1))

    def other_chip(values):
        return lax.ppermute(values, "tp", swap(tp, 2))

    def next_group(values):
        return lax.ppermute(values, "dp", swap(groups, 1))

    chain = Chain()
    weights = (query_weight.T, key_weight.T, value_weight.T, out_weight)
    core_weights = [other_core(w) for w in weights]
    small = jnp.concatenate([gain_one, shift_one, out_bias, gain_two, shift_two, down_bias, up_bias, query_bias, value_bias])
    first = other_chip(jnp.where(place[BITS] == 0, weights[0], weights[1]))
    last_v, last_o = other_chip(weights[2]), other_chip(weights[3])
    vectors, biases = chain.run(functools.partial(gather_vectors, shard=shard, d=d, ff=ff), small)
    biases_b, biases_x = other_core(biases), other_chip(biases)
    w_own, n1, qkv_own = chain.run(functools.partial(project_own, seqs * SEQ_LEN), place, block_input, vectors, biases, biases_b, (*weights[:3], *core_weights[:3]))
    first, biases_x = chain.after((first, biases_x))
    second = next_group(first)
    mixed, logs_own, part, wo_own = chain.run(attend_own, place, pieces, qkv_own, weights[3], core_weights[3], need=(first, biases_x))
    up_weight, down_weight = chain.after((up_weight, down_weight))
    up_b, down_b = other_core(up_weight), other_core(down_weight)
    joined = chain.run(join_weights, place, first, second, last_v, biases_x)
    w_oth, qkv_oth, logs_oth, mixed_oth = chain.run(attend_other, place, pieces, joined, other_core(joined), n1)
    last_o = chain.after(last_o)
    wo_oth, middle, n2 = chain.run(middle_rows, place, pieces, last_o, other_core(last_o), block_input, mixed_oth, part, vectors)

    sent, got, made = {}, {}, {}
    units = {}

    def unit(name, at, send, keep):
        order = [*ORDERS[at], *bits[len(ORDERS[at]) :]]
        units[name] = Unit(groups, order, place, send, keep)

    def take(name):
        u = units[name]
        u.keep, u.got = tie((u.keep, u.got), chain.last)
        u.take()
        chain.last = u.keep

    def begin(name):
        u = units[name]
        u.send = chain.after(u.send)
        with jax.named_scope(f"send_{name}_{u.step}"):
            u.start()

    def complete(name):
        u = units[name]
        while u.step < u.last:
            take(name)
            begin(name)

    def mlp(part):
        first, count = (0, 1) if part == 0 else (1, seqs - 1)
        out = chain.run(functools.partial(mlp_rows, first, count), place, pieces, n2, cotangent, biases, biases_b, up_weight, up_b, down_weight, down_b)
        for key, value in zip(("active", "hidden", "branch", "sums", "n2"), out):
            made.setdefault(key, []).append(value)
        made.setdefault("gn2", []).extend(out[5:])

    def sides(at):
        return (made["hidden"], made["n2"]) if at == 0 else (made["active"], made["branch"])

    def step(name):
        kind, at = name.rstrip("0123456789"), name[len(name.rstrip("0123456789")) :]
        at = int(at) if at else 0
        if kind == "mlp":
            mlp(at)
        elif kind == "down":
            made["down"] = chain.run(down_rows, down_weight, down_b, made["active"])
        elif kind == "gs":
            sent[f"cb{at}"] = chain.run(functools.partial(grad_sent, 1), *sides(at))
        elif kind == "gk":
            unit(f"u{at}", at, *chain.run(functools.partial(grad_kept, ORDERS[at][0]), place, *sides(at), got[f"cb{at}"][0]))
        elif kind == "ob":
            made[f"ob{at}"] = chain.run(functools.partial(own_back, at), place, pieces, cotangent, middle, made["gn2"][at], got[f"G{at}"][0], vectors,
                                        qkv_own, logs_own, mixed, w_own, wo_own)
        elif kind in ("ao", "ak"):
            kinds = (0, 1) if at == 0 else (2, 3)
            owns = [made[f"ob{s}"] for s in range(seqs)]
            operands = ([o[1] for o in owns], [o[2] for o in owns], n1)
            if kind == "ao":
                sent[f"ca{at}"] = chain.run(functools.partial(attn_sent, kinds), *operands)
            else:
                unit(f"u{2 + at}", 2 + at, *chain.run(functools.partial(attn_kept, kinds, ORDERS[2 + at][0]), place, *operands, got[f"ca{at}"][0]))
        elif kind == "xb":
            own = made[f"ob{at}"]
            made[f"xb{at}"] = chain.run(functools.partial(other_back, at), place, pieces, block_input, own[0], own[2], own[3], vectors,
                                        qkv_oth, logs_oth, w_oth, wo_oth)
            sent[f"gc{at}"] = made[f"xb{at}"][:1]
        elif kind == "sums":
            made["small"], more = chain.run(functools.partial(small_sums, shard), [made[f"ob{s}"][4] for s in range(seqs)],
                                            [made[f"xb{s}"][1] for s in range(seqs)], made["sums"])
            sent["sc"] = [more]
        elif kind == "sa":
            made["small"] = chain.run(add, made["small"], got["sc" if at == 0 else f"s{at - 1}"][0])
            sent[f"s{at}"] = [made["small"]]
        elif kind == "out":
            sent["oc"] = chain.run(output_rows, place, pieces, middle, vectors, made["down"][0], got["D0"][0])
        elif kind == "gin":
            made["input_grad"] = chain.run(both_cores, place, sum((list(sent[f"gc{s}"]) for s in range(seqs)), []), sum((list(got[f"gc{s}"]) for s in range(seqs)), []))
        elif kind == "bout":
            made["block_output"] = chain.run(both_cores, place, sent["oc"], got["oc"])
        elif kind == "u":
            take(f"u{at}")
        elif kind == "finish":
            name = f"u{at}"
            complete(name)
            u = units[name]
            if at == 0:
                out = chain.run(functools.partial(finish, finish_up_kernel, "finish_up", u.order[0], (d, ff)), place, u.keep, u.got)
            elif at == 1:
                out = chain.run(functools.partial(finish, finish_down_kernel, "finish_down", u.order[0], (ff, d)), place, u.keep, u.got)
            else:
                out = chain.run(functools.partial(finish_rows, u.order[0]), place, u.keep, u.got)
            made[name] = out

    def start(name):
        if name[0] == "u":
            return begin(name)
        if name[0] == "G":
            sent[name] = [made["gn2"][int(name[1:])]]
        elif name[0] == "D":
            sent[name] = made["down"]
        if name[0] in "GD":
            move = other_chip
        elif name[0] == "s" and name != "sc":
            move = functools.partial(lax.ppermute, axis_name="dp", perm=swap(groups, 1 << int(name[1:])))
        else:
            move = other_core
        sent[name] = chain.after(sent[name])
        with jax.named_scope(f"send_{name}"):
            got[name] = [move(value) for value in sent[name]]

    for name in SCHEDULE:
        if name[0] == "+":
            start(name[1:])
        elif name[0] == "-":
            chain.need(units[name[1:]].got if name[1] == "u" else got[name[1:]])
        else:
            step(name)
    for at in range(3, len(bits)):
        start(f"s{at}")
        step(f"sa{at + 1}")
    totals, input_grad, block_output = made["small"], made["input_grad"], made["block_output"]
    up_grad, down_grad, attn = made["u0"], made["u1"], [*made["u2"], *made["u3"]]
    return (
        block_output,
        input_grad,
        totals[0],
        totals[1],
        attn[0].T,
        totals[6, :shard],
        attn[1].T,
        attn[2].T,
        totals[6, shard : 2 * shard],
        attn[3],
        totals[2],
        totals[3],
        totals[4],
        up_grad,
        totals[7:].reshape(-1),
        down_grad,
        totals[5],
    )


def solution(mesh):
    rows, cols, col, copied = P("dp", None), P(None, "tp"), P("tp"), P()
    return jax.shard_map(
        functools.partial(on_device, mesh.shape["dp"], mesh.shape["tp"]),
        mesh=mesh,
        in_specs=(rows, rows, copied, copied, cols, col, cols, cols, col, P("tp", None), copied, copied, copied, cols, col, P("tp", None), copied, rows),
        out_specs=(rows, rows, copied, copied, cols, col, cols, cols, col, P("tp", None), copied, copied, copied, cols, col, P("tp", None), copied),
        check_vma=False,
    )
```

```python
import functools

import jax
import jax.numpy as jnp
from jax import lax
from jax.experimental import pallas as pl
from jax.experimental.pallas import tpu as pltpu
from jax.sharding import PartitionSpec as P

HEAD = 64
SEQ_LEN = 256
EPS = 1e-06
SCALE = 0.125
NEG = -1000000000.0
ROOT_HALF = 0.7071067811865476
INV_ROOT_TAU = 0.3989422804014327
F32 = jnp.float32
BF16 = jnp.bfloat16
VMEM_LIMIT = 14 * 1024 * 1024


def dot_nn(a, b):
    return lax.dot_general(a, b, (((1,), (0,)), ((), ())), preferred_element_type=F32)


def dot_nt(a, b):
    return lax.dot_general(a, b, (((1,), (1,)), ((), ())), preferred_element_type=F32)


def dot_tn(a, b):
    return lax.dot_general(a, b, (((0,), (0,)), ((), ())), preferred_element_type=F32)


def standardize(values):
    centred = values - jnp.mean(values, axis=-1, keepdims=True)
    spread = jnp.mean(centred * centred, axis=-1, keepdims=True)
    scaler = lax.rsqrt(spread + EPS)
    return centred * scaler, scaler


def norm_back(grad_normed, gain, normed, scaler):
    scaled = grad_normed * gain
    centred = scaled - jnp.mean(scaled, axis=-1, keepdims=True)
    return scaler * (centred - normed * jnp.mean(scaled * normed, axis=-1, keepdims=True))


def gelu_parts(hidden):
    cumul = 0.5 * (1.0 + lax.erf(hidden * ROOT_HALF))
    return hidden * cumul, cumul + hidden * (jnp.exp(-0.5 * hidden * hidden) * INV_ROOT_TAU)


def segment_at(pieces_ref, row, amount, shape, axis):
    place = lax.broadcasted_iota(jnp.int32, shape, axis)
    end = jnp.int32(0)
    segment = jnp.zeros(shape, jnp.int32)
    for k in range(amount):
        end = end + pieces_ref[row, k]
        segment = segment + (place >= end).astype(jnp.int32)
    return segment


def mask_bias(pieces_ref, row, amount):
    shape = (SEQ_LEN, SEQ_LEN)
    down = segment_at(pieces_ref, row, amount, shape, 0)
    across = segment_at(pieces_ref, row, amount, shape, 1)
    same = (down == across) & (across < amount - 1)
    diagonal = lax.broadcasted_iota(jnp.int32, shape, 0) == lax.broadcasted_iota(jnp.int32, shape, 1)
    return jnp.where(same | diagonal, 0.0, NEG).astype(F32)


def keep_rows(pieces_ref, row, amount):
    segment = segment_at(pieces_ref, row, amount, (SEQ_LEN, 1), 0)
    return (segment < amount - 1).astype(F32)


def head_lanes(shape):
    return lax.broadcasted_iota(jnp.int32, shape, 1) < HEAD


def both_sides(values, low_lanes):
    zero = jnp.zeros_like(values)
    return jnp.concatenate([jnp.where(low_lanes, values, zero), jnp.where(low_lanes, zero, values)], axis=0)


def attend(qkv_ref, rows, bias, width):
    low_lanes = head_lanes((SEQ_LEN, 2 * HEAD))
    lane = lax.broadcasted_iota(jnp.int32, (SEQ_LEN, 2 * HEAD), 1)
    logs = jnp.zeros((SEQ_LEN, 2 * HEAD), F32)
    pairs = range(width // (2 * HEAD))
    where = [[slice(k * width + p * 2 * HEAD, k * width + (p + 1) * 2 * HEAD) for k in range(3)] for p in pairs]
    scores = [dot_nt(both_sides(qkv_ref[rows, where[p][0]], low_lanes), qkv_ref[rows, where[p][1]]) for p in pairs]
    mixed = []
    for p in pairs:
        probs = []
        for side in range(2):
            mine = scores[p][side * SEQ_LEN : (side + 1) * SEQ_LEN] + bias
            largest = jnp.max(mine, axis=-1, keepdims=True)
            weights = jnp.exp(mine - largest)
            totals = jnp.sum(weights, axis=-1, keepdims=True)
            probs.append((weights * (1.0 / totals)).astype(BF16))
            logs = jnp.where(lane == 2 * p + side, largest + jnp.log(totals), logs)
        out = dot_nn(jnp.concatenate(probs, axis=0), qkv_ref[rows, where[p][2]])
        mixed.append(jnp.where(low_lanes, out[:SEQ_LEN], out[SEQ_LEN:]).astype(BF16))
    return jnp.concatenate(mixed, axis=1), logs


def held(*_):
    return pl.BlockSpec(memory_space=pltpu.VMEM)


def seq_rows(seq):
    return pl.ds(pl.multiple_of(seq * SEQ_LEN, SEQ_LEN), SEQ_LEN)


def anywhere(*_):
    return pl.BlockSpec(memory_space=pltpu.HBM)


def call(kernel, name, scalars, operands, outs, grid=(1,), scratch=(), loose=0, limit=VMEM_LIMIT, us=1.0):
    return pl.pallas_call(
        kernel,
        grid_spec=pltpu.PrefetchScalarGridSpec(
            num_scalar_prefetch=len(scalars), grid=grid, in_specs=[anywhere()] * loose + [held()] * (len(operands) - loose), out_specs=[held()] * len(outs), scratch_shapes=list(scratch)),
        out_shape=[jax.ShapeDtypeStruct(shape, dtype) for shape, dtype in outs],
        compiler_params=pltpu.CompilerParams(vmem_limit_bytes=limit),
        cost_estimate=pl.CostEstimate(flops=int(us * 5e8), bytes_accessed=int(us * 1e6), transcendentals=0),
        name=name,
    )(*scalars, *operands)


def copy_all(copies, sems):
    started = [pltpu.make_async_copy(source, target, sems.at[at]) for at, (source, target) in enumerate(copies)]
    for copy in started:
        copy.start()
    return started


def column_sum(values):
    return jnp.sum(values.reshape(values.shape[0] // 8, 8, values.shape[1]), axis=0)


VECTORS = 6
BITS = 2
TAIL = 16


def vectors_kernel(shard, small_ref, vectors_ref, row_ref):
    d = vectors_ref.shape[1]

    def vector(at, size):
        return small_ref[pl.ds(at, size)].reshape(1, size)

    vectors_ref[...] = jnp.zeros_like(vectors_ref)
    for k in range(VECTORS):
        vectors_ref[k : k + 1, :] = vector(k * d, d)
    ff = row_ref.shape[1] - 4 * shard
    row_ref[:, 4 * shard :] = vector(VECTORS * d, ff)
    zero = jnp.zeros((1, shard), F32)
    at = VECTORS * d + ff
    row_ref[:, : 4 * shard] = jnp.concatenate([vector(at, shard), zero, vector(at + shard, shard), zero], axis=1)


def gather_vectors(small, shard, d, ff):
    return call(functools.partial(vectors_kernel, shard), "vectors", (), (small,), [((8, d), F32), ((1, 4 * shard + ff), F32)])


def join_kernel(place_ref, first_ref, second_ref, v_ref, row_ref, out_ref):
    shard, d = first_ref.shape
    out_ref[pl.ds(pl.multiple_of(place_ref[BITS] * shard, shard), shard), :] = first_ref[...]
    out_ref[pl.ds(pl.multiple_of((1 - place_ref[BITS]) * shard, shard), shard), :] = second_ref[...]
    out_ref[2 * shard : 3 * shard, :] = v_ref[...]
    rest = row_ref[:, : 4 * shard]
    rows = []
    for _ in range(3):
        part = rest.astype(BF16).astype(F32)
        rows.append(part)
        rest = rest - part
    rows.append(jnp.zeros((TAIL - 3, 4 * shard), F32))
    out_ref[3 * shard :, : 4 * shard] = jnp.concatenate(rows, axis=0).astype(BF16)


def join_weights(place, first, second, v, row):
    shard, d = first.shape
    return call(join_kernel, "join", (place,), (first, second, v, row), [((3 * shard + TAIL, d), BF16)])[0]


def spread_bias(a, b, shard):
    return a + jnp.concatenate([jnp.zeros((1, shard), F32), b[:, : 3 * shard]], axis=1)


def project(lowered, w_ref, bias, qkv_ref, at, width):
    for k in range(3):
        proj = dot_nt(lowered, w_ref[k * width : (k + 1) * width, :])
        if k == 0:
            proj = (proj + bias[:, :width]).astype(BF16) * jnp.asarray(SCALE, BF16)
        elif k == 2:
            proj = proj + bias[:, width:]
        qkv_ref[at, k * width : (k + 1) * width] = proj.astype(BF16)


def project_kernel(shard, place_ref, x_ref, vectors_ref, a_ref, b_ref, *refs):
    w_refs, (w_ref, normed_ref, qkv_ref) = refs[:6], refs[6:]
    step = pl.program_id(0)
    width = 2 * shard

    @pl.when(step == 0)
    def _():
        for k, ref in enumerate(w_refs):
            to = (k % 3) * width + (k // 3) * shard
            w_ref[to : to + shard, :] = ref[...]

    normed, _ = standardize(x_ref[seq_rows(place_ref[0] + step), :].astype(F32))
    lowered = (normed * vectors_ref[0:1, :] + vectors_ref[1:2, :]).astype(BF16)
    at = seq_rows(step)
    normed_ref[at, :] = lowered
    bias = spread_bias(a_ref[:, : 4 * shard], b_ref[:, : 4 * shard], shard)
    project(lowered, w_ref, bias, qkv_ref, at, width)


def project_own(rows, place, x, vectors, a, b, weights):
    shard, d = weights[0].shape
    outs = [((6 * shard, d), BF16), ((rows, d), BF16), ((rows, 6 * shard), BF16)]
    return call(functools.partial(project_kernel, shard), "project_own", (place,), (x, vectors, a, b, *weights), outs, (rows // SEQ_LEN,), us=3.5)


def attend_kernel(amount, width, place_ref, pieces_ref, qkv_ref, wa_ref, wb_ref, mixed_ref, logs_ref, part_ref, wo_ref):
    step = pl.program_id(0)

    @pl.when(step == 0)
    def _():
        wo_ref[: width // 2, :] = wa_ref[...]
        wo_ref[width // 2 :, :] = wb_ref[...]

    at = seq_rows(step)
    mixed, logs = attend(qkv_ref, at, mask_bias(pieces_ref, place_ref[0] + step, amount), width)
    logs_ref[pl.ds(pl.multiple_of(step * 8, 8), 8), :] = logs.T[:8, :]
    mixed_ref[at, :] = mixed
    part_ref[at, :] = dot_nn(mixed, wo_ref[...])


def attend_own(place, pieces, qkv, wa, wb):
    seqs, amount = pieces.shape[0] // 2, pieces.shape[1]
    width, d = 2 * wa.shape[0], wa.shape[1]
    rows = seqs * SEQ_LEN
    outs = [((rows, width), BF16), ((seqs * 8, SEQ_LEN), F32), ((rows, d), F32), ((width, d), BF16)]
    return call(functools.partial(attend_kernel, amount, width), "attend_own", (place, pieces), (qkv, wa, wb), outs, (seqs,), us=4.9)


def other_kernel(amount, shard, place_ref, pieces_ref, a_ref, b_ref, normed_in_ref, w_ref, qkv_ref, logs_ref, mixed_ref):
    step = pl.program_id(0)
    width = 2 * shard

    @pl.when(step == 0)
    def _():
        for side, ref in enumerate((a_ref, b_ref)):
            for k in range(3):
                to = k * width + side * shard
                w_ref[to : to + shard, :] = ref[k * shard : (k + 1) * shard, :]

    at = seq_rows(step)
    a, b = (jnp.sum(ref[3 * shard : 3 * shard + 3, : 4 * shard].astype(F32), axis=0, keepdims=True) for ref in (a_ref, b_ref))
    project(normed_in_ref[at, :], w_ref, spread_bias(a, b, shard), qkv_ref, at, width)
    mixed, logs = attend(qkv_ref, at, mask_bias(pieces_ref, place_ref[0] + step, amount), width)
    logs_ref[pl.ds(pl.multiple_of(step * 8, 8), 8), :] = logs.T[:8, :]
    mixed_ref[at, :] = mixed


def attend_other(place, pieces, a, b, normed):
    seqs, amount = pieces.shape[0] // 2, pieces.shape[1]
    shard, d = (a.shape[0] - TAIL) // 3, a.shape[1]
    rows = seqs * SEQ_LEN
    outs = [((6 * shard, d), BF16), ((rows, 6 * shard), BF16), ((seqs * 8, SEQ_LEN), F32), ((rows, 2 * shard), BF16)]
    return call(functools.partial(other_kernel, amount, shard), "attend_other", (place, pieces), (a, b, normed), outs, (seqs,), us=6.0)


def middle_kernel(amount, place_ref, pieces_ref, wa_ref, wb_ref, x_ref, mixed_ref, part_in_ref, vectors_ref, w_ref, middle_ref, normed_ref, sum_ref):
    step = pl.program_id(0)
    shard = wa_ref.shape[0]
    first = place_ref[0] * SEQ_LEN

    @pl.when(step == 0)
    def _():
        w_ref[:shard, :] = wa_ref[...]
        w_ref[shard:, :] = wb_ref[...]

    at = seq_rows(step)
    sum_ref[...] = dot_nn(mixed_ref[at, :], w_ref[...])
    keep_all = keep_rows(pieces_ref, place_ref[0] + step, amount)
    block = 64
    for r in range(0, SEQ_LEN, block):
        here = pl.ds(pl.multiple_of(step * SEQ_LEN + r, block), block)
        added = part_in_ref[here, :] + sum_ref[r : r + block, :] + vectors_ref[2:3, :]
        middle = x_ref[pl.ds(pl.multiple_of(first + step * SEQ_LEN + r, block), block), :].astype(F32) + keep_all[r : r + block] * added
        middle_ref[here, :] = middle
        normed, _ = standardize(middle)
        normed_ref[here, :] = (normed * vectors_ref[3:4, :] + vectors_ref[4:5, :]).astype(BF16)


def middle_rows(place, pieces, wa, wb, x, mixed, part, vectors):
    (rows, width), d = mixed.shape, x.shape[1]
    outs = [((width, d), BF16), ((rows, d), F32), ((rows, d), BF16)]
    return call(functools.partial(middle_kernel, pieces.shape[1]), "middle", (place, pieces), (wa, wb, x, mixed, part, vectors), outs, (rows // SEQ_LEN,),
                [pltpu.VMEM((SEQ_LEN, d), F32)], us=3.0)


def mlp_kernel(amount, first, seqs, place_ref, pieces_ref, n2_ref, cot_ref, ba_ref, bb_ref, upa_ref, upb_ref, dna_ref, dnb_ref,
               active_ref, gh_ref, gb_ref, sums_ref, n2_out_ref, *gn2_refs):
    ff = upa_ref.shape[1]
    skip = ba_ref.shape[1] - ff
    block = 256 if ff % 256 == 0 else ff
    total = [None] * (2 * ff // block)
    for s in range(seqs):
        rows = slice(s * SEQ_LEN, (s + 1) * SEQ_LEN)
        here = slice((first + s) * SEQ_LEN, (first + s + 1) * SEQ_LEN)
        keep = keep_rows(pieces_ref, place_ref[0] + first + s, amount)
        branch = (keep * cot_ref[seq_rows(place_ref[0] + first + s), :].astype(F32)).astype(BF16)
        gb_ref[rows, :] = branch
        n2 = n2_ref[here, :]
        n2_out_ref[rows, :] = n2
        for side, (up_ref, dn_ref, bias_ref) in enumerate(((upa_ref, dna_ref, ba_ref), (upb_ref, dnb_ref, bb_ref))):
            for j in range(0, ff, block):
                at = slice(side * ff + j, side * ff + j + block)
                hidden = dot_nn(n2, up_ref[:, j : j + block]) + bias_ref[:, skip + j : skip + j + block]
                active, slope = gelu_parts(hidden)
                active_ref[rows, at] = active.astype(BF16)
                grad_active = dot_nt(branch, dn_ref[j : j + block, :])
                grad_hidden = (grad_active * slope).astype(BF16)
                gh_ref[rows, at] = grad_hidden
                part = jnp.sum(grad_hidden.astype(F32), axis=0, keepdims=True)
                k = at.start // block
                total[k] = part if total[k] is None else total[k] + part
        gn2_refs[s][...] = (dot_nt(gh_ref[rows, :ff], upa_ref[...]) + dot_nt(gh_ref[rows, ff:], upb_ref[...])).astype(BF16)
    for k, part in enumerate(total):
        sums_ref[:, k * block : (k + 1) * block] = part


def mlp_rows(first, seqs, place, pieces, n2, cot, bias, bias_b, upa, upb, dna, dnb):
    d, ff = upa.shape
    rows = seqs * SEQ_LEN
    outs = [((rows, 2 * ff), BF16), ((rows, 2 * ff), BF16), ((rows, d), BF16), ((1, 2 * ff), F32), ((rows, d), BF16)] + [((SEQ_LEN, d), BF16)] * seqs
    return call(functools.partial(mlp_kernel, pieces.shape[1], first, seqs), "mlp", (place, pieces), (n2, cot, bias, bias_b, upa, upb, dna, dnb), outs, us=2.7 * seqs)


def down_kernel(count, dna_ref, dnb_ref, *refs):
    ff = dna_ref.shape[0]
    out_ref = refs[-1]
    at = 0
    for active_ref in refs[:count]:
        for r in range(0, active_ref.shape[0], SEQ_LEN):
            rows = slice(r, r + SEQ_LEN)
            out_ref[at : at + SEQ_LEN, :] = (dot_nn(active_ref[rows, :ff], dna_ref[...]) + dot_nn(active_ref[rows, ff:], dnb_ref[...])).astype(BF16)
            at += SEQ_LEN


def down_rows(dna, dnb, actives):
    rows, d = sum(a.shape[0] for a in actives), dna.shape[1]
    return call(functools.partial(down_kernel, len(actives)), "down", (), (dna, dnb, *actives), [((rows, d), BF16)], us=2.0)


def sent_kernel(count, side, *refs):
    out_ref = refs[-1]
    size = out_ref.shape[0]
    block = 256 if size % 256 == 0 else size
    for j in range(0, size, block):
        at = slice(side * size + j, side * size + j + block)
        total = sum(dot_tn(refs[k][:, at], refs[count + k][...]) for k in range(count))
        out_ref[j : j + block, :] = total.astype(BF16)


def grad_sent(side, lefts, rights):
    size, d = lefts[0].shape[1] // 2, rights[0].shape[1]
    return call(functools.partial(sent_kernel, len(lefts), side), "grad_sent", (), (*lefts, *rights), [((size, d), BF16)], us=1.1)


def kept_kernel(count, bit, place_ref, *refs):
    add_ref, send_ref, keep_ref = refs[-3:]
    half = keep_ref.shape[0]
    for which, out_ref in enumerate((send_ref, keep_ref)):
        mine = place_ref[BITS + bit] if which else 1 - place_ref[BITS + bit]
        at = pl.ds(pl.multiple_of(mine * half, half), half)
        total = sum(dot_tn(refs[k][:, at], refs[count + k][...]) for k in range(count))
        out_ref[...] = (total + add_ref[at, :].astype(F32)).astype(BF16)


def grad_kept(bit, place, lefts, rights, add):
    half, d = lefts[0].shape[1] // 4, rights[0].shape[1]
    return call(functools.partial(kept_kernel, len(lefts), bit), "grad_kept", (place,), (*lefts, *rights, add), [((half, d), BF16)] * 2, us=1.7)


def attn_dots(refs, attns, n1_ref, seqs, shard, side, kind):
    width = 2 * shard
    at = slice(kind * width + side * shard, kind * width + (side + 1) * shard)
    rights = [attns[s][...] if kind == 3 else n1_ref[s * SEQ_LEN : (s + 1) * SEQ_LEN, :] for s in range(seqs)]
    return sum(dot_tn(refs[s][:, at], rights[s]) for s in range(seqs))


def attn_sent_kernel(seqs, kinds, *refs):
    out_ref = refs[-1]
    shard = out_ref.shape[0] // len(kinds)
    for k, kind in enumerate(kinds):
        out_ref[k * shard : (k + 1) * shard, :] = attn_dots(refs[:seqs], refs[seqs : 2 * seqs], refs[2 * seqs], seqs, shard, 1, kind).astype(BF16)


def attn_sent(kinds, lefts, attns, n1):
    shard, d = lefts[0].shape[1] // 8, n1.shape[1]
    return call(functools.partial(attn_sent_kernel, len(lefts), kinds), "attn_sent", (), (*lefts, *attns, n1), [((len(kinds) * shard, d), BF16)], us=0.9)


def attn_kept_kernel(seqs, kinds, bit, place_ref, *refs):
    add_ref, send_ref, keep_ref, both_ref = refs[-4:]
    shard = keep_ref.shape[0]
    for which, kind in enumerate(kinds):
        total = attn_dots(refs[:seqs], refs[seqs : 2 * seqs], refs[2 * seqs], seqs, shard, 0, kind)
        at = slice(which * shard, (which + 1) * shard)
        both_ref[at, :] = (total + add_ref[at, :].astype(F32)).astype(BF16)
    mine = place_ref[BITS + bit]
    for out_ref, chosen in ((keep_ref, mine), (send_ref, 1 - mine)):
        out_ref[...] = both_ref[pl.ds(pl.multiple_of(chosen * shard, shard), shard), :]


def attn_kept(kinds, bit, place, lefts, attns, n1, add):
    shard, d = lefts[0].shape[1] // 8, n1.shape[1]
    return call(functools.partial(attn_kept_kernel, len(lefts), kinds, bit), "attn_kept", (place,), (*lefts, *attns, n1, add), [((shard, d), BF16)] * 2,
                scratch=[pltpu.VMEM((2 * shard, d), BF16)], us=1.2)


def attend_back(qkv_ref, rows, gm_ref, logs_ref, first, bias, width, grads_ref):
    low_lanes = head_lanes((SEQ_LEN, 2 * HEAD))
    pairs = range(width // (2 * HEAD))
    where = [[slice(k * width + p * 2 * HEAD, k * width + (p + 1) * 2 * HEAD) for k in range(3)] for p in pairs]
    scores = [dot_nt(both_sides(qkv_ref[rows, where[p][1]], low_lanes), qkv_ref[rows, where[p][0]]) for p in pairs]
    grad_probs = [dot_nt(both_sides(qkv_ref[rows, where[p][2]], low_lanes), gm_ref[:, where[p][0]]) for p in pairs]
    for p in pairs:
        probs, grad_scores = [], []
        for side in range(2):
            mine = slice(side * SEQ_LEN, (side + 1) * SEQ_LEN)
            head = first + 2 * p + side
            prob = jnp.exp(scores[p][mine] + bias - logs_ref[head : head + 1, :])
            inner = jnp.sum(grad_probs[p][mine] * prob, axis=0, keepdims=True)
            grad_scores.append((prob * (grad_probs[p][mine] - inner)).astype(BF16))
            probs.append(prob.astype(BF16))
        grad_key = dot_nn(jnp.concatenate(grad_scores, axis=0), qkv_ref[rows, where[p][0]])
        grad_value = dot_nn(jnp.concatenate(probs, axis=0), gm_ref[:, where[p][0]])
        grad_query = dot_tn(jnp.concatenate(grad_scores, axis=1), qkv_ref[rows, where[p][1]])
        grads_ref[:, where[p][0]] = (jnp.where(low_lanes, grad_query[:SEQ_LEN], grad_query[SEQ_LEN:]) * SCALE).astype(BF16)
        grads_ref[:, where[p][1]] = jnp.where(low_lanes, grad_key[:SEQ_LEN], grad_key[SEQ_LEN:]).astype(BF16)
        grads_ref[:, where[p][2]] = jnp.where(low_lanes, grad_value[:SEQ_LEN], grad_value[SEQ_LEN:]).astype(BF16)


def own_back_kernel(amount, seq, place_ref, pieces_ref, cot_ref, middle_ref, own_ref, got_ref, vectors_ref, qkv_ref, logs_ref, mixed_ref, w_ref, wo_ref,
                    grad_ref, all_ref, attn_ref, part_ref, sums_ref, gm_ref):
    row = place_ref[0] + seq
    width = mixed_ref.shape[1]
    d = cot_ref.shape[1]
    keep_all = keep_rows(pieces_ref, row, amount)
    sums = [jnp.zeros((8, d), F32)] * 4
    block = 32
    for r in range(0, SEQ_LEN, block):
        at = slice(r, r + block)
        keep = keep_all[at]
        cot = cot_ref[pl.ds(pl.multiple_of(row * SEQ_LEN + r, block), block), :].astype(F32)
        gn2 = own_ref[at, :].astype(F32) + got_ref[at, :].astype(F32)
        normed, scaler = standardize(middle_ref[seq * SEQ_LEN + r : seq * SEQ_LEN + r + block, :])
        grad_middle = cot + norm_back(gn2, vectors_ref[3:4, :], normed, scaler)
        attn = (keep * grad_middle).astype(BF16)
        attn_ref[at, :] = attn
        grad_ref[at, :] = grad_middle
        terms = (attn.astype(F32), gn2 * normed, gn2, (keep * cot).astype(BF16).astype(F32))
        sums = [s + column_sum(t) for s, t in zip(sums, terms)]
    sums_ref[...] = jnp.zeros_like(sums_ref)
    for k in range(4):
        sums_ref[2 + k : 3 + k, :] = jnp.sum(sums[k], axis=0, keepdims=True)
    gm_ref[...] = dot_nt(attn_ref[...], wo_ref[...]).astype(BF16)
    rows = slice(seq * SEQ_LEN, (seq + 1) * SEQ_LEN)
    attend_back(qkv_ref, rows, gm_ref, logs_ref, 8 * seq, mask_bias(pieces_ref, row, amount), width, all_ref)
    part_ref[...] = dot_nn(all_ref[:, : 3 * width], w_ref[...])
    all_ref[:, 3 * width :] = mixed_ref[rows, :]
    sums_ref[6:7, :width] = jnp.sum(all_ref[:, :width].astype(F32), axis=0, keepdims=True)
    sums_ref[7:8, :width] = jnp.sum(all_ref[:, 2 * width : 3 * width].astype(F32), axis=0, keepdims=True)


def own_back(seq, place, pieces, cot, middle, own, got, vectors, qkv, logs, mixed, w, wo):
    d, width = cot.shape[1], mixed.shape[1]
    outs = [((SEQ_LEN, d), F32), ((SEQ_LEN, 4 * width), BF16), ((SEQ_LEN, d), BF16), ((SEQ_LEN, d), F32), ((8, d), F32)]
    return call(functools.partial(own_back_kernel, pieces.shape[1], seq), "own_back", (place, pieces),
                (cot, middle, own, got, vectors, qkv, logs, mixed, w, wo), outs, scratch=[pltpu.VMEM((SEQ_LEN, width), BF16)], us=5.2)


def other_back_kernel(amount, seq, place_ref, pieces_ref, x_ref, grad_in_ref, attn_ref, part_ref, vectors_ref, qkv_ref, logs_ref, w_ref, wo_ref,
                      grad_ref, sums_ref, gm_ref, all_ref, sum_ref):
    row = place_ref[0] + seq
    width = gm_ref.shape[1]
    d = x_ref.shape[1]
    bias = mask_bias(pieces_ref, row, amount)
    gm_ref[...] = dot_nt(attn_ref[...], wo_ref[...]).astype(BF16)
    rows = slice(seq * SEQ_LEN, (seq + 1) * SEQ_LEN)
    attend_back(qkv_ref, rows, gm_ref, logs_ref, 8 * seq, bias, width, all_ref)
    sum_ref[...] = dot_nn(all_ref[...], w_ref[...])
    sums = [jnp.zeros((8, d), F32)] * 2
    block = 32
    for r in range(0, SEQ_LEN, block):
        at = slice(r, r + block)
        gn1 = part_ref[at, :] + sum_ref[at, :]
        normed, scaler = standardize(x_ref[pl.ds(pl.multiple_of(row * SEQ_LEN + r, block), block), :].astype(F32))
        grad_ref[at, :] = grad_in_ref[at, :] + norm_back(gn1, vectors_ref[0:1, :], normed, scaler)
        sums = [s + column_sum(t) for s, t in zip(sums, (gn1 * normed, gn1))]
    sums_ref[...] = jnp.zeros_like(sums_ref)
    for k in range(2):
        sums_ref[k : k + 1, :] = jnp.sum(sums[k], axis=0, keepdims=True)


def other_back(seq, place, pieces, x, grad_in, attn, part, vectors, qkv, logs, w, wo):
    d, width = wo.shape[1], wo.shape[0]
    outs = [((SEQ_LEN, d), F32), ((8, d), F32)]
    return call(functools.partial(other_back_kernel, pieces.shape[1], seq), "other_back", (place, pieces),
                (x, grad_in, attn, part, vectors, qkv, logs, w, wo), outs,
                scratch=[pltpu.VMEM((SEQ_LEN, width), BF16), pltpu.VMEM((SEQ_LEN, 3 * width), BF16), pltpu.VMEM((SEQ_LEN, d), F32)], us=4.5)


def output_kernel(amount, place_ref, pieces_ref, middle_ref, vectors_ref, own_ref, got_ref, out_ref):
    block = 64
    for seq in range(out_ref.shape[0] // SEQ_LEN):
        keep_all = keep_rows(pieces_ref, place_ref[0] + seq, amount)
        for r in range(0, SEQ_LEN, block):
            at = slice(seq * SEQ_LEN + r, seq * SEQ_LEN + r + block)
            total = own_ref[at, :].astype(F32) + got_ref[at, :].astype(F32) + vectors_ref[5:6, :]
            out_ref[at, :] = (middle_ref[at, :] + keep_all[r : r + block] * total).astype(BF16)


def output_rows(place, pieces, middle, vectors, own, got):
    return call(functools.partial(output_kernel, pieces.shape[1]), "block_output", (place, pieces),
                (middle, vectors, own, got), [(middle.shape, BF16)], us=1.4)


def both_kernel(count, place_ref, *refs):
    out_ref, sems = refs[-2:]
    size = refs[0].shape[0]
    copies = []
    for k in range(2 * count):
        at = (place_ref[1] if k < count else 1 - place_ref[1]) * count + k % count
        copies.append(pltpu.make_async_copy(refs[k], out_ref.at[pl.ds(pl.multiple_of(at * size, size), size)], sems.at[k]))
        copies[-1].start()
    for copy in copies:
        copy.wait()


def both_cores(place, mine, theirs):
    count = len(mine)
    rows, d = mine[0].shape
    return pl.pallas_call(
        functools.partial(both_kernel, count),
        grid_spec=pltpu.PrefetchScalarGridSpec(
            num_scalar_prefetch=1, grid=(1,), in_specs=[held()] * (2 * count), out_specs=pl.BlockSpec(memory_space=pl.ANY),
            scratch_shapes=[pltpu.SemaphoreType.DMA((2 * count,))]),
        out_shape=jax.ShapeDtypeStruct((2 * count * rows, d), mine[0].dtype),
        compiler_params=pltpu.CompilerParams(vmem_limit_bytes=VMEM_LIMIT),
        cost_estimate=pl.CostEstimate(flops=1, bytes_accessed=1, transcendentals=0),
        name="both_cores",
    )(place, *mine, *theirs)


def swap(size, bit):
    return [(i, i ^ bit) for i in range(size)]


def tie(values, *after):
    return lax.optimization_barrier((values, after))[0]


def merge_kernel(at, place_ref, keep_ref, got_ref, send_ref, out_ref):
    size = out_ref.shape[0]
    for which, ref in enumerate((send_ref, out_ref)):
        bit = place_ref[BITS + at] if which else 1 - place_ref[BITS + at]
        rows = pl.ds(pl.multiple_of(bit * size, size), size)
        ref[...] = (keep_ref[rows, :].astype(F32) + got_ref[rows, :].astype(F32)).astype(BF16)


def merge(bit, place, keep, got):
    rows, d = keep.shape
    half = rows // 2
    if half % 16:
        total = (keep.astype(F32) + got.astype(F32)).astype(BF16)
        low = place[BITS + bit] == 0
        return jnp.where(low, total[half:], total[:half]), jnp.where(low, total[:half], total[half:])
    return call(functools.partial(merge_kernel, bit), "merge", (place,), (keep, got), [((half, d), BF16)] * 2, us=0.6)


def add_kernel(keep_ref, got_ref, out_ref):
    out_ref[...] = (keep_ref[...].astype(F32) + got_ref[...].astype(F32)).astype(out_ref.dtype)


def add(keep, got):
    return call(add_kernel, "add", (), (keep, got), [(keep.shape, keep.dtype)])[0]


def grow_kernel(at, place_ref, keep_ref, got_ref, out_ref):
    size = keep_ref.shape[0]
    out_ref[pl.ds(pl.multiple_of(place_ref[BITS + at] * size, size), size), :] = keep_ref[...]
    out_ref[pl.ds(pl.multiple_of((1 - place_ref[BITS + at]) * size, size), size), :] = got_ref[...]


def grow(bit, place, keep, got):
    rows, d = keep.shape
    if rows % 16:
        return jnp.where(place[BITS + bit] == 0, jnp.concatenate([keep, got]), jnp.concatenate([got, keep]))
    return call(functools.partial(grow_kernel, bit), "grow", (place,), (keep, got), [((2 * rows, d), BF16)])[0]


def finish_up_kernel(at, place_ref, keep_ref, got_ref, out_ref):
    size = keep_ref.shape[0]
    out_ref[:, pl.ds(pl.multiple_of(place_ref[BITS + at] * size, 128), size)] = keep_ref[...].astype(F32).T
    out_ref[:, pl.ds(pl.multiple_of((1 - place_ref[BITS + at]) * size, 128), size)] = got_ref[...].astype(F32).T


def finish_down_kernel(at, place_ref, keep_ref, got_ref, out_ref):
    size = keep_ref.shape[0]
    out_ref[pl.ds(pl.multiple_of(place_ref[BITS + at] * size, size), size), :] = keep_ref[...].astype(F32)
    out_ref[pl.ds(pl.multiple_of((1 - place_ref[BITS + at]) * size, size), size), :] = got_ref[...].astype(F32)


def finish(kernel, name, bit, shape, place, keep, got):
    return call(functools.partial(kernel, bit), name, (place,), (keep, got), [(shape, F32)])[0]


def rows_kernel(at, place_ref, keep_ref, got_ref, low_ref, high_ref):
    mine = place_ref[BITS + at] == 0
    keep, got = keep_ref[...].astype(F32), got_ref[...].astype(F32)
    low_ref[...] = jnp.where(mine, keep, got)
    high_ref[...] = jnp.where(mine, got, keep)


def finish_rows(bit, place, keep, got):
    return call(functools.partial(rows_kernel, bit), "finish_rows", (place,), (keep, got), [(keep.shape, F32)] * 2, us=1.6)


def put_parts(out_ref, at, sums):
    rows, d = sums.shape
    parts = []
    for _ in range(3):
        part = sums.astype(BF16).astype(F32)
        parts.append(part)
        sums = sums - part
    parts.append(jnp.zeros((out_ref.shape[0] - at - 3 * rows, d), F32))
    out_ref[at:, :] = jnp.concatenate(parts, axis=0).astype(BF16)


def get_parts(ref, at, rows):
    parts = ref[at:, :].astype(F32)
    return sum(parts[k * rows : (k + 1) * rows] for k in range(3))


def add_sums_kernel(rows, first, keep_ref, got_ref, sums_ref, more_ref, send_ref, out_ref, total_ref):
    size = keep_ref.shape[0]
    kept = (keep_ref[...].astype(F32) + got_ref[:size, :].astype(F32)).astype(BF16)
    out_ref[...] = kept
    send_ref[:size, :] = kept
    total = sums_ref[...] + (more_ref[...] if first else get_parts(more_ref, size, rows))
    total_ref[...] = total
    put_parts(send_ref, size, total)


def add_sums(keep, got, sums, more):
    first = more is None
    size, d = keep.shape
    rows = sums.shape[0]
    padded = -(-3 * rows // 16) * 16
    return call(functools.partial(add_sums_kernel, rows, not first), "add_sums", (), (keep, got, sums, got if first else more),
                [((size + padded, d), BF16), (keep.shape, BF16), (sums.shape, F32)], us=0.6)


def grow_sums_kernel(at, rows, size, place_ref, keep_ref, got_ref, sums_ref, send_ref, total_ref):
    send_ref[pl.ds(pl.multiple_of(place_ref[BITS + at] * size, size), size), :] = keep_ref[:size, :]
    send_ref[pl.ds(pl.multiple_of((1 - place_ref[BITS + at]) * size, size), size), :] = got_ref[:size, :]
    total = sums_ref[...] + get_parts(got_ref, size, rows)
    total_ref[...] = total
    put_parts(send_ref, 2 * size, total)


def grow_sums(bit, place, keep, got, sums):
    rows, d = sums.shape
    padded = -(-3 * rows // 16) * 16
    size = got.shape[0] - padded
    keep = keep[:size] if size % 16 else keep
    if size % 16:
        low = place[BITS + bit] == 0
        kept = jnp.where(low, jnp.concatenate([keep, got[:size]]), jnp.concatenate([got[:size], keep]))
        parts = got[size:].astype(F32)
        total = sums + sum(parts[k * rows : (k + 1) * rows] for k in range(3))
        rest, split = total, []
        for _ in range(3):
            split.append(lax.reduce_precision(rest, 8, 7))
            rest = rest - split[-1]
        split.append(jnp.zeros((padded - 3 * rows, d), F32))
        return jnp.concatenate([kept, jnp.concatenate(split).astype(BF16)]), kept, total
    send, total = call(functools.partial(grow_sums_kernel, bit, rows, size), "grow_sums", (place,), (keep, got, sums),
                       [((2 * size + padded, d), BF16), (sums.shape, F32)], us=0.7)
    return send, send, total


def rows_sums_kernel(at, rows, shard, place_ref, keep_ref, got_ref, sums_ref, low_ref, high_ref, *flat_refs):
    size = low_ref.shape[0]
    mine = place_ref[BITS + at] == 0
    keep, got = keep_ref[:size, :].astype(F32), got_ref[:size, :].astype(F32)
    low_ref[...] = jnp.where(mine, keep, got)
    high_ref[...] = jnp.where(mine, got, keep)
    total = sums_ref[...] + get_parts(got_ref, size, rows)
    for k in range(6):
        flat_refs[k][...] = total[k]
    flat_refs[6][...] = total[6, :shard]
    flat_refs[7][...] = total[6, shard : 2 * shard]
    d = total.shape[1]
    for k in range(7, rows):
        flat_refs[8][pl.ds((k - 7) * d, d)] = total[k]


def finish_sums(bit, shard, place, keep, got, sums):
    rows, d = sums.shape
    size = got.shape[0] - -(-3 * rows // 16) * 16
    outs = [((size, d), F32)] * 2 + [((d,), F32)] * 6 + [((shard,), F32)] * 2 + [(((rows - 7) * d,), F32)]
    return call(functools.partial(rows_sums_kernel, bit, rows, shard), "finish_sums", (place,), (keep, got, sums), outs, us=1.8)


class Unit:
    def __init__(self, groups, order, place, send, keep):
        self.groups, self.order, self.place = groups, order, place
        self.send, self.keep, self.step = send, keep, 0
        self.middle = len(order) - 1
        self.last = 2 * self.middle

    def start(self):
        at = min(self.step, self.last - self.step)
        self.got = lax.ppermute(self.send, "dp", swap(self.groups, 1 << self.order[at]))

    def take(self):
        if self.step < self.middle - 1:
            self.send, self.keep = merge(self.order[self.step + 1], self.place, self.keep, self.got)
        elif self.step <= self.middle:
            self.send = self.keep = add(self.keep, self.got)
        else:
            self.send = self.keep = grow(self.order[self.last - self.step], self.place, self.keep, self.got)
        self.step += 1


class SumsUnit(Unit):
    def take(self):
        if self.step < self.middle - 1:
            return super().take()
        if self.step <= self.middle:
            more = self.more if self.step == self.middle - 1 else None
            self.send, self.keep, self.sums = add_sums(self.keep, self.got, self.sums, more)
        else:
            self.send, self.keep, self.sums = grow_sums(self.order[self.last - self.step], self.place, self.keep, self.got, self.sums)
        self.step += 1


class Chain:
    def __init__(self):
        self.last = ()

    def run(self, kernel, *args, need=()):
        args = tie(args, self.last, need)
        out = kernel(*args)
        self.last = out
        return out

    def after(self, values):
        return tie(values, self.last)

    def need(self, values):
        self.last = (self.last, values)


SCHEDULE = (
    "mlp0", "mlp1", "+G2", "gs0", "+G1", "+cb0", "gs1", "+cb1", "down", "gk0", "+u0", "gk1", "+u1", "ob2", "+G0", "xb2", "u0", "+u0",
    "ob1", "u1", "+u1", "ob0", "ao1", "+D0", "ao0", "+ca0", "u1", "u0", "+ca1", "+u1", "+u0", "xb0", "ak0", "+u2", "ak1", "u0", "+u0",
    "+u3", "xb1", "u1", "+u1", "sums", "u2", "+u2", "+sc", "u3", "+u3", "out", "u2", "+oc", "u1", "+u1", "u3", "u0", "+u3", "+u0", "+gc2",
    "+u2", "u3", "+u3", "u2", "+u2", "finish1", "u3", "finish0", "+u3", "u2", "+u2", "+gc0", "+gc1", "bout", "gin", "finish3", "finish2",
)
ORDERS = ((0, 2, 1), (1, 0, 2), (0, 1, 2), (1, 0, 2))


def small_kernel(seqs, shard, *refs):
    own, oth, ups, outs = refs[:seqs], refs[seqs : 2 * seqs], refs[2 * seqs : -2], refs[-2:]
    total = sum(r[...] for r in own) + sum(r[...] for r in oth)
    up = sum(r[...] for r in ups)
    d = total.shape[1]
    ff = up.shape[1] // 2
    for side, out_ref in enumerate(outs):
        out_ref[0:6, :] = total[0:6]
        at = slice(side * shard, (side + 1) * shard)
        out_ref[6:7, :] = jnp.concatenate([total[6:7, at], total[7:8, at], jnp.zeros((1, d - 2 * shard), F32)], axis=1)
        for k in range(ff // d):
            out_ref[7 + k : 8 + k, :] = up[:, side * ff + k * d : side * ff + (k + 1) * d]


def small_sums(shard, own, oth, ups):
    seqs, d = len(own), own[0].shape[1]
    rows = 7 + ups[0].shape[1] // 2 // d
    operands = [*own, *oth, *ups]
    return call(functools.partial(small_kernel, seqs, shard), "small_sums", (), operands, [((rows, d), F32)] * 2)


def on_device(groups, tp, block_input, pieces, gain_one, shift_one, query_weight, query_bias, key_weight, value_weight, value_bias,
              out_weight, out_bias, gain_two, shift_two, up_weight, up_bias, down_weight, down_bias, cotangent):
    d = block_input.shape[1]
    shard = query_weight.shape[1]
    ff = up_weight.shape[1]
    seqs = pieces.shape[0] // 2
    core = lax.axis_index("tp") & 1
    group = lax.axis_index("dp")
    bits = list(range(groups.bit_length() - 1))
    place = jnp.stack([core * seqs, core] + [(group >> bit) & 1 for bit in bits]).astype(jnp.int32)

    def other_core(values):
        return lax.ppermute(values, "tp", swap(tp, 1))

    def other_chip(values):
        return lax.ppermute(values, "tp", swap(tp, 2))

    def next_group(values):
        return lax.ppermute(values, "dp", swap(groups, 1))

    chain = Chain()
    weights = (query_weight.T, key_weight.T, value_weight.T, out_weight)
    core_weights = [other_core(w) for w in weights]
    small = jnp.concatenate([gain_one, shift_one, out_bias, gain_two, shift_two, down_bias, up_bias, query_bias, value_bias])
    first = other_chip(jnp.where(place[BITS] == 0, weights[0], weights[1]))
    last_v, last_o = other_chip(weights[2]), other_chip(weights[3])
    vectors, biases = chain.run(functools.partial(gather_vectors, shard=shard, d=d, ff=ff), small)
    biases_b, biases_x = other_core(biases), other_chip(biases)
    w_own, n1, qkv_own = chain.run(functools.partial(project_own, seqs * SEQ_LEN), place, block_input, vectors, biases, biases_b, (*weights[:3], *core_weights[:3]))
    first, biases_x = chain.after((first, biases_x))
    second = next_group(first)
    mixed, logs_own, part, wo_own = chain.run(attend_own, place, pieces, qkv_own, weights[3], core_weights[3], need=(first, biases_x))
    up_weight, down_weight = chain.after((up_weight, down_weight))
    up_b, down_b = other_core(up_weight), other_core(down_weight)
    joined = chain.run(join_weights, place, first, second, last_v, biases_x)
    w_oth, qkv_oth, logs_oth, mixed_oth = chain.run(attend_other, place, pieces, joined, other_core(joined), n1)
    last_o = chain.after(last_o)
    wo_oth, middle, n2 = chain.run(middle_rows, place, pieces, last_o, other_core(last_o), block_input, mixed_oth, part, vectors)

    sent, got, made = {}, {}, {}
    units = {}

    def unit(name, at, send, keep):
        order = [*ORDERS[at], *bits[len(ORDERS[at]) :]]
        units[name] = (SumsUnit if name == "u2" else Unit)(groups, order, place, send, keep)

    def take(name):
        u = units[name]
        u.keep, u.got = tie((u.keep, u.got), chain.last)
        if name == "u2" and u.step == u.middle - 1:
            u.sums, u.more = tie((made["small"], got["sc"][0]), chain.last)
        u.take()
        chain.last = u.keep

    def begin(name):
        u = units[name]
        u.send = chain.after(u.send)
        with jax.named_scope(f"send_{name}_{u.step}"):
            u.start()

    def complete(name):
        u = units[name]
        while u.step < u.last:
            take(name)
            begin(name)

    def mlp(part):
        first, count = (0, 1) if part == 0 else (1, seqs - 1)
        out = chain.run(functools.partial(mlp_rows, first, count), place, pieces, n2, cotangent, biases, biases_b, up_weight, up_b, down_weight, down_b)
        for key, value in zip(("active", "hidden", "branch", "sums", "n2"), out):
            made.setdefault(key, []).append(value)
        made.setdefault("gn2", []).extend(out[5:])

    def sides(at):
        return (made["hidden"], made["n2"]) if at == 0 else (made["active"], made["branch"])

    def step(name):
        kind, at = name.rstrip("0123456789"), name[len(name.rstrip("0123456789")) :]
        at = int(at) if at else 0
        if kind == "mlp":
            mlp(at)
        elif kind == "down":
            made["down"] = chain.run(down_rows, down_weight, down_b, made["active"])
        elif kind == "gs":
            sent[f"cb{at}"] = chain.run(functools.partial(grad_sent, 1), *sides(at))
        elif kind == "gk":
            unit(f"u{at}", at, *chain.run(functools.partial(grad_kept, ORDERS[at][0]), place, *sides(at), got[f"cb{at}"][0]))
        elif kind == "ob":
            made[f"ob{at}"] = chain.run(functools.partial(own_back, at), place, pieces, cotangent, middle, made["gn2"][at], got[f"G{at}"][0], vectors,
                                        qkv_own, logs_own, mixed, w_own, wo_own)
        elif kind in ("ao", "ak"):
            kinds = (0, 1) if at == 0 else (2, 3)
            owns = [made[f"ob{s}"] for s in range(seqs)]
            operands = ([o[1] for o in owns], [o[2] for o in owns], n1)
            if kind == "ao":
                sent[f"ca{at}"] = chain.run(functools.partial(attn_sent, kinds), *operands)
            else:
                unit(f"u{2 + at}", 2 + at, *chain.run(functools.partial(attn_kept, kinds, ORDERS[2 + at][0]), place, *operands, got[f"ca{at}"][0]))
        elif kind == "xb":
            own = made[f"ob{at}"]
            made[f"xb{at}"] = chain.run(functools.partial(other_back, at), place, pieces, block_input, own[0], own[2], own[3], vectors,
                                        qkv_oth, logs_oth, w_oth, wo_oth)
            sent[f"gc{at}"] = made[f"xb{at}"][:1]
        elif kind == "sums":
            made["small"], more = chain.run(functools.partial(small_sums, shard), [made[f"ob{s}"][4] for s in range(seqs)],
                                            [made[f"xb{s}"][1] for s in range(seqs)], made["sums"])
            sent["sc"] = [more]
        elif kind == "out":
            sent["oc"] = chain.run(output_rows, place, pieces, middle, vectors, made["down"][0], got["D0"][0])
        elif kind == "gin":
            made["input_grad"] = chain.run(both_cores, place, sum((list(sent[f"gc{s}"]) for s in range(seqs)), []), sum((list(got[f"gc{s}"]) for s in range(seqs)), []))
        elif kind == "bout":
            made["block_output"] = chain.run(both_cores, place, sent["oc"], got["oc"])
        elif kind == "u":
            take(f"u{at}")
        elif kind == "finish":
            name = f"u{at}"
            complete(name)
            u = units[name]
            if at == 0:
                out = chain.run(functools.partial(finish, finish_up_kernel, "finish_up", u.order[0], (d, ff)), place, u.keep, u.got)
            elif at == 1:
                out = chain.run(functools.partial(finish, finish_down_kernel, "finish_down", u.order[0], (ff, d)), place, u.keep, u.got)
            elif at == 2:
                out = chain.run(functools.partial(finish_sums, u.order[0], shard), place, u.keep, u.got, u.sums)
                made["flat"] = out[2:]
                out = out[:2]
            else:
                out = chain.run(functools.partial(finish_rows, u.order[0]), place, u.keep, u.got)
            made[name] = out

    def start(name):
        if name[0] == "u":
            return begin(name)
        if name[0] == "G":
            sent[name] = [made["gn2"][int(name[1:])]]
        elif name[0] == "D":
            sent[name] = made["down"]
        if name[0] in "GD":
            move = other_chip
        else:
            move = other_core
        sent[name] = chain.after(sent[name])
        with jax.named_scope(f"send_{name}"):
            got[name] = [move(value) for value in sent[name]]

    for name in SCHEDULE:
        if name[0] == "+":
            start(name[1:])
        elif name[0] == "-":
            chain.need(units[name[1:]].got if name[1] == "u" else got[name[1:]])
        else:
            step(name)
    totals, input_grad, block_output = made["flat"], made["input_grad"], made["block_output"]
    up_grad, down_grad, attn = made["u0"], made["u1"], [*made["u2"], *made["u3"]]
    return (
        block_output,
        input_grad,
        totals[0],
        totals[1],
        attn[0].T,
        totals[6],
        attn[1].T,
        attn[2].T,
        totals[7],
        attn[3],
        totals[2],
        totals[3],
        totals[4],
        up_grad,
        totals[8],
        down_grad,
        totals[5],
    )


def solution(mesh):
    rows, cols, col, copied = P("dp", None), P(None, "tp"), P("tp"), P()
    return jax.shard_map(
        functools.partial(on_device, mesh.shape["dp"], mesh.shape["tp"]),
        mesh=mesh,
        in_specs=(rows, rows, copied, copied, cols, col, cols, cols, col, P("tp", None), copied, copied, copied, cols, col, P("tp", None), copied, rows),
        out_specs=(rows, rows, copied, copied, cols, col, cols, cols, col, P("tp", None), copied, copied, copied, cols, col, P("tp", None), copied),
        check_vma=False,
    )
```

```python
import functools

import jax
import jax.numpy as jnp
from jax import lax
from jax.experimental import pallas as pl
from jax.experimental.pallas import tpu as pltpu
from jax.sharding import PartitionSpec as P

HEAD = 64
SEQ_LEN = 256
EPS = 1e-06
SCALE = 0.125
NEG = -1000000000.0
ROOT_HALF = 0.7071067811865476
INV_ROOT_TAU = 0.3989422804014327
F32 = jnp.float32
BF16 = jnp.bfloat16
VMEM_LIMIT = 14 * 1024 * 1024


def dot_nn(a, b):
    return lax.dot_general(a, b, (((1,), (0,)), ((), ())), preferred_element_type=F32)


def dot_nt(a, b):
    return lax.dot_general(a, b, (((1,), (1,)), ((), ())), preferred_element_type=F32)


def dot_tn(a, b):
    return lax.dot_general(a, b, (((0,), (0,)), ((), ())), preferred_element_type=F32)


def standardize(values):
    centred = values - jnp.mean(values, axis=-1, keepdims=True)
    spread = jnp.mean(centred * centred, axis=-1, keepdims=True)
    scaler = lax.rsqrt(spread + EPS)
    return centred * scaler, scaler


def norm_back(grad_normed, gain, normed, scaler):
    scaled = grad_normed * gain
    centred = scaled - jnp.mean(scaled, axis=-1, keepdims=True)
    return scaler * (centred - normed * jnp.mean(scaled * normed, axis=-1, keepdims=True))


def gelu_parts(hidden):
    cumul = 0.5 * (1.0 + lax.erf(hidden * ROOT_HALF))
    return hidden * cumul, cumul + hidden * (jnp.exp(-0.5 * hidden * hidden) * INV_ROOT_TAU)


def segment_at(pieces_ref, row, amount, shape, axis):
    place = lax.broadcasted_iota(jnp.int32, shape, axis)
    end = jnp.int32(0)
    segment = jnp.zeros(shape, jnp.int32)
    for k in range(amount):
        end = end + pieces_ref[row, k]
        segment = segment + (place >= end).astype(jnp.int32)
    return segment


def mask_bias(pieces_ref, row, amount):
    shape = (SEQ_LEN, SEQ_LEN)
    down = segment_at(pieces_ref, row, amount, shape, 0)
    across = segment_at(pieces_ref, row, amount, shape, 1)
    same = (down == across) & (across < amount - 1)
    diagonal = lax.broadcasted_iota(jnp.int32, shape, 0) == lax.broadcasted_iota(jnp.int32, shape, 1)
    return jnp.where(same | diagonal, 0.0, NEG).astype(F32)


def keep_rows(pieces_ref, row, amount):
    segment = segment_at(pieces_ref, row, amount, (SEQ_LEN, 1), 0)
    return (segment < amount - 1).astype(F32)


def head_lanes(shape):
    return lax.broadcasted_iota(jnp.int32, shape, 1) < HEAD


def both_sides(values, low_lanes):
    zero = jnp.zeros_like(values)
    return jnp.concatenate([jnp.where(low_lanes, values, zero), jnp.where(low_lanes, zero, values)], axis=0)


def attend(qkv_ref, rows, bias, width):
    low_lanes = head_lanes((SEQ_LEN, 2 * HEAD))
    lane = lax.broadcasted_iota(jnp.int32, (SEQ_LEN, 2 * HEAD), 1)
    logs = jnp.zeros((SEQ_LEN, 2 * HEAD), F32)
    pairs = range(width // (2 * HEAD))
    where = [[slice(k * width + p * 2 * HEAD, k * width + (p + 1) * 2 * HEAD) for k in range(3)] for p in pairs]
    scores = [dot_nt(both_sides(qkv_ref[rows, where[p][0]], low_lanes), qkv_ref[rows, where[p][1]]) for p in pairs]
    mixed = []
    for p in pairs:
        probs = []
        for side in range(2):
            mine = scores[p][side * SEQ_LEN : (side + 1) * SEQ_LEN] + bias
            largest = jnp.max(mine, axis=-1, keepdims=True)
            weights = jnp.exp(mine - largest)
            totals = jnp.sum(weights, axis=-1, keepdims=True)
            probs.append((weights * (1.0 / totals)).astype(BF16))
            logs = jnp.where(lane == 2 * p + side, largest + jnp.log(totals), logs)
        out = dot_nn(jnp.concatenate(probs, axis=0), qkv_ref[rows, where[p][2]])
        mixed.append(jnp.where(low_lanes, out[:SEQ_LEN], out[SEQ_LEN:]).astype(BF16))
    return jnp.concatenate(mixed, axis=1), logs


def held(*_):
    return pl.BlockSpec(memory_space=pltpu.VMEM)


def seq_rows(seq):
    return pl.ds(pl.multiple_of(seq * SEQ_LEN, SEQ_LEN), SEQ_LEN)


def anywhere(*_):
    return pl.BlockSpec(memory_space=pltpu.HBM)


def call(kernel, name, scalars, operands, outs, grid=(1,), scratch=(), loose=0, free=0, limit=VMEM_LIMIT, us=1.0):
    return pl.pallas_call(
        kernel,
        grid_spec=pltpu.PrefetchScalarGridSpec(
            num_scalar_prefetch=len(scalars), grid=grid, in_specs=[anywhere()] * loose + [held()] * (len(operands) - loose), out_specs=[anywhere()] * free + [held()] * (len(outs) - free), scratch_shapes=list(scratch)),
        out_shape=[jax.ShapeDtypeStruct(shape, dtype) for shape, dtype in outs],
        compiler_params=pltpu.CompilerParams(vmem_limit_bytes=limit),
        cost_estimate=pl.CostEstimate(flops=int(us * 5e8), bytes_accessed=int(us * 1e6), transcendentals=0),
        name=name,
    )(*scalars, *operands)


def copy_all(copies, sems):
    started = [pltpu.make_async_copy(source, target, sems.at[at]) for at, (source, target) in enumerate(copies)]
    for copy in started:
        copy.start()
    return started


def column_sum(values):
    return jnp.sum(values.reshape(values.shape[0] // 8, 8, values.shape[1]), axis=0)


VECTORS = 6
BITS = 2
TAIL = 16


def vectors_kernel(shard, small_ref, vectors_ref, row_ref):
    d = vectors_ref.shape[1]

    def vector(at, size):
        return small_ref[pl.ds(at, size)].reshape(1, size)

    vectors_ref[...] = jnp.zeros_like(vectors_ref)
    for k in range(VECTORS):
        vectors_ref[k : k + 1, :] = vector(k * d, d)
    ff = row_ref.shape[1] - 4 * shard
    row_ref[:, 4 * shard :] = vector(VECTORS * d, ff)
    zero = jnp.zeros((1, shard), F32)
    at = VECTORS * d + ff
    row_ref[:, : 4 * shard] = jnp.concatenate([vector(at, shard), zero, vector(at + shard, shard), zero], axis=1)


def gather_vectors(small, shard, d, ff):
    return call(functools.partial(vectors_kernel, shard), "vectors", (), (small,), [((8, d), F32), ((1, 4 * shard + ff), F32)])


def join_kernel(place_ref, first_ref, second_ref, v_ref, row_ref, out_ref):
    shard, d = first_ref.shape
    out_ref[pl.ds(pl.multiple_of(place_ref[BITS] * shard, shard), shard), :] = first_ref[...]
    out_ref[pl.ds(pl.multiple_of((1 - place_ref[BITS]) * shard, shard), shard), :] = second_ref[...]
    out_ref[2 * shard : 3 * shard, :] = v_ref[...]
    rest = row_ref[:, : 4 * shard]
    rows = []
    for _ in range(3):
        part = rest.astype(BF16).astype(F32)
        rows.append(part)
        rest = rest - part
    rows.append(jnp.zeros((TAIL - 3, 4 * shard), F32))
    out_ref[3 * shard :, : 4 * shard] = jnp.concatenate(rows, axis=0).astype(BF16)


def join_weights(place, first, second, v, row):
    shard, d = first.shape
    return call(join_kernel, "join", (place,), (first, second, v, row), [((3 * shard + TAIL, d), BF16)])[0]


def spread_bias(a, b, shard):
    return a + jnp.concatenate([jnp.zeros((1, shard), F32), b[:, : 3 * shard]], axis=1)


def project(lowered, w_ref, bias, qkv_ref, at, width):
    for k in range(3):
        proj = dot_nt(lowered, w_ref[k * width : (k + 1) * width, :])
        if k == 0:
            proj = (proj + bias[:, :width]).astype(BF16) * jnp.asarray(SCALE, BF16)
        elif k == 2:
            proj = proj + bias[:, width:]
        qkv_ref[at, k * width : (k + 1) * width] = proj.astype(BF16)


def project_kernel(shard, place_ref, x_ref, vectors_ref, a_ref, b_ref, *refs):
    w_refs, (w_ref, normed_ref, qkv_ref) = refs[:6], refs[6:]
    step = pl.program_id(0)
    width = 2 * shard

    @pl.when(step == 0)
    def _():
        for k, ref in enumerate(w_refs):
            to = (k % 3) * width + (k // 3) * shard
            w_ref[to : to + shard, :] = ref[...]

    normed, _ = standardize(x_ref[seq_rows(place_ref[0] + step), :].astype(F32))
    lowered = (normed * vectors_ref[0:1, :] + vectors_ref[1:2, :]).astype(BF16)
    at = seq_rows(step)
    normed_ref[at, :] = lowered
    bias = spread_bias(a_ref[:, : 4 * shard], b_ref[:, : 4 * shard], shard)
    project(lowered, w_ref, bias, qkv_ref, at, width)


def project_own(rows, place, x, vectors, a, b, weights):
    shard, d = weights[0].shape
    outs = [((6 * shard, d), BF16), ((rows, d), BF16), ((rows, 6 * shard), BF16)]
    return call(functools.partial(project_kernel, shard), "project_own", (place,), (x, vectors, a, b, *weights), outs, (rows // SEQ_LEN,), us=3.5)


def attend_kernel(amount, width, place_ref, pieces_ref, qkv_ref, wa_ref, wb_ref, mixed_ref, logs_ref, part_ref, wo_ref):
    step = pl.program_id(0)

    @pl.when(step == 0)
    def _():
        wo_ref[: width // 2, :] = wa_ref[...]
        wo_ref[width // 2 :, :] = wb_ref[...]

    at = seq_rows(step)
    mixed, logs = attend(qkv_ref, at, mask_bias(pieces_ref, place_ref[0] + step, amount), width)
    logs_ref[pl.ds(pl.multiple_of(step * 8, 8), 8), :] = logs.T[:8, :]
    mixed_ref[at, :] = mixed
    part_ref[at, :] = dot_nn(mixed, wo_ref[...])


def attend_own(place, pieces, qkv, wa, wb):
    seqs, amount = pieces.shape[0] // 2, pieces.shape[1]
    width, d = 2 * wa.shape[0], wa.shape[1]
    rows = seqs * SEQ_LEN
    outs = [((rows, width), BF16), ((seqs * 8, SEQ_LEN), F32), ((rows, d), F32), ((width, d), BF16)]
    return call(functools.partial(attend_kernel, amount, width), "attend_own", (place, pieces), (qkv, wa, wb), outs, (seqs,), us=4.9)


def other_kernel(amount, shard, place_ref, pieces_ref, a_ref, b_ref, normed_in_ref, w_ref, qkv_ref, logs_ref, mixed_ref):
    step = pl.program_id(0)
    width = 2 * shard

    @pl.when(step == 0)
    def _():
        for side, ref in enumerate((a_ref, b_ref)):
            for k in range(3):
                to = k * width + side * shard
                w_ref[to : to + shard, :] = ref[k * shard : (k + 1) * shard, :]

    at = seq_rows(step)
    a, b = (jnp.sum(ref[3 * shard : 3 * shard + 3, : 4 * shard].astype(F32), axis=0, keepdims=True) for ref in (a_ref, b_ref))
    project(normed_in_ref[at, :], w_ref, spread_bias(a, b, shard), qkv_ref, at, width)
    mixed, logs = attend(qkv_ref, at, mask_bias(pieces_ref, place_ref[0] + step, amount), width)
    logs_ref[pl.ds(pl.multiple_of(step * 8, 8), 8), :] = logs.T[:8, :]
    mixed_ref[at, :] = mixed


def attend_other(place, pieces, a, b, normed):
    seqs, amount = pieces.shape[0] // 2, pieces.shape[1]
    shard, d = (a.shape[0] - TAIL) // 3, a.shape[1]
    rows = seqs * SEQ_LEN
    outs = [((6 * shard, d), BF16), ((rows, 6 * shard), BF16), ((seqs * 8, SEQ_LEN), F32), ((rows, 2 * shard), BF16)]
    return call(functools.partial(other_kernel, amount, shard), "attend_other", (place, pieces), (a, b, normed), outs, (seqs,), us=6.0)


def middle_kernel(amount, place_ref, pieces_ref, wa_ref, wb_ref, x_ref, mixed_ref, part_in_ref, vectors_ref, w_ref, middle_ref, normed_ref, sum_ref):
    step = pl.program_id(0)
    shard = wa_ref.shape[0]
    first = place_ref[0] * SEQ_LEN

    @pl.when(step == 0)
    def _():
        w_ref[:shard, :] = wa_ref[...]
        w_ref[shard:, :] = wb_ref[...]

    at = seq_rows(step)
    sum_ref[...] = dot_nn(mixed_ref[at, :], w_ref[...])
    keep_all = keep_rows(pieces_ref, place_ref[0] + step, amount)
    block = 64
    for r in range(0, SEQ_LEN, block):
        here = pl.ds(pl.multiple_of(step * SEQ_LEN + r, block), block)
        added = part_in_ref[here, :] + sum_ref[r : r + block, :] + vectors_ref[2:3, :]
        middle = x_ref[pl.ds(pl.multiple_of(first + step * SEQ_LEN + r, block), block), :].astype(F32) + keep_all[r : r + block] * added
        middle_ref[here, :] = middle
        normed, _ = standardize(middle)
        normed_ref[here, :] = (normed * vectors_ref[3:4, :] + vectors_ref[4:5, :]).astype(BF16)


def middle_rows(place, pieces, wa, wb, x, mixed, part, vectors):
    (rows, width), d = mixed.shape, x.shape[1]
    outs = [((width, d), BF16), ((rows, d), F32), ((rows, d), BF16)]
    return call(functools.partial(middle_kernel, pieces.shape[1]), "middle", (place, pieces), (wa, wb, x, mixed, part, vectors), outs, (rows // SEQ_LEN,),
                [pltpu.VMEM((SEQ_LEN, d), F32)], us=3.0)


def mlp_kernel(amount, first, seqs, place_ref, pieces_ref, n2_ref, cot_ref, ba_ref, bb_ref, upa_ref, upb_ref, dna_ref, dnb_ref,
               active_ref, gh_ref, gb_ref, sums_ref, n2_out_ref, *gn2_refs):
    ff = upa_ref.shape[1]
    skip = ba_ref.shape[1] - ff
    block = 256 if ff % 256 == 0 else ff
    total = [None] * (2 * ff // block)
    for s in range(seqs):
        rows = slice(s * SEQ_LEN, (s + 1) * SEQ_LEN)
        here = slice((first + s) * SEQ_LEN, (first + s + 1) * SEQ_LEN)
        keep = keep_rows(pieces_ref, place_ref[0] + first + s, amount)
        branch = (keep * cot_ref[seq_rows(place_ref[0] + first + s), :].astype(F32)).astype(BF16)
        gb_ref[rows, :] = branch
        n2 = n2_ref[here, :]
        n2_out_ref[rows, :] = n2
        for side, (up_ref, dn_ref, bias_ref) in enumerate(((upa_ref, dna_ref, ba_ref), (upb_ref, dnb_ref, bb_ref))):
            for j in range(0, ff, block):
                at = slice(side * ff + j, side * ff + j + block)
                hidden = dot_nn(n2, up_ref[:, j : j + block]) + bias_ref[:, skip + j : skip + j + block]
                active, slope = gelu_parts(hidden)
                active_ref[rows, at] = active.astype(BF16)
                grad_active = dot_nt(branch, dn_ref[j : j + block, :])
                grad_hidden = (grad_active * slope).astype(BF16)
                gh_ref[rows, at] = grad_hidden
                part = jnp.sum(grad_hidden.astype(F32), axis=0, keepdims=True)
                k = at.start // block
                total[k] = part if total[k] is None else total[k] + part
        gn2_refs[s][...] = (dot_nt(gh_ref[rows, :ff], upa_ref[...]) + dot_nt(gh_ref[rows, ff:], upb_ref[...])).astype(BF16)
    for k, part in enumerate(total):
        sums_ref[:, k * block : (k + 1) * block] = part


def mlp_rows(first, seqs, place, pieces, n2, cot, bias, bias_b, upa, upb, dna, dnb):
    d, ff = upa.shape
    rows = seqs * SEQ_LEN
    outs = [((rows, 2 * ff), BF16), ((rows, 2 * ff), BF16), ((rows, d), BF16), ((1, 2 * ff), F32), ((rows, d), BF16)] + [((SEQ_LEN, d), BF16)] * seqs
    return call(functools.partial(mlp_kernel, pieces.shape[1], first, seqs), "mlp", (place, pieces), (n2, cot, bias, bias_b, upa, upb, dna, dnb), outs, us=2.7 * seqs)


def down_kernel(count, dna_ref, dnb_ref, *refs):
    ff = dna_ref.shape[0]
    out_ref = refs[-1]
    at = 0
    for active_ref in refs[:count]:
        for r in range(0, active_ref.shape[0], SEQ_LEN):
            rows = slice(r, r + SEQ_LEN)
            out_ref[at : at + SEQ_LEN, :] = (dot_nn(active_ref[rows, :ff], dna_ref[...]) + dot_nn(active_ref[rows, ff:], dnb_ref[...])).astype(BF16)
            at += SEQ_LEN


def down_rows(dna, dnb, actives):
    rows, d = sum(a.shape[0] for a in actives), dna.shape[1]
    return call(functools.partial(down_kernel, len(actives)), "down", (), (dna, dnb, *actives), [((rows, d), BF16)], us=2.0)


def sent_kernel(count, side, *refs):
    out_ref = refs[-1]
    size = out_ref.shape[0]
    block = 256 if size % 256 == 0 else size
    for j in range(0, size, block):
        at = slice(side * size + j, side * size + j + block)
        total = sum(dot_tn(refs[k][:, at], refs[count + k][...]) for k in range(count))
        out_ref[j : j + block, :] = total.astype(BF16)


def grad_sent(side, lefts, rights):
    size, d = lefts[0].shape[1] // 2, rights[0].shape[1]
    return call(functools.partial(sent_kernel, len(lefts), side), "grad_sent", (), (*lefts, *rights), [((size, d), BF16)], us=1.1)


def kept_kernel(count, bit, place_ref, *refs):
    add_ref, send_ref, keep_ref = refs[-3:]
    half = keep_ref.shape[0]
    for which, out_ref in enumerate((send_ref, keep_ref)):
        mine = place_ref[BITS + bit] if which else 1 - place_ref[BITS + bit]
        at = pl.ds(pl.multiple_of(mine * half, half), half)
        total = sum(dot_tn(refs[k][:, at], refs[count + k][...]) for k in range(count))
        out_ref[...] = (total + add_ref[at, :].astype(F32)).astype(BF16)


def grad_kept(bit, place, lefts, rights, add):
    half, d = lefts[0].shape[1] // 4, rights[0].shape[1]
    return call(functools.partial(kept_kernel, len(lefts), bit), "grad_kept", (place,), (*lefts, *rights, add), [((half, d), BF16)] * 2, us=1.7)


def attn_dots(refs, attns, n1_ref, seqs, shard, side, kind):
    width = 2 * shard
    at = slice(kind * width + side * shard, kind * width + (side + 1) * shard)
    rights = [attns[s][...] if kind == 3 else n1_ref[s * SEQ_LEN : (s + 1) * SEQ_LEN, :] for s in range(seqs)]
    return sum(dot_tn(refs[s][:, at], rights[s]) for s in range(seqs))


def attn_sent_kernel(seqs, kinds, *refs):
    out_ref = refs[-1]
    shard = out_ref.shape[0] // len(kinds)
    for k, kind in enumerate(kinds):
        out_ref[k * shard : (k + 1) * shard, :] = attn_dots(refs[:seqs], refs[seqs : 2 * seqs], refs[2 * seqs], seqs, shard, 1, kind).astype(BF16)


def attn_sent(kinds, lefts, attns, n1):
    shard, d = lefts[0].shape[1] // 8, n1.shape[1]
    return call(functools.partial(attn_sent_kernel, len(lefts), kinds), "attn_sent", (), (*lefts, *attns, n1), [((len(kinds) * shard, d), BF16)], us=0.9)


def attn_kept_kernel(seqs, kinds, bit, place_ref, *refs):
    add_ref, send_ref, keep_ref, both_ref = refs[-4:]
    shard = keep_ref.shape[0]
    for which, kind in enumerate(kinds):
        total = attn_dots(refs[:seqs], refs[seqs : 2 * seqs], refs[2 * seqs], seqs, shard, 0, kind)
        at = slice(which * shard, (which + 1) * shard)
        both_ref[at, :] = (total + add_ref[at, :].astype(F32)).astype(BF16)
    mine = place_ref[BITS + bit]
    for out_ref, chosen in ((keep_ref, mine), (send_ref, 1 - mine)):
        out_ref[...] = both_ref[pl.ds(pl.multiple_of(chosen * shard, shard), shard), :]


def attn_kept(kinds, bit, place, lefts, attns, n1, add):
    shard, d = lefts[0].shape[1] // 8, n1.shape[1]
    return call(functools.partial(attn_kept_kernel, len(lefts), kinds, bit), "attn_kept", (place,), (*lefts, *attns, n1, add), [((shard, d), BF16)] * 2,
                scratch=[pltpu.VMEM((2 * shard, d), BF16)], us=1.2)


def attend_back(qkv_ref, rows, gm_ref, logs_ref, first, bias, width, grads_ref):
    low_lanes = head_lanes((SEQ_LEN, 2 * HEAD))
    pairs = range(width // (2 * HEAD))
    where = [[slice(k * width + p * 2 * HEAD, k * width + (p + 1) * 2 * HEAD) for k in range(3)] for p in pairs]
    scores = [dot_nt(both_sides(qkv_ref[rows, where[p][1]], low_lanes), qkv_ref[rows, where[p][0]]) for p in pairs]
    grad_probs = [dot_nt(both_sides(qkv_ref[rows, where[p][2]], low_lanes), gm_ref[:, where[p][0]]) for p in pairs]
    for p in pairs:
        probs, grad_scores = [], []
        for side in range(2):
            mine = slice(side * SEQ_LEN, (side + 1) * SEQ_LEN)
            head = first + 2 * p + side
            prob = jnp.exp(scores[p][mine] + bias - logs_ref[head : head + 1, :])
            inner = jnp.sum(grad_probs[p][mine] * prob, axis=0, keepdims=True)
            grad_scores.append((prob * (grad_probs[p][mine] - inner)).astype(BF16))
            probs.append(prob.astype(BF16))
        grad_key = dot_nn(jnp.concatenate(grad_scores, axis=0), qkv_ref[rows, where[p][0]])
        grad_value = dot_nn(jnp.concatenate(probs, axis=0), gm_ref[:, where[p][0]])
        grad_query = dot_tn(jnp.concatenate(grad_scores, axis=1), qkv_ref[rows, where[p][1]])
        grads_ref[:, where[p][0]] = (jnp.where(low_lanes, grad_query[:SEQ_LEN], grad_query[SEQ_LEN:]) * SCALE).astype(BF16)
        grads_ref[:, where[p][1]] = jnp.where(low_lanes, grad_key[:SEQ_LEN], grad_key[SEQ_LEN:]).astype(BF16)
        grads_ref[:, where[p][2]] = jnp.where(low_lanes, grad_value[:SEQ_LEN], grad_value[SEQ_LEN:]).astype(BF16)


def own_back_kernel(amount, seq, place_ref, pieces_ref, cot_ref, middle_ref, own_ref, got_ref, vectors_ref, qkv_ref, logs_ref, mixed_ref, w_ref, wo_ref,
                    grad_ref, all_ref, attn_ref, part_ref, sums_ref, gm_ref):
    row = place_ref[0] + seq
    width = mixed_ref.shape[1]
    d = cot_ref.shape[1]
    keep_all = keep_rows(pieces_ref, row, amount)
    sums = [jnp.zeros((8, d), F32)] * 4
    block = 32
    for r in range(0, SEQ_LEN, block):
        at = slice(r, r + block)
        keep = keep_all[at]
        cot = cot_ref[pl.ds(pl.multiple_of(row * SEQ_LEN + r, block), block), :].astype(F32)
        gn2 = own_ref[at, :].astype(F32) + got_ref[at, :].astype(F32)
        normed, scaler = standardize(middle_ref[seq * SEQ_LEN + r : seq * SEQ_LEN + r + block, :])
        grad_middle = cot + norm_back(gn2, vectors_ref[3:4, :], normed, scaler)
        attn = (keep * grad_middle).astype(BF16)
        attn_ref[at, :] = attn
        grad_ref[at, :] = grad_middle
        terms = (attn.astype(F32), gn2 * normed, gn2, (keep * cot).astype(BF16).astype(F32))
        sums = [s + column_sum(t) for s, t in zip(sums, terms)]
    sums_ref[...] = jnp.zeros_like(sums_ref)
    for k in range(4):
        sums_ref[2 + k : 3 + k, :] = jnp.sum(sums[k], axis=0, keepdims=True)
    gm_ref[...] = dot_nt(attn_ref[...], wo_ref[...]).astype(BF16)
    rows = slice(seq * SEQ_LEN, (seq + 1) * SEQ_LEN)
    attend_back(qkv_ref, rows, gm_ref, logs_ref, 8 * seq, mask_bias(pieces_ref, row, amount), width, all_ref)
    part_ref[...] = dot_nn(all_ref[:, : 3 * width], w_ref[...])
    all_ref[:, 3 * width :] = mixed_ref[rows, :]
    sums_ref[6:7, :width] = jnp.sum(all_ref[:, :width].astype(F32), axis=0, keepdims=True)
    sums_ref[7:8, :width] = jnp.sum(all_ref[:, 2 * width : 3 * width].astype(F32), axis=0, keepdims=True)


def own_back(seq, place, pieces, cot, middle, own, got, vectors, qkv, logs, mixed, w, wo):
    d, width = cot.shape[1], mixed.shape[1]
    outs = [((SEQ_LEN, d), F32), ((SEQ_LEN, 4 * width), BF16), ((SEQ_LEN, d), BF16), ((SEQ_LEN, d), F32), ((8, d), F32)]
    return call(functools.partial(own_back_kernel, pieces.shape[1], seq), "own_back", (place, pieces),
                (cot, middle, own, got, vectors, qkv, logs, mixed, w, wo), outs, scratch=[pltpu.VMEM((SEQ_LEN, width), BF16)], us=5.2)


def other_back_kernel(amount, seq, place_ref, pieces_ref, x_ref, grad_in_ref, attn_ref, part_ref, vectors_ref, qkv_ref, logs_ref, w_ref, wo_ref,
                      grad_ref, sums_ref, gm_ref, all_ref, sum_ref):
    row = place_ref[0] + seq
    width = gm_ref.shape[1]
    d = x_ref.shape[1]
    bias = mask_bias(pieces_ref, row, amount)
    gm_ref[...] = dot_nt(attn_ref[...], wo_ref[...]).astype(BF16)
    rows = slice(seq * SEQ_LEN, (seq + 1) * SEQ_LEN)
    attend_back(qkv_ref, rows, gm_ref, logs_ref, 8 * seq, bias, width, all_ref)
    sum_ref[...] = dot_nn(all_ref[...], w_ref[...])
    sums = [jnp.zeros((8, d), F32)] * 2
    block = 32
    for r in range(0, SEQ_LEN, block):
        at = slice(r, r + block)
        gn1 = part_ref[at, :] + sum_ref[at, :]
        normed, scaler = standardize(x_ref[pl.ds(pl.multiple_of(row * SEQ_LEN + r, block), block), :].astype(F32))
        grad_ref[at, :] = grad_in_ref[at, :] + norm_back(gn1, vectors_ref[0:1, :], normed, scaler)
        sums = [s + column_sum(t) for s, t in zip(sums, (gn1 * normed, gn1))]
    sums_ref[...] = jnp.zeros_like(sums_ref)
    for k in range(2):
        sums_ref[k : k + 1, :] = jnp.sum(sums[k], axis=0, keepdims=True)


def other_back(seq, place, pieces, x, grad_in, attn, part, vectors, qkv, logs, w, wo):
    d, width = wo.shape[1], wo.shape[0]
    outs = [((SEQ_LEN, d), F32), ((8, d), F32)]
    return call(functools.partial(other_back_kernel, pieces.shape[1], seq), "other_back", (place, pieces),
                (x, grad_in, attn, part, vectors, qkv, logs, w, wo), outs,
                scratch=[pltpu.VMEM((SEQ_LEN, width), BF16), pltpu.VMEM((SEQ_LEN, 3 * width), BF16), pltpu.VMEM((SEQ_LEN, d), F32)], us=4.5)


def output_kernel(amount, place_ref, pieces_ref, middle_ref, vectors_ref, own_ref, got_ref, out_ref):
    block = 64
    for seq in range(out_ref.shape[0] // SEQ_LEN):
        keep_all = keep_rows(pieces_ref, place_ref[0] + seq, amount)
        for r in range(0, SEQ_LEN, block):
            at = slice(seq * SEQ_LEN + r, seq * SEQ_LEN + r + block)
            total = own_ref[at, :].astype(F32) + got_ref[at, :].astype(F32) + vectors_ref[5:6, :]
            out_ref[at, :] = (middle_ref[at, :] + keep_all[r : r + block] * total).astype(BF16)


def output_rows(place, pieces, middle, vectors, own, got):
    return call(functools.partial(output_kernel, pieces.shape[1]), "block_output", (place, pieces),
                (middle, vectors, own, got), [(middle.shape, BF16)], us=1.4)


def both_kernel(count, place_ref, *refs):
    out_ref, sems = refs[-2:]
    size = refs[0].shape[0]
    copies = []
    for k in range(2 * count):
        at = (place_ref[1] if k < count else 1 - place_ref[1]) * count + k % count
        copies.append(pltpu.make_async_copy(refs[k], out_ref.at[pl.ds(pl.multiple_of(at * size, size), size)], sems.at[k]))
        copies[-1].start()
    for copy in copies:
        copy.wait()


def both_cores(place, mine, theirs):
    count = len(mine)
    rows, d = mine[0].shape
    return pl.pallas_call(
        functools.partial(both_kernel, count),
        grid_spec=pltpu.PrefetchScalarGridSpec(
            num_scalar_prefetch=1, grid=(1,), in_specs=[held()] * (2 * count), out_specs=pl.BlockSpec(memory_space=pl.ANY),
            scratch_shapes=[pltpu.SemaphoreType.DMA((2 * count,))]),
        out_shape=jax.ShapeDtypeStruct((2 * count * rows, d), mine[0].dtype),
        compiler_params=pltpu.CompilerParams(vmem_limit_bytes=VMEM_LIMIT),
        cost_estimate=pl.CostEstimate(flops=1, bytes_accessed=1, transcendentals=0),
        name="both_cores",
    )(place, *mine, *theirs)


def swap(size, bit):
    return [(i, i ^ bit) for i in range(size)]


def tie(values, *after):
    return lax.optimization_barrier((values, after))[0]


def merge_kernel(at, place_ref, keep_ref, got_ref, send_ref, out_ref):
    size = out_ref.shape[0]
    for which, ref in enumerate((send_ref, out_ref)):
        bit = place_ref[BITS + at] if which else 1 - place_ref[BITS + at]
        rows = pl.ds(pl.multiple_of(bit * size, size), size)
        ref[...] = (keep_ref[rows, :].astype(F32) + got_ref[rows, :].astype(F32)).astype(BF16)


def merge(bit, place, keep, got):
    rows, d = keep.shape
    half = rows // 2
    if half % 16:
        total = (keep.astype(F32) + got.astype(F32)).astype(BF16)
        low = place[BITS + bit] == 0
        return jnp.where(low, total[half:], total[:half]), jnp.where(low, total[:half], total[half:])
    return call(functools.partial(merge_kernel, bit), "merge", (place,), (keep, got), [((half, d), BF16)] * 2, us=0.6)


def add_kernel(keep_ref, got_ref, out_ref):
    out_ref[...] = (keep_ref[...].astype(F32) + got_ref[...].astype(F32)).astype(out_ref.dtype)


def add(keep, got):
    return call(add_kernel, "add", (), (keep, got), [(keep.shape, keep.dtype)])[0]


def grow_kernel(at, place_ref, keep_ref, got_ref, out_ref):
    size = keep_ref.shape[0]
    out_ref[pl.ds(pl.multiple_of(place_ref[BITS + at] * size, size), size), :] = keep_ref[...]
    out_ref[pl.ds(pl.multiple_of((1 - place_ref[BITS + at]) * size, size), size), :] = got_ref[...]


def grow(bit, place, keep, got):
    rows, d = keep.shape
    if rows % 16:
        return jnp.where(place[BITS + bit] == 0, jnp.concatenate([keep, got]), jnp.concatenate([got, keep]))
    return call(functools.partial(grow_kernel, bit), "grow", (place,), (keep, got), [((2 * rows, d), BF16)])[0]


def finish_up_kernel(at, place_ref, keep_ref, got_ref, out_ref):
    size = keep_ref.shape[0]
    out_ref[:, pl.ds(pl.multiple_of(place_ref[BITS + at] * size, 128), size)] = keep_ref[...].astype(F32).T
    out_ref[:, pl.ds(pl.multiple_of((1 - place_ref[BITS + at]) * size, 128), size)] = got_ref[...].astype(F32).T


def finish_down_kernel(at, place_ref, keep_ref, got_ref, out_ref):
    size = keep_ref.shape[0]
    out_ref[pl.ds(pl.multiple_of(place_ref[BITS + at] * size, size), size), :] = keep_ref[...].astype(F32)
    out_ref[pl.ds(pl.multiple_of((1 - place_ref[BITS + at]) * size, size), size), :] = got_ref[...].astype(F32)


def finish(kernel, name, bit, shape, place, keep, got):
    return call(functools.partial(kernel, bit), name, (place,), (keep, got), [(shape, F32)])[0]


def put_parts(out_ref, at, sums):
    rows, d = sums.shape
    parts = []
    for _ in range(3):
        part = sums.astype(BF16).astype(F32)
        parts.append(part)
        sums = sums - part
    parts.append(jnp.zeros((out_ref.shape[0] - at - 3 * rows, d), F32))
    out_ref[at:, :] = jnp.concatenate(parts, axis=0).astype(BF16)


def get_parts(ref, at, rows):
    parts = ref[at:, :].astype(F32)
    return sum(parts[k * rows : (k + 1) * rows] for k in range(3))


def add_sums_kernel(rows, first, keep_ref, got_ref, sums_ref, more_ref, send_ref, out_ref, total_ref):
    size = keep_ref.shape[0]
    kept = (keep_ref[...].astype(F32) + got_ref[:size, :].astype(F32)).astype(BF16)
    out_ref[...] = kept
    send_ref[:size, :] = kept
    total = sums_ref[...] + (more_ref[...] if first else get_parts(more_ref, size, rows))
    total_ref[...] = total
    put_parts(send_ref, size, total)


def add_sums(keep, got, sums, more):
    first = more is None
    size, d = keep.shape
    rows = sums.shape[0]
    padded = -(-3 * rows // 16) * 16
    return call(functools.partial(add_sums_kernel, rows, not first), "add_sums", (), (keep, got, sums, got if first else more),
                [((size + padded, d), BF16), (keep.shape, BF16), (sums.shape, F32)], us=0.6)


def grow_sums_kernel(at, rows, size, place_ref, keep_ref, got_ref, sums_ref, send_ref, total_ref):
    send_ref[pl.ds(pl.multiple_of(place_ref[BITS + at] * size, size), size), :] = keep_ref[:size, :]
    send_ref[pl.ds(pl.multiple_of((1 - place_ref[BITS + at]) * size, size), size), :] = got_ref[:size, :]
    total = sums_ref[...] + get_parts(got_ref, size, rows)
    total_ref[...] = total
    put_parts(send_ref, 2 * size, total)


def grow_sums(bit, place, keep, got, sums):
    rows, d = sums.shape
    padded = -(-3 * rows // 16) * 16
    size = got.shape[0] - padded
    keep = keep[:size] if size % 16 else keep
    if size % 16:
        low = place[BITS + bit] == 0
        kept = jnp.where(low, jnp.concatenate([keep, got[:size]]), jnp.concatenate([got[:size], keep]))
        parts = got[size:].astype(F32)
        total = sums + sum(parts[k * rows : (k + 1) * rows] for k in range(3))
        rest, split = total, []
        for _ in range(3):
            split.append(lax.reduce_precision(rest, 8, 7))
            rest = rest - split[-1]
        split.append(jnp.zeros((padded - 3 * rows, d), F32))
        return jnp.concatenate([kept, jnp.concatenate(split).astype(BF16)]), kept, total
    send, total = call(functools.partial(grow_sums_kernel, bit, rows, size), "grow_sums", (place,), (keep, got, sums),
                       [((2 * size + padded, d), BF16), (sums.shape, F32)], us=0.7)
    return send, send, total


def attn_out_kernel(first, second, rows, shard, place_ref, keep_ref, got_ref, sums_ref, keep2_ref, got2_ref, q_ref, k_ref, v_ref, o_ref, *refs):
    flat_refs, held_ref, sems = refs[:-2], refs[-2], refs[-1]
    size = held_ref.shape[1]
    todo = []
    for bit, own_ref, other_ref, low_ref, high_ref in ((first, keep_ref, got_ref, q_ref, k_ref), (second, keep2_ref, got2_ref, v_ref, o_ref)):
        mine = place_ref[BITS + bit] == 0
        for ref, one_ref, two_ref in ((own_ref, low_ref, high_ref), (other_ref, high_ref, low_ref)):
            at = len(todo)
            held_ref[at] = ref[:size, :].astype(F32)
            for chosen, out_ref in ((mine, one_ref), (jnp.logical_not(mine), two_ref)):
                @pl.when(chosen)
                def _():
                    pltpu.make_async_copy(held_ref.at[at], out_ref, sems.at[at]).start()

            todo.append(one_ref)
    total = sums_ref[...] + get_parts(got_ref, size, rows)
    for k in range(6):
        flat_refs[k][...] = total[k]
    flat_refs[6][...] = total[6, :shard]
    flat_refs[7][...] = total[6, shard : 2 * shard]
    d = total.shape[1]
    for k in range(7, rows):
        flat_refs[8][pl.ds((k - 7) * d, d)] = total[k]
    for at, out_ref in enumerate(todo):
        pltpu.make_async_copy(held_ref.at[at], out_ref, sems.at[at]).wait()


def finish_attn(first, second, shard, place, keep, got, sums, keep2, got2):
    rows, d = sums.shape
    size = keep2.shape[0]
    outs = [((size, d), F32)] * 4 + [((d,), F32)] * 6 + [((shard,), F32)] * 2 + [(((rows - 7) * d,), F32)]
    return call(functools.partial(attn_out_kernel, first, second, rows, shard), "finish_attn", (place,), (keep, got, sums, keep2, got2), outs, free=4, us=2.0,
                scratch=[pltpu.VMEM((4, size, d), F32), pltpu.SemaphoreType.DMA((4,))])


class Unit:
    def __init__(self, groups, order, place, send, keep):
        self.groups, self.order, self.place = groups, order, place
        self.send, self.keep, self.step = send, keep, 0
        self.middle = len(order) - 1
        self.last = 2 * self.middle

    def start(self):
        at = min(self.step, self.last - self.step)
        self.got = lax.ppermute(self.send, "dp", swap(self.groups, 1 << self.order[at]))

    def take(self):
        if self.step < self.middle - 1:
            self.send, self.keep = merge(self.order[self.step + 1], self.place, self.keep, self.got)
        elif self.step <= self.middle:
            self.send = self.keep = add(self.keep, self.got)
        else:
            self.send = self.keep = grow(self.order[self.last - self.step], self.place, self.keep, self.got)
        self.step += 1


class SumsUnit(Unit):
    def take(self):
        if self.step < self.middle - 1:
            return super().take()
        if self.step <= self.middle:
            more = self.more if self.step == self.middle - 1 else None
            self.send, self.keep, self.sums = add_sums(self.keep, self.got, self.sums, more)
        else:
            self.send, self.keep, self.sums = grow_sums(self.order[self.last - self.step], self.place, self.keep, self.got, self.sums)
        self.step += 1


class Chain:
    def __init__(self):
        self.last = ()

    def run(self, kernel, *args, need=()):
        args = tie(args, self.last, need)
        out = kernel(*args)
        self.last = out
        return out

    def after(self, values):
        return tie(values, self.last)

    def need(self, values):
        self.last = (self.last, values)


SCHEDULE = (
    "mlp0", "mlp1", "+G2", "gs0", "+G1", "+cb0", "gs1", "+cb1", "down", "gk0", "+u0", "gk1", "+u1", "ob2", "+G0", "xb2", "u0", "+u0",
    "ob1", "u1", "+u1", "ob0", "ao1", "+D0", "ao0", "+ca0", "u1", "u0", "+ca1", "+u1", "+u0", "xb0", "ak0", "+u2", "ak1", "u0", "+u0",
    "+u3", "xb1", "u1", "+u1", "sums", "u2", "+u2", "+sc", "u3", "+u3", "out", "u2", "+oc", "u1", "+u1", "u3", "u0", "+u3", "+u0", "+gc2",
    "+u2", "u3", "+u3", "u2", "+u2", "finish1", "u3", "finish0", "+u3", "u2", "+u2", "+gc0", "+gc1", "bout", "gin", "finish3", "finish2",
)
ORDERS = ((0, 2, 1), (1, 0, 2), (0, 1, 2), (1, 0, 2))


def small_kernel(seqs, shard, *refs):
    own, oth, ups, outs = refs[:seqs], refs[seqs : 2 * seqs], refs[2 * seqs : -2], refs[-2:]
    total = sum(r[...] for r in own) + sum(r[...] for r in oth)
    up = sum(r[...] for r in ups)
    d = total.shape[1]
    ff = up.shape[1] // 2
    for side, out_ref in enumerate(outs):
        out_ref[0:6, :] = total[0:6]
        at = slice(side * shard, (side + 1) * shard)
        out_ref[6:7, :] = jnp.concatenate([total[6:7, at], total[7:8, at], jnp.zeros((1, d - 2 * shard), F32)], axis=1)
        for k in range(ff // d):
            out_ref[7 + k : 8 + k, :] = up[:, side * ff + k * d : side * ff + (k + 1) * d]


def small_sums(shard, own, oth, ups):
    seqs, d = len(own), own[0].shape[1]
    rows = 7 + ups[0].shape[1] // 2 // d
    operands = [*own, *oth, *ups]
    return call(functools.partial(small_kernel, seqs, shard), "small_sums", (), operands, [((rows, d), F32)] * 2)


def on_device(groups, tp, block_input, pieces, gain_one, shift_one, query_weight, query_bias, key_weight, value_weight, value_bias,
              out_weight, out_bias, gain_two, shift_two, up_weight, up_bias, down_weight, down_bias, cotangent):
    d = block_input.shape[1]
    shard = query_weight.shape[1]
    ff = up_weight.shape[1]
    seqs = pieces.shape[0] // 2
    core = lax.axis_index("tp") & 1
    group = lax.axis_index("dp")
    bits = list(range(groups.bit_length() - 1))
    place = jnp.stack([core * seqs, core] + [(group >> bit) & 1 for bit in bits]).astype(jnp.int32)

    def other_core(values):
        return lax.ppermute(values, "tp", swap(tp, 1))

    def other_chip(values):
        return lax.ppermute(values, "tp", swap(tp, 2))

    def next_group(values):
        return lax.ppermute(values, "dp", swap(groups, 1))

    chain = Chain()
    weights = (query_weight.T, key_weight.T, value_weight.T, out_weight)
    core_weights = [other_core(w) for w in weights]
    small = jnp.concatenate([gain_one, shift_one, out_bias, gain_two, shift_two, down_bias, up_bias, query_bias, value_bias])
    first = other_chip(jnp.where(place[BITS] == 0, weights[0], weights[1]))
    last_v, last_o = other_chip(weights[2]), other_chip(weights[3])
    vectors, biases = chain.run(functools.partial(gather_vectors, shard=shard, d=d, ff=ff), small)
    biases_b, biases_x = other_core(biases), other_chip(biases)
    w_own, n1, qkv_own = chain.run(functools.partial(project_own, seqs * SEQ_LEN), place, block_input, vectors, biases, biases_b, (*weights[:3], *core_weights[:3]))
    first, biases_x = chain.after((first, biases_x))
    second = next_group(first)
    mixed, logs_own, part, wo_own = chain.run(attend_own, place, pieces, qkv_own, weights[3], core_weights[3], need=(first, biases_x))
    up_weight, down_weight = chain.after((up_weight, down_weight))
    up_b, down_b = other_core(up_weight), other_core(down_weight)
    joined = chain.run(join_weights, place, first, second, last_v, biases_x)
    w_oth, qkv_oth, logs_oth, mixed_oth = chain.run(attend_other, place, pieces, joined, other_core(joined), n1)
    last_o = chain.after(last_o)
    wo_oth, middle, n2 = chain.run(middle_rows, place, pieces, last_o, other_core(last_o), block_input, mixed_oth, part, vectors)

    sent, got, made = {}, {}, {}
    units = {}

    def unit(name, at, send, keep):
        order = [*ORDERS[at], *bits[len(ORDERS[at]) :]]
        units[name] = (SumsUnit if name == "u2" else Unit)(groups, order, place, send, keep)

    def take(name):
        u = units[name]
        u.keep, u.got = tie((u.keep, u.got), chain.last)
        if name == "u2" and u.step == u.middle - 1:
            u.sums, u.more = tie((made["small"], got["sc"][0]), chain.last)
        u.take()
        chain.last = u.keep

    def begin(name):
        u = units[name]
        u.send = chain.after(u.send)
        with jax.named_scope(f"send_{name}_{u.step}"):
            u.start()

    def complete(name):
        u = units[name]
        while u.step < u.last:
            take(name)
            begin(name)

    def mlp(part):
        first, count = (0, 1) if part == 0 else (1, seqs - 1)
        out = chain.run(functools.partial(mlp_rows, first, count), place, pieces, n2, cotangent, biases, biases_b, up_weight, up_b, down_weight, down_b)
        for key, value in zip(("active", "hidden", "branch", "sums", "n2"), out):
            made.setdefault(key, []).append(value)
        made.setdefault("gn2", []).extend(out[5:])

    def sides(at):
        return (made["hidden"], made["n2"]) if at == 0 else (made["active"], made["branch"])

    def step(name):
        kind, at = name.rstrip("0123456789"), name[len(name.rstrip("0123456789")) :]
        at = int(at) if at else 0
        if kind == "mlp":
            mlp(at)
        elif kind == "down":
            made["down"] = chain.run(down_rows, down_weight, down_b, made["active"])
        elif kind == "gs":
            sent[f"cb{at}"] = chain.run(functools.partial(grad_sent, 1), *sides(at))
        elif kind == "gk":
            unit(f"u{at}", at, *chain.run(functools.partial(grad_kept, ORDERS[at][0]), place, *sides(at), got[f"cb{at}"][0]))
        elif kind == "ob":
            made[f"ob{at}"] = chain.run(functools.partial(own_back, at), place, pieces, cotangent, middle, made["gn2"][at], got[f"G{at}"][0], vectors,
                                        qkv_own, logs_own, mixed, w_own, wo_own)
        elif kind in ("ao", "ak"):
            kinds = (0, 1) if at == 0 else (2, 3)
            owns = [made[f"ob{s}"] for s in range(seqs)]
            operands = ([o[1] for o in owns], [o[2] for o in owns], n1)
            if kind == "ao":
                sent[f"ca{at}"] = chain.run(functools.partial(attn_sent, kinds), *operands)
            else:
                unit(f"u{2 + at}", 2 + at, *chain.run(functools.partial(attn_kept, kinds, ORDERS[2 + at][0]), place, *operands, got[f"ca{at}"][0]))
        elif kind == "xb":
            own = made[f"ob{at}"]
            made[f"xb{at}"] = chain.run(functools.partial(other_back, at), place, pieces, block_input, own[0], own[2], own[3], vectors,
                                        qkv_oth, logs_oth, w_oth, wo_oth)
            sent[f"gc{at}"] = made[f"xb{at}"][:1]
        elif kind == "sums":
            made["small"], more = chain.run(functools.partial(small_sums, shard), [made[f"ob{s}"][4] for s in range(seqs)],
                                            [made[f"xb{s}"][1] for s in range(seqs)], made["sums"])
            sent["sc"] = [more]
        elif kind == "out":
            sent["oc"] = chain.run(output_rows, place, pieces, middle, vectors, made["down"][0], got["D0"][0])
        elif kind == "gin":
            made["input_grad"] = chain.run(both_cores, place, sum((list(sent[f"gc{s}"]) for s in range(seqs)), []), sum((list(got[f"gc{s}"]) for s in range(seqs)), []))
        elif kind == "bout":
            made["block_output"] = chain.run(both_cores, place, sent["oc"], got["oc"])
        elif kind == "u":
            take(f"u{at}")
        elif kind == "finish":
            name = f"u{at}"
            complete(name)
            u = units[name]
            if at == 0:
                out = chain.run(functools.partial(finish, finish_up_kernel, "finish_up", u.order[0], (d, ff)), place, u.keep, u.got)
            elif at == 1:
                out = chain.run(functools.partial(finish, finish_down_kernel, "finish_down", u.order[0], (ff, d)), place, u.keep, u.got)
            elif "late" not in made:
                made["late"] = True
                return
            else:
                a, b = units["u2"], units["u3"]
                out = chain.run(functools.partial(finish_attn, a.order[0], b.order[0], shard), place, a.keep, a.got, a.sums, b.keep, b.got)
                made["attn"], made["flat"] = out[:4], out[4:]
            made[name] = out

    def start(name):
        if name[0] == "u":
            return begin(name)
        if name[0] == "G":
            sent[name] = [made["gn2"][int(name[1:])]]
        elif name[0] == "D":
            sent[name] = made["down"]
        if name[0] in "GD":
            move = other_chip
        else:
            move = other_core
        sent[name] = chain.after(sent[name])
        with jax.named_scope(f"send_{name}"):
            got[name] = [move(value) for value in sent[name]]

    for name in SCHEDULE:
        if name[0] == "+":
            start(name[1:])
        elif name[0] == "-":
            chain.need(units[name[1:]].got if name[1] == "u" else got[name[1:]])
        else:
            step(name)
    totals, input_grad, block_output = made["flat"], made["input_grad"], made["block_output"]
    up_grad, down_grad, attn = made["u0"], made["u1"], made["attn"]
    return (
        block_output,
        input_grad,
        totals[0],
        totals[1],
        attn[0].T,
        totals[6],
        attn[1].T,
        attn[2].T,
        totals[7],
        attn[3],
        totals[2],
        totals[3],
        totals[4],
        up_grad,
        totals[8],
        down_grad,
        totals[5],
    )


def solution(mesh):
    rows, cols, col, copied = P("dp", None), P(None, "tp"), P("tp"), P()
    return jax.shard_map(
        functools.partial(on_device, mesh.shape["dp"], mesh.shape["tp"]),
        mesh=mesh,
        in_specs=(rows, rows, copied, copied, cols, col, cols, cols, col, P("tp", None), copied, copied, copied, cols, col, P("tp", None), copied, rows),
        out_specs=(rows, rows, copied, copied, cols, col, cols, cols, col, P("tp", None), copied, copied, copied, cols, col, P("tp", None), copied),
        check_vma=False,
    )
```

```python
import functools

import jax
import jax.numpy as jnp
from jax import lax
from jax.experimental import pallas as pl
from jax.experimental.pallas import tpu as pltpu
from jax.sharding import PartitionSpec as P

HEAD = 64
SEQ_LEN = 256
EPS = 1e-06
SCALE = 0.125
NEG = -1000000000.0
ROOT_HALF = 0.7071067811865476
INV_ROOT_TAU = 0.3989422804014327
F32 = jnp.float32
BF16 = jnp.bfloat16
VMEM_LIMIT = 14 * 1024 * 1024


def dot_nn(a, b):
    return lax.dot_general(a, b, (((1,), (0,)), ((), ())), preferred_element_type=F32)


def dot_nt(a, b):
    return lax.dot_general(a, b, (((1,), (1,)), ((), ())), preferred_element_type=F32)


def dot_tn(a, b):
    return lax.dot_general(a, b, (((0,), (0,)), ((), ())), preferred_element_type=F32)


def standardize(values):
    centred = values - jnp.mean(values, axis=-1, keepdims=True)
    spread = jnp.mean(centred * centred, axis=-1, keepdims=True)
    scaler = lax.rsqrt(spread + EPS)
    return centred * scaler, scaler


def norm_back(grad_normed, gain, normed, scaler):
    scaled = grad_normed * gain
    centred = scaled - jnp.mean(scaled, axis=-1, keepdims=True)
    return scaler * (centred - normed * jnp.mean(scaled * normed, axis=-1, keepdims=True))


def gelu_parts(hidden):
    cumul = 0.5 * (1.0 + lax.erf(hidden * ROOT_HALF))
    return hidden * cumul, cumul + hidden * (jnp.exp(-0.5 * hidden * hidden) * INV_ROOT_TAU)


def segment_at(pieces_ref, row, amount, shape, axis):
    place = lax.broadcasted_iota(jnp.int32, shape, axis)
    end = jnp.int32(0)
    segment = jnp.zeros(shape, jnp.int32)
    for k in range(amount):
        end = end + pieces_ref[row, k]
        segment = segment + (place >= end).astype(jnp.int32)
    return segment


def mask_bias(pieces_ref, row, amount):
    shape = (SEQ_LEN, SEQ_LEN)
    down = segment_at(pieces_ref, row, amount, shape, 0)
    across = segment_at(pieces_ref, row, amount, shape, 1)
    same = (down == across) & (across < amount - 1)
    diagonal = lax.broadcasted_iota(jnp.int32, shape, 0) == lax.broadcasted_iota(jnp.int32, shape, 1)
    return jnp.where(same | diagonal, 0.0, NEG).astype(F32)


def keep_rows(pieces_ref, row, amount):
    segment = segment_at(pieces_ref, row, amount, (SEQ_LEN, 1), 0)
    return (segment < amount - 1).astype(F32)


def head_lanes(shape):
    return lax.broadcasted_iota(jnp.int32, shape, 1) < HEAD


def both_sides(values, low_lanes):
    zero = jnp.zeros_like(values)
    return jnp.concatenate([jnp.where(low_lanes, values, zero), jnp.where(low_lanes, zero, values)], axis=0)


def attend(qkv_ref, rows, bias, width):
    low_lanes = head_lanes((SEQ_LEN, 2 * HEAD))
    lane = lax.broadcasted_iota(jnp.int32, (SEQ_LEN, 2 * HEAD), 1)
    logs = jnp.zeros((SEQ_LEN, 2 * HEAD), F32)
    pairs = range(width // (2 * HEAD))
    where = [[slice(k * width + p * 2 * HEAD, k * width + (p + 1) * 2 * HEAD) for k in range(3)] for p in pairs]
    scores = [dot_nt(both_sides(qkv_ref[rows, where[p][0]], low_lanes), qkv_ref[rows, where[p][1]]) for p in pairs]
    mixed = []
    for p in pairs:
        probs = []
        for side in range(2):
            mine = scores[p][side * SEQ_LEN : (side + 1) * SEQ_LEN] + bias
            largest = jnp.max(mine, axis=-1, keepdims=True)
            weights = jnp.exp(mine - largest)
            totals = jnp.sum(weights, axis=-1, keepdims=True)
            probs.append((weights * (1.0 / totals)).astype(BF16))
            logs = jnp.where(lane == 2 * p + side, largest + jnp.log(totals), logs)
        out = dot_nn(jnp.concatenate(probs, axis=0), qkv_ref[rows, where[p][2]])
        mixed.append(jnp.where(low_lanes, out[:SEQ_LEN], out[SEQ_LEN:]).astype(BF16))
    return jnp.concatenate(mixed, axis=1), logs


def held(*_):
    return pl.BlockSpec(memory_space=pltpu.VMEM)


def seq_rows(seq):
    return pl.ds(pl.multiple_of(seq * SEQ_LEN, SEQ_LEN), SEQ_LEN)


def anywhere(*_):
    return pl.BlockSpec(memory_space=pltpu.HBM)


def call(kernel, name, scalars, operands, outs, grid=(1,), scratch=(), loose=0, free=0, limit=VMEM_LIMIT, us=1.0):
    return pl.pallas_call(
        kernel,
        grid_spec=pltpu.PrefetchScalarGridSpec(
            num_scalar_prefetch=len(scalars), grid=grid, in_specs=[anywhere()] * loose + [held()] * (len(operands) - loose), out_specs=[anywhere()] * free + [held()] * (len(outs) - free), scratch_shapes=list(scratch)),
        out_shape=[jax.ShapeDtypeStruct(shape, dtype) for shape, dtype in outs],
        compiler_params=pltpu.CompilerParams(vmem_limit_bytes=limit),
        cost_estimate=pl.CostEstimate(flops=int(us * 5e8), bytes_accessed=int(us * 1e6), transcendentals=0),
        name=name,
    )(*scalars, *operands)


def copy_all(copies, sems):
    started = [pltpu.make_async_copy(source, target, sems.at[at]) for at, (source, target) in enumerate(copies)]
    for copy in started:
        copy.start()
    return started


def column_sum(values):
    return jnp.sum(values.reshape(values.shape[0] // 8, 8, values.shape[1]), axis=0)


VECTORS = 6
BITS = 2
TAIL = 16


def vectors_kernel(shard, small_ref, vectors_ref, row_ref):
    d = vectors_ref.shape[1]

    def vector(at, size):
        return small_ref[pl.ds(at, size)].reshape(1, size)

    vectors_ref[...] = jnp.zeros_like(vectors_ref)
    for k in range(VECTORS):
        vectors_ref[k : k + 1, :] = vector(k * d, d)
    ff = row_ref.shape[1] - 4 * shard
    row_ref[:, 4 * shard :] = vector(VECTORS * d, ff)
    zero = jnp.zeros((1, shard), F32)
    at = VECTORS * d + ff
    row_ref[:, : 4 * shard] = jnp.concatenate([vector(at, shard), zero, vector(at + shard, shard), zero], axis=1)


def gather_vectors(small, shard, d, ff):
    return call(functools.partial(vectors_kernel, shard), "vectors", (), (small,), [((8, d), F32), ((1, 4 * shard + ff), F32)])


def join_kernel(place_ref, first_ref, second_ref, v_ref, row_ref, out_ref):
    shard, d = first_ref.shape
    out_ref[pl.ds(pl.multiple_of(place_ref[BITS] * shard, shard), shard), :] = first_ref[...]
    out_ref[pl.ds(pl.multiple_of((1 - place_ref[BITS]) * shard, shard), shard), :] = second_ref[...]
    out_ref[2 * shard : 3 * shard, :] = v_ref[...]
    rest = row_ref[:, : 4 * shard]
    rows = []
    for _ in range(3):
        part = rest.astype(BF16).astype(F32)
        rows.append(part)
        rest = rest - part
    rows.append(jnp.zeros((TAIL - 3, 4 * shard), F32))
    out_ref[3 * shard :, : 4 * shard] = jnp.concatenate(rows, axis=0).astype(BF16)


def join_weights(place, first, second, v, row):
    shard, d = first.shape
    return call(join_kernel, "join", (place,), (first, second, v, row), [((3 * shard + TAIL, d), BF16)])[0]


def spread_bias(a, b, shard):
    return a + jnp.concatenate([jnp.zeros((1, shard), F32), b[:, : 3 * shard]], axis=1)


def project(lowered, w_ref, bias, qkv_ref, at, width):
    for k in range(3):
        proj = dot_nt(lowered, w_ref[k * width : (k + 1) * width, :])
        if k == 0:
            proj = (proj + bias[:, :width]).astype(BF16) * jnp.asarray(SCALE, BF16)
        elif k == 2:
            proj = proj + bias[:, width:]
        qkv_ref[at, k * width : (k + 1) * width] = proj.astype(BF16)


def project_kernel(shard, place_ref, x_ref, vectors_ref, a_ref, b_ref, *refs):
    w_refs, (w_ref, normed_ref, qkv_ref) = refs[:6], refs[6:]
    step = pl.program_id(0)
    width = 2 * shard

    @pl.when(step == 0)
    def _():
        for k, ref in enumerate(w_refs):
            to = (k % 3) * width + (k // 3) * shard
            w_ref[to : to + shard, :] = ref[...]

    normed, _ = standardize(x_ref[seq_rows(place_ref[0] + step), :].astype(F32))
    lowered = (normed * vectors_ref[0:1, :] + vectors_ref[1:2, :]).astype(BF16)
    at = seq_rows(step)
    normed_ref[at, :] = lowered
    bias = spread_bias(a_ref[:, : 4 * shard], b_ref[:, : 4 * shard], shard)
    project(lowered, w_ref, bias, qkv_ref, at, width)


def project_own(rows, place, x, vectors, a, b, weights):
    shard, d = weights[0].shape
    outs = [((6 * shard, d), BF16), ((rows, d), BF16), ((rows, 6 * shard), BF16)]
    return call(functools.partial(project_kernel, shard), "project_own", (place,), (x, vectors, a, b, *weights), outs, (rows // SEQ_LEN,), us=3.5)


def attend_kernel(amount, width, place_ref, pieces_ref, qkv_ref, wa_ref, wb_ref, mixed_ref, logs_ref, part_ref, wo_ref):
    step = pl.program_id(0)

    @pl.when(step == 0)
    def _():
        wo_ref[: width // 2, :] = wa_ref[...]
        wo_ref[width // 2 :, :] = wb_ref[...]

    at = seq_rows(step)
    mixed, logs = attend(qkv_ref, at, mask_bias(pieces_ref, place_ref[0] + step, amount), width)
    logs_ref[pl.ds(pl.multiple_of(step * 8, 8), 8), :] = logs.T[:8, :]
    mixed_ref[at, :] = mixed
    part_ref[at, :] = dot_nn(mixed, wo_ref[...])


def attend_own(place, pieces, qkv, wa, wb):
    seqs, amount = pieces.shape[0] // 2, pieces.shape[1]
    width, d = 2 * wa.shape[0], wa.shape[1]
    rows = seqs * SEQ_LEN
    outs = [((rows, width), BF16), ((seqs * 8, SEQ_LEN), F32), ((rows, d), F32), ((width, d), BF16)]
    return call(functools.partial(attend_kernel, amount, width), "attend_own", (place, pieces), (qkv, wa, wb), outs, (seqs,), us=4.9)


def other_kernel(amount, shard, place_ref, pieces_ref, a_ref, b_ref, normed_in_ref, w_ref, qkv_ref, logs_ref, mixed_ref):
    step = pl.program_id(0)
    width = 2 * shard

    @pl.when(step == 0)
    def _():
        for side, ref in enumerate((a_ref, b_ref)):
            for k in range(3):
                to = k * width + side * shard
                w_ref[to : to + shard, :] = ref[k * shard : (k + 1) * shard, :]

    at = seq_rows(step)
    a, b = (jnp.sum(ref[3 * shard : 3 * shard + 3, : 4 * shard].astype(F32), axis=0, keepdims=True) for ref in (a_ref, b_ref))
    project(normed_in_ref[at, :], w_ref, spread_bias(a, b, shard), qkv_ref, at, width)
    mixed, logs = attend(qkv_ref, at, mask_bias(pieces_ref, place_ref[0] + step, amount), width)
    logs_ref[pl.ds(pl.multiple_of(step * 8, 8), 8), :] = logs.T[:8, :]
    mixed_ref[at, :] = mixed


def attend_other(place, pieces, a, b, normed):
    seqs, amount = pieces.shape[0] // 2, pieces.shape[1]
    shard, d = (a.shape[0] - TAIL) // 3, a.shape[1]
    rows = seqs * SEQ_LEN
    outs = [((6 * shard, d), BF16), ((rows, 6 * shard), BF16), ((seqs * 8, SEQ_LEN), F32), ((rows, 2 * shard), BF16)]
    return call(functools.partial(other_kernel, amount, shard), "attend_other", (place, pieces), (a, b, normed), outs, (seqs,), us=6.0)


def middle_kernel(amount, place_ref, pieces_ref, wa_ref, wb_ref, x_ref, mixed_ref, part_in_ref, vectors_ref, w_ref, middle_ref, normed_ref, sum_ref):
    step = pl.program_id(0)
    shard = wa_ref.shape[0]
    first = place_ref[0] * SEQ_LEN

    @pl.when(step == 0)
    def _():
        w_ref[:shard, :] = wa_ref[...]
        w_ref[shard:, :] = wb_ref[...]

    at = seq_rows(step)
    sum_ref[...] = dot_nn(mixed_ref[at, :], w_ref[...])
    keep_all = keep_rows(pieces_ref, place_ref[0] + step, amount)
    block = 64
    for r in range(0, SEQ_LEN, block):
        here = pl.ds(pl.multiple_of(step * SEQ_LEN + r, block), block)
        added = part_in_ref[here, :] + sum_ref[r : r + block, :] + vectors_ref[2:3, :]
        middle = x_ref[pl.ds(pl.multiple_of(first + step * SEQ_LEN + r, block), block), :].astype(F32) + keep_all[r : r + block] * added
        middle_ref[here, :] = middle
        normed, _ = standardize(middle)
        normed_ref[here, :] = (normed * vectors_ref[3:4, :] + vectors_ref[4:5, :]).astype(BF16)


def middle_rows(place, pieces, wa, wb, x, mixed, part, vectors):
    (rows, width), d = mixed.shape, x.shape[1]
    outs = [((width, d), BF16), ((rows, d), F32), ((rows, d), BF16)]
    return call(functools.partial(middle_kernel, pieces.shape[1]), "middle", (place, pieces), (wa, wb, x, mixed, part, vectors), outs, (rows // SEQ_LEN,),
                [pltpu.VMEM((SEQ_LEN, d), F32)], us=3.0)


def mlp_kernel(amount, first, seqs, place_ref, pieces_ref, n2_ref, cot_ref, ba_ref, bb_ref, upa_ref, upb_ref, dna_ref, dnb_ref,
               active_ref, gh_ref, gb_ref, sums_ref, n2_out_ref, *gn2_refs):
    ff = upa_ref.shape[1]
    skip = ba_ref.shape[1] - ff
    block = 256 if ff % 256 == 0 else ff
    total = [None] * (2 * ff // block)
    for s in range(seqs):
        rows = slice(s * SEQ_LEN, (s + 1) * SEQ_LEN)
        here = slice((first + s) * SEQ_LEN, (first + s + 1) * SEQ_LEN)
        keep = keep_rows(pieces_ref, place_ref[0] + first + s, amount)
        branch = (keep * cot_ref[seq_rows(place_ref[0] + first + s), :].astype(F32)).astype(BF16)
        gb_ref[rows, :] = branch
        n2 = n2_ref[here, :]
        n2_out_ref[rows, :] = n2
        for side, (up_ref, dn_ref, bias_ref) in enumerate(((upa_ref, dna_ref, ba_ref), (upb_ref, dnb_ref, bb_ref))):
            for j in range(0, ff, block):
                at = slice(side * ff + j, side * ff + j + block)
                hidden = dot_nn(n2, up_ref[:, j : j + block]) + bias_ref[:, skip + j : skip + j + block]
                active, slope = gelu_parts(hidden)
                active_ref[rows, at] = active.astype(BF16)
                grad_active = dot_nt(branch, dn_ref[j : j + block, :])
                grad_hidden = (grad_active * slope).astype(BF16)
                gh_ref[rows, at] = grad_hidden
                part = jnp.sum(grad_hidden.astype(F32), axis=0, keepdims=True)
                k = at.start // block
                total[k] = part if total[k] is None else total[k] + part
        gn2_refs[s][...] = (dot_nt(gh_ref[rows, :ff], upa_ref[...]) + dot_nt(gh_ref[rows, ff:], upb_ref[...])).astype(BF16)
    for k, part in enumerate(total):
        sums_ref[:, k * block : (k + 1) * block] = part


def mlp_rows(first, seqs, place, pieces, n2, cot, bias, bias_b, upa, upb, dna, dnb):
    d, ff = upa.shape
    rows = seqs * SEQ_LEN
    outs = [((rows, 2 * ff), BF16), ((rows, 2 * ff), BF16), ((rows, d), BF16), ((1, 2 * ff), F32), ((rows, d), BF16)] + [((SEQ_LEN, d), BF16)] * seqs
    return call(functools.partial(mlp_kernel, pieces.shape[1], first, seqs), "mlp", (place, pieces), (n2, cot, bias, bias_b, upa, upb, dna, dnb), outs, us=2.7 * seqs)


def down_kernel(count, dna_ref, dnb_ref, *refs):
    ff = dna_ref.shape[0]
    out_ref = refs[-1]
    at = 0
    for active_ref in refs[:count]:
        for r in range(0, active_ref.shape[0], SEQ_LEN):
            rows = slice(r, r + SEQ_LEN)
            out_ref[at : at + SEQ_LEN, :] = (dot_nn(active_ref[rows, :ff], dna_ref[...]) + dot_nn(active_ref[rows, ff:], dnb_ref[...])).astype(BF16)
            at += SEQ_LEN


def down_rows(dna, dnb, actives):
    rows, d = sum(a.shape[0] for a in actives), dna.shape[1]
    return call(functools.partial(down_kernel, len(actives)), "down", (), (dna, dnb, *actives), [((rows, d), BF16)], us=2.0)


def sent_kernel(count, side, *refs):
    out_ref = refs[-1]
    size = out_ref.shape[0]
    block = 256 if size % 256 == 0 else size
    for j in range(0, size, block):
        at = slice(side * size + j, side * size + j + block)
        total = sum(dot_tn(refs[k][:, at], refs[count + k][...]) for k in range(count))
        out_ref[j : j + block, :] = total.astype(BF16)


def grad_sent(side, lefts, rights):
    size, d = lefts[0].shape[1] // 2, rights[0].shape[1]
    return call(functools.partial(sent_kernel, len(lefts), side), "grad_sent", (), (*lefts, *rights), [((size, d), BF16)], us=1.1)


def kept_kernel(count, bit, place_ref, *refs):
    add_ref, send_ref, keep_ref = refs[-3:]
    half = keep_ref.shape[0]
    for which, out_ref in enumerate((send_ref, keep_ref)):
        mine = place_ref[BITS + bit] if which else 1 - place_ref[BITS + bit]
        at = pl.ds(pl.multiple_of(mine * half, half), half)
        total = sum(dot_tn(refs[k][:, at], refs[count + k][...]) for k in range(count))
        out_ref[...] = (total + add_ref[at, :].astype(F32)).astype(BF16)


def grad_kept(bit, place, lefts, rights, add):
    half, d = lefts[0].shape[1] // 4, rights[0].shape[1]
    return call(functools.partial(kept_kernel, len(lefts), bit), "grad_kept", (place,), (*lefts, *rights, add), [((half, d), BF16)] * 2, us=1.7)


def attn_dots(refs, attns, n1_ref, seqs, shard, side, kind):
    width = 2 * shard
    at = slice(kind * width + side * shard, kind * width + (side + 1) * shard)
    rights = [attns[s][...] if kind == 3 else n1_ref[s * SEQ_LEN : (s + 1) * SEQ_LEN, :] for s in range(seqs)]
    return sum(dot_tn(refs[s][:, at], rights[s]) for s in range(seqs))


def attn_sent_kernel(seqs, kinds, *refs):
    out_ref = refs[-1]
    shard = out_ref.shape[0] // len(kinds)
    for k, kind in enumerate(kinds):
        out_ref[k * shard : (k + 1) * shard, :] = attn_dots(refs[:seqs], refs[seqs : 2 * seqs], refs[2 * seqs], seqs, shard, 1, kind).astype(BF16)


def attn_sent(kinds, lefts, attns, n1):
    shard, d = lefts[0].shape[1] // 8, n1.shape[1]
    return call(functools.partial(attn_sent_kernel, len(lefts), kinds), "attn_sent", (), (*lefts, *attns, n1), [((len(kinds) * shard, d), BF16)], us=0.9)


def attn_kept_kernel(seqs, kinds, bit, place_ref, *refs):
    add_ref, send_ref, keep_ref, both_ref = refs[-4:]
    shard = keep_ref.shape[0]
    for which, kind in enumerate(kinds):
        total = attn_dots(refs[:seqs], refs[seqs : 2 * seqs], refs[2 * seqs], seqs, shard, 0, kind)
        at = slice(which * shard, (which + 1) * shard)
        both_ref[at, :] = (total + add_ref[at, :].astype(F32)).astype(BF16)
    mine = place_ref[BITS + bit]
    for out_ref, chosen in ((keep_ref, mine), (send_ref, 1 - mine)):
        out_ref[...] = both_ref[pl.ds(pl.multiple_of(chosen * shard, shard), shard), :]


def attn_kept(kinds, bit, place, lefts, attns, n1, add):
    shard, d = lefts[0].shape[1] // 8, n1.shape[1]
    return call(functools.partial(attn_kept_kernel, len(lefts), kinds, bit), "attn_kept", (place,), (*lefts, *attns, n1, add), [((shard, d), BF16)] * 2,
                scratch=[pltpu.VMEM((2 * shard, d), BF16)], us=1.2)


def attend_back(qkv_ref, rows, gm_ref, logs_ref, first, bias, width, grads_ref):
    low_lanes = head_lanes((SEQ_LEN, 2 * HEAD))
    pairs = range(width // (2 * HEAD))
    where = [[slice(k * width + p * 2 * HEAD, k * width + (p + 1) * 2 * HEAD) for k in range(3)] for p in pairs]
    scores = [dot_nt(both_sides(qkv_ref[rows, where[p][1]], low_lanes), qkv_ref[rows, where[p][0]]) for p in pairs]
    grad_probs = [dot_nt(both_sides(qkv_ref[rows, where[p][2]], low_lanes), gm_ref[:, where[p][0]]) for p in pairs]
    for p in pairs:
        probs, grad_scores = [], []
        for side in range(2):
            mine = slice(side * SEQ_LEN, (side + 1) * SEQ_LEN)
            head = first + 2 * p + side
            prob = jnp.exp(scores[p][mine] + bias - logs_ref[head : head + 1, :])
            inner = jnp.sum(grad_probs[p][mine] * prob, axis=0, keepdims=True)
            grad_scores.append((prob * (grad_probs[p][mine] - inner)).astype(BF16))
            probs.append(prob.astype(BF16))
        grad_key = dot_nn(jnp.concatenate(grad_scores, axis=0), qkv_ref[rows, where[p][0]])
        grad_value = dot_nn(jnp.concatenate(probs, axis=0), gm_ref[:, where[p][0]])
        grad_query = dot_tn(jnp.concatenate(grad_scores, axis=1), qkv_ref[rows, where[p][1]])
        grads_ref[:, where[p][0]] = (jnp.where(low_lanes, grad_query[:SEQ_LEN], grad_query[SEQ_LEN:]) * SCALE).astype(BF16)
        grads_ref[:, where[p][1]] = jnp.where(low_lanes, grad_key[:SEQ_LEN], grad_key[SEQ_LEN:]).astype(BF16)
        grads_ref[:, where[p][2]] = jnp.where(low_lanes, grad_value[:SEQ_LEN], grad_value[SEQ_LEN:]).astype(BF16)


def own_back_kernel(amount, seq, place_ref, pieces_ref, cot_ref, middle_ref, own_ref, got_ref, vectors_ref, qkv_ref, logs_ref, mixed_ref, w_ref, wo_ref,
                    grad_ref, all_ref, attn_ref, part_ref, sums_ref, gm_ref):
    row = place_ref[0] + seq
    width = mixed_ref.shape[1]
    d = cot_ref.shape[1]
    keep_all = keep_rows(pieces_ref, row, amount)
    sums = [jnp.zeros((8, d), F32)] * 4
    block = 32
    for r in range(0, SEQ_LEN, block):
        at = slice(r, r + block)
        keep = keep_all[at]
        cot = cot_ref[pl.ds(pl.multiple_of(row * SEQ_LEN + r, block), block), :].astype(F32)
        gn2 = own_ref[at, :].astype(F32) + got_ref[at, :].astype(F32)
        normed, scaler = standardize(middle_ref[seq * SEQ_LEN + r : seq * SEQ_LEN + r + block, :])
        grad_middle = cot + norm_back(gn2, vectors_ref[3:4, :], normed, scaler)
        attn = (keep * grad_middle).astype(BF16)
        attn_ref[at, :] = attn
        grad_ref[at, :] = grad_middle
        terms = (attn.astype(F32), gn2 * normed, gn2, (keep * cot).astype(BF16).astype(F32))
        sums = [s + column_sum(t) for s, t in zip(sums, terms)]
    sums_ref[...] = jnp.zeros_like(sums_ref)
    for k in range(4):
        sums_ref[2 + k : 3 + k, :] = jnp.sum(sums[k], axis=0, keepdims=True)
    gm_ref[...] = dot_nt(attn_ref[...], wo_ref[...]).astype(BF16)
    rows = slice(seq * SEQ_LEN, (seq + 1) * SEQ_LEN)
    attend_back(qkv_ref, rows, gm_ref, logs_ref, 8 * seq, mask_bias(pieces_ref, row, amount), width, all_ref)
    part_ref[...] = dot_nn(all_ref[:, : 3 * width], w_ref[...])
    all_ref[:, 3 * width :] = mixed_ref[rows, :]
    sums_ref[6:7, :width] = jnp.sum(all_ref[:, :width].astype(F32), axis=0, keepdims=True)
    sums_ref[7:8, :width] = jnp.sum(all_ref[:, 2 * width : 3 * width].astype(F32), axis=0, keepdims=True)


def own_back(seq, place, pieces, cot, middle, own, got, vectors, qkv, logs, mixed, w, wo):
    d, width = cot.shape[1], mixed.shape[1]
    outs = [((SEQ_LEN, d), F32), ((SEQ_LEN, 4 * width), BF16), ((SEQ_LEN, d), BF16), ((SEQ_LEN, d), F32), ((8, d), F32)]
    return call(functools.partial(own_back_kernel, pieces.shape[1], seq), "own_back", (place, pieces),
                (cot, middle, own, got, vectors, qkv, logs, mixed, w, wo), outs, scratch=[pltpu.VMEM((SEQ_LEN, width), BF16)], us=5.2)


def other_back_kernel(amount, seq, place_ref, pieces_ref, x_ref, grad_in_ref, attn_ref, part_ref, vectors_ref, qkv_ref, logs_ref, w_ref, wo_ref,
                      grad_ref, sums_ref, gm_ref, all_ref, sum_ref):
    row = place_ref[0] + seq
    width = gm_ref.shape[1]
    d = x_ref.shape[1]
    bias = mask_bias(pieces_ref, row, amount)
    gm_ref[...] = dot_nt(attn_ref[...], wo_ref[...]).astype(BF16)
    rows = slice(seq * SEQ_LEN, (seq + 1) * SEQ_LEN)
    attend_back(qkv_ref, rows, gm_ref, logs_ref, 8 * seq, bias, width, all_ref)
    sum_ref[...] = dot_nn(all_ref[...], w_ref[...])
    sums = [jnp.zeros((8, d), F32)] * 2
    block = 32
    for r in range(0, SEQ_LEN, block):
        at = slice(r, r + block)
        gn1 = part_ref[at, :] + sum_ref[at, :]
        normed, scaler = standardize(x_ref[pl.ds(pl.multiple_of(row * SEQ_LEN + r, block), block), :].astype(F32))
        grad_ref[at, :] = grad_in_ref[at, :] + norm_back(gn1, vectors_ref[0:1, :], normed, scaler)
        sums = [s + column_sum(t) for s, t in zip(sums, (gn1 * normed, gn1))]
    sums_ref[...] = jnp.zeros_like(sums_ref)
    for k in range(2):
        sums_ref[k : k + 1, :] = jnp.sum(sums[k], axis=0, keepdims=True)


def other_back(seq, place, pieces, x, grad_in, attn, part, vectors, qkv, logs, w, wo):
    d, width = wo.shape[1], wo.shape[0]
    outs = [((SEQ_LEN, d), F32), ((8, d), F32)]
    return call(functools.partial(other_back_kernel, pieces.shape[1], seq), "other_back", (place, pieces),
                (x, grad_in, attn, part, vectors, qkv, logs, w, wo), outs,
                scratch=[pltpu.VMEM((SEQ_LEN, width), BF16), pltpu.VMEM((SEQ_LEN, 3 * width), BF16), pltpu.VMEM((SEQ_LEN, d), F32)], us=4.5)


def output_kernel(amount, place_ref, pieces_ref, middle_ref, vectors_ref, own_ref, got_ref, out_ref):
    block = 64
    for seq in range(out_ref.shape[0] // SEQ_LEN):
        keep_all = keep_rows(pieces_ref, place_ref[0] + seq, amount)
        for r in range(0, SEQ_LEN, block):
            at = slice(seq * SEQ_LEN + r, seq * SEQ_LEN + r + block)
            total = own_ref[at, :].astype(F32) + got_ref[at, :].astype(F32) + vectors_ref[5:6, :]
            out_ref[at, :] = (middle_ref[at, :] + keep_all[r : r + block] * total).astype(BF16)


def output_rows(place, pieces, middle, vectors, own, got):
    return call(functools.partial(output_kernel, pieces.shape[1]), "block_output", (place, pieces),
                (middle, vectors, own, got), [(middle.shape, BF16)], us=1.4)


def both_kernel(count, place_ref, *refs):
    out_ref, sems = refs[-2:]
    size = refs[0].shape[0]
    copies = []
    for k in range(2 * count):
        at = (place_ref[1] if k < count else 1 - place_ref[1]) * count + k % count
        copies.append(pltpu.make_async_copy(refs[k], out_ref.at[pl.ds(pl.multiple_of(at * size, size), size)], sems.at[k]))
        copies[-1].start()
    for copy in copies:
        copy.wait()


def both_cores(place, mine, theirs):
    count = len(mine)
    rows, d = mine[0].shape
    return pl.pallas_call(
        functools.partial(both_kernel, count),
        grid_spec=pltpu.PrefetchScalarGridSpec(
            num_scalar_prefetch=1, grid=(1,), in_specs=[held()] * (2 * count), out_specs=pl.BlockSpec(memory_space=pl.ANY),
            scratch_shapes=[pltpu.SemaphoreType.DMA((2 * count,))]),
        out_shape=jax.ShapeDtypeStruct((2 * count * rows, d), mine[0].dtype),
        compiler_params=pltpu.CompilerParams(vmem_limit_bytes=VMEM_LIMIT),
        cost_estimate=pl.CostEstimate(flops=1, bytes_accessed=1, transcendentals=0),
        name="both_cores",
    )(place, *mine, *theirs)


def swap(size, bit):
    return [(i, i ^ bit) for i in range(size)]


def tie(values, *after):
    return lax.optimization_barrier((values, after))[0]


def merge_kernel(at, place_ref, keep_ref, got_ref, send_ref, out_ref):
    size = out_ref.shape[0]
    for which, ref in enumerate((send_ref, out_ref)):
        bit = place_ref[BITS + at] if which else 1 - place_ref[BITS + at]
        rows = pl.ds(pl.multiple_of(bit * size, size), size)
        ref[...] = (keep_ref[rows, :].astype(F32) + got_ref[rows, :].astype(F32)).astype(BF16)


def merge(bit, place, keep, got):
    rows, d = keep.shape
    half = rows // 2
    if half % 16:
        total = (keep.astype(F32) + got.astype(F32)).astype(BF16)
        low = place[BITS + bit] == 0
        return jnp.where(low, total[half:], total[:half]), jnp.where(low, total[:half], total[half:])
    return call(functools.partial(merge_kernel, bit), "merge", (place,), (keep, got), [((half, d), BF16)] * 2, us=0.6)


def add_kernel(keep_ref, got_ref, out_ref):
    out_ref[...] = (keep_ref[...].astype(F32) + got_ref[...].astype(F32)).astype(out_ref.dtype)


def add(keep, got):
    return call(add_kernel, "add", (), (keep, got), [(keep.shape, keep.dtype)])[0]


def grow_kernel(at, place_ref, keep_ref, got_ref, out_ref):
    size = keep_ref.shape[0]
    out_ref[pl.ds(pl.multiple_of(place_ref[BITS + at] * size, size), size), :] = keep_ref[...]
    out_ref[pl.ds(pl.multiple_of((1 - place_ref[BITS + at]) * size, size), size), :] = got_ref[...]


def grow(bit, place, keep, got):
    rows, d = keep.shape
    if rows % 16:
        return jnp.where(place[BITS + bit] == 0, jnp.concatenate([keep, got]), jnp.concatenate([got, keep]))
    return call(functools.partial(grow_kernel, bit), "grow", (place,), (keep, got), [((2 * rows, d), BF16)])[0]


def finish_up_kernel(at, place_ref, keep_ref, got_ref, out_ref):
    size = keep_ref.shape[0]
    out_ref[:, pl.ds(pl.multiple_of(place_ref[BITS + at] * size, 128), size)] = keep_ref[...].astype(F32).T
    out_ref[:, pl.ds(pl.multiple_of((1 - place_ref[BITS + at]) * size, 128), size)] = got_ref[...].astype(F32).T


def finish_down_kernel(at, place_ref, keep_ref, got_ref, out_ref):
    size = keep_ref.shape[0]
    out_ref[pl.ds(pl.multiple_of(place_ref[BITS + at] * size, size), size), :] = keep_ref[...].astype(F32)
    out_ref[pl.ds(pl.multiple_of((1 - place_ref[BITS + at]) * size, size), size), :] = got_ref[...].astype(F32)


def finish(kernel, name, bit, shape, place, keep, got):
    return call(functools.partial(kernel, bit), name, (place,), (keep, got), [(shape, F32)])[0]


def put_parts(out_ref, at, sums):
    rows, d = sums.shape
    parts = []
    for _ in range(3):
        part = sums.astype(BF16).astype(F32)
        parts.append(part)
        sums = sums - part
    parts.append(jnp.zeros((out_ref.shape[0] - at - 3 * rows, d), F32))
    out_ref[at:, :] = jnp.concatenate(parts, axis=0).astype(BF16)


def get_parts(ref, at, rows):
    parts = ref[at:, :].astype(F32)
    return sum(parts[k * rows : (k + 1) * rows] for k in range(3))


def add_sums_kernel(rows, first, keep_ref, got_ref, sums_ref, more_ref, send_ref, out_ref, total_ref):
    size = keep_ref.shape[0]
    kept = (keep_ref[...].astype(F32) + got_ref[:size, :].astype(F32)).astype(BF16)
    out_ref[...] = kept
    send_ref[:size, :] = kept
    total = sums_ref[...] + (more_ref[...] if first else get_parts(more_ref, size, rows))
    total_ref[...] = total
    put_parts(send_ref, size, total)


def add_sums(keep, got, sums, more):
    first = more is None
    size, d = keep.shape
    rows = sums.shape[0]
    padded = -(-3 * rows // 16) * 16
    return call(functools.partial(add_sums_kernel, rows, not first), "add_sums", (), (keep, got, sums, got if first else more),
                [((size + padded, d), BF16), (keep.shape, BF16), (sums.shape, F32)], us=0.6)


def grow_sums_kernel(at, rows, size, place_ref, keep_ref, got_ref, sums_ref, send_ref, total_ref):
    send_ref[pl.ds(pl.multiple_of(place_ref[BITS + at] * size, size), size), :] = keep_ref[:size, :]
    send_ref[pl.ds(pl.multiple_of((1 - place_ref[BITS + at]) * size, size), size), :] = got_ref[:size, :]
    total = sums_ref[...] + get_parts(got_ref, size, rows)
    total_ref[...] = total
    put_parts(send_ref, 2 * size, total)


def grow_sums(bit, place, keep, got, sums):
    rows, d = sums.shape
    padded = -(-3 * rows // 16) * 16
    size = got.shape[0] - padded
    keep = keep[:size] if size % 16 else keep
    if size % 16:
        low = place[BITS + bit] == 0
        kept = jnp.where(low, jnp.concatenate([keep, got[:size]]), jnp.concatenate([got[:size], keep]))
        parts = got[size:].astype(F32)
        total = sums + sum(parts[k * rows : (k + 1) * rows] for k in range(3))
        rest, split = total, []
        for _ in range(3):
            split.append(lax.reduce_precision(rest, 8, 7))
            rest = rest - split[-1]
        split.append(jnp.zeros((padded - 3 * rows, d), F32))
        return jnp.concatenate([kept, jnp.concatenate(split).astype(BF16)]), kept, total
    send, total = call(functools.partial(grow_sums_kernel, bit, rows, size), "grow_sums", (place,), (keep, got, sums),
                       [((2 * size + padded, d), BF16), (sums.shape, F32)], us=0.7)
    return send, send, total


def attn_out_kernel(first, second, rows, shard, place_ref, keep_ref, got_ref, sums_ref, keep2_ref, got2_ref, q_ref, k_ref, v_ref, o_ref, *refs):
    flat_refs, held_ref, sems = refs[:-2], refs[-2], refs[-1]
    size = held_ref.shape[1]
    todo = []
    for bit, own_ref, other_ref, low_ref, high_ref in ((first, keep_ref, got_ref, q_ref, k_ref), (second, keep2_ref, got2_ref, v_ref, o_ref)):
        mine = place_ref[BITS + bit] == 0
        for ref, one_ref, two_ref in ((own_ref, low_ref, high_ref), (other_ref, high_ref, low_ref)):
            at = len(todo)
            held_ref[at] = ref[:size, :].astype(F32)
            for chosen, out_ref in ((mine, one_ref), (jnp.logical_not(mine), two_ref)):
                @pl.when(chosen)
                def _():
                    pltpu.make_async_copy(held_ref.at[at], out_ref, sems.at[at]).start()

            todo.append(one_ref)
    total = sums_ref[...] + get_parts(got_ref, size, rows)
    for k in range(6):
        flat_refs[k][...] = total[k]
    flat_refs[6][...] = total[6, :shard]
    flat_refs[7][...] = total[6, shard : 2 * shard]
    d = total.shape[1]
    for k in range(7, rows):
        flat_refs[8][pl.ds((k - 7) * d, d)] = total[k]
    for at, out_ref in enumerate(todo):
        pltpu.make_async_copy(held_ref.at[at], out_ref, sems.at[at]).wait()


def finish_attn(first, second, shard, place, keep, got, sums, keep2, got2):
    rows, d = sums.shape
    size = keep2.shape[0]
    outs = [((size, d), F32)] * 4 + [((d,), F32)] * 6 + [((shard,), F32)] * 2 + [(((rows - 7) * d,), F32)]
    return call(functools.partial(attn_out_kernel, first, second, rows, shard), "finish_attn", (place,), (keep, got, sums, keep2, got2), outs, free=4, us=2.0,
                scratch=[pltpu.VMEM((4, size, d), F32), pltpu.SemaphoreType.DMA((4,))])


class Unit:
    def __init__(self, groups, order, place, send, keep):
        self.groups, self.order, self.place = groups, order, place
        self.send, self.keep, self.step = send, keep, 0
        self.middle = len(order) - 1
        self.last = 2 * self.middle

    def start(self):
        at = min(self.step, self.last - self.step)
        self.got = lax.ppermute(self.send, "dp", swap(self.groups, 1 << self.order[at]))

    def take(self):
        if self.step < self.middle - 1:
            self.send, self.keep = merge(self.order[self.step + 1], self.place, self.keep, self.got)
        elif self.step <= self.middle:
            self.send = self.keep = add(self.keep, self.got)
        else:
            self.send = self.keep = grow(self.order[self.last - self.step], self.place, self.keep, self.got)
        self.step += 1


class SumsUnit(Unit):
    def take(self):
        if self.step < self.middle - 1:
            return super().take()
        if self.step <= self.middle:
            more = self.more if self.step == self.middle - 1 else None
            self.send, self.keep, self.sums = add_sums(self.keep, self.got, self.sums, more)
        else:
            self.send, self.keep, self.sums = grow_sums(self.order[self.last - self.step], self.place, self.keep, self.got, self.sums)
        self.step += 1


class Chain:
    def __init__(self):
        self.last = ()

    def run(self, kernel, *args, need=()):
        args = tie(args, self.last, need)
        out = kernel(*args)
        self.last = out
        return out

    def after(self, values):
        return tie(values, self.last)

    def need(self, values):
        self.last = (self.last, values)


SCHEDULE = (
    "mlp0", "mlp1", "+G2", "gs0", "+G1", "+cb0", "gs1", "+cb1", "down", "gk0", "+u0", "gk1", "+u1", "ob2", "+G0", "xb2", "u0", "+u0",
    "ob1", "u1", "+u1", "ob0", "ao1", "+D0", "ao0", "+ca0", "u1", "u0", "+ca1", "+u1", "+u0", "xb0", "ak0", "+u2", "ak1", "u0", "+u0",
    "+u3", "xb1", "u1", "+u1", "sums", "u2", "+u2", "+sc", "u3", "+u3", "out", "u2", "+oc", "u1", "+u1", "u3", "u0", "+u3", "+u0", "+gc2",
    "+u2", "u3", "+u3", "u2", "+u2", "finish1", "u3", "finish0", "+u3", "u2", "+u2", "+gc0", "+gc1", "bout", "gin", "finish3", "finish2",
)
ORDERS = ((0, 2, 1), (1, 0, 2), (0, 1, 2), (1, 0, 2))


def small_kernel(seqs, shard, *refs):
    own, oth, ups, outs = refs[:seqs], refs[seqs : 2 * seqs], refs[2 * seqs : -2], refs[-2:]
    total = sum(r[...] for r in own) + sum(r[...] for r in oth)
    up = sum(r[...] for r in ups)
    d = total.shape[1]
    ff = up.shape[1] // 2
    for side, out_ref in enumerate(outs):
        out_ref[0:6, :] = total[0:6]
        at = slice(side * shard, (side + 1) * shard)
        out_ref[6:7, :] = jnp.concatenate([total[6:7, at], total[7:8, at], jnp.zeros((1, d - 2 * shard), F32)], axis=1)
        for k in range(ff // d):
            out_ref[7 + k : 8 + k, :] = up[:, side * ff + k * d : side * ff + (k + 1) * d]


def small_sums(shard, own, oth, ups):
    seqs, d = len(own), own[0].shape[1]
    rows = 7 + ups[0].shape[1] // 2 // d
    operands = [*own, *oth, *ups]
    return call(functools.partial(small_kernel, seqs, shard), "small_sums", (), operands, [((rows, d), F32)] * 2)


def on_device(groups, tp, block_input, pieces, gain_one, shift_one, query_weight, query_bias, key_weight, value_weight, value_bias,
              out_weight, out_bias, gain_two, shift_two, up_weight, up_bias, down_weight, down_bias, cotangent):
    d = block_input.shape[1]
    shard = query_weight.shape[1]
    ff = up_weight.shape[1]
    seqs = pieces.shape[0] // 2
    core = lax.axis_index("tp") & 1
    group = lax.axis_index("dp")
    bits = list(range(groups.bit_length() - 1))
    place = jnp.stack([core * seqs, core] + [(group >> bit) & 1 for bit in bits]).astype(jnp.int32)

    def other_core(values):
        return lax.ppermute(values, "tp", swap(tp, 1))

    def other_chip(values):
        return lax.ppermute(values, "tp", swap(tp, 2))

    def next_group(values):
        return lax.ppermute(values, "dp", swap(groups, 1))

    chain = Chain()
    weights = (query_weight.T, key_weight.T, value_weight.T, out_weight)
    core_weights = [other_core(w) for w in weights]
    small = jnp.concatenate([gain_one, shift_one, out_bias, gain_two, shift_two, down_bias, up_bias, query_bias, value_bias])
    first, small, place = tie((jnp.where(place[BITS] == 0, weights[0], weights[1]), small, place))
    first = other_chip(first)
    last_v, last_o = other_chip(weights[2]), other_chip(weights[3])
    vectors, biases = chain.run(functools.partial(gather_vectors, shard=shard, d=d, ff=ff), small)
    biases_b, biases_x = other_core(biases), other_chip(biases)
    w_own, n1, qkv_own = chain.run(functools.partial(project_own, seqs * SEQ_LEN), place, block_input, vectors, biases, biases_b, (*weights[:3], *core_weights[:3]))
    first, biases_x = chain.after((first, biases_x))
    second = next_group(first)
    mixed, logs_own, part, wo_own = chain.run(attend_own, place, pieces, qkv_own, weights[3], core_weights[3], need=(first, biases_x))
    up_weight, down_weight = chain.after((up_weight, down_weight))
    up_b, down_b = other_core(up_weight), other_core(down_weight)
    joined = chain.run(join_weights, place, first, second, last_v, biases_x)
    w_oth, qkv_oth, logs_oth, mixed_oth = chain.run(attend_other, place, pieces, joined, other_core(joined), n1)
    last_o = chain.after(last_o)
    wo_oth, middle, n2 = chain.run(middle_rows, place, pieces, last_o, other_core(last_o), block_input, mixed_oth, part, vectors)

    sent, got, made = {}, {}, {}
    units = {}

    def unit(name, at, send, keep):
        order = [*ORDERS[at], *bits[len(ORDERS[at]) :]]
        units[name] = (SumsUnit if name == "u2" else Unit)(groups, order, place, send, keep)

    def take(name):
        u = units[name]
        u.keep, u.got = tie((u.keep, u.got), chain.last)
        if name == "u2" and u.step == u.middle - 1:
            u.sums, u.more = tie((made["small"], got["sc"][0]), chain.last)
        u.take()
        chain.last = u.keep

    def begin(name):
        u = units[name]
        u.send = chain.after(u.send)
        with jax.named_scope(f"send_{name}_{u.step}"):
            u.start()

    def complete(name):
        u = units[name]
        while u.step < u.last:
            take(name)
            begin(name)

    def mlp(part):
        first, count = (0, 1) if part == 0 else (1, seqs - 1)
        out = chain.run(functools.partial(mlp_rows, first, count), place, pieces, n2, cotangent, biases, biases_b, up_weight, up_b, down_weight, down_b)
        for key, value in zip(("active", "hidden", "branch", "sums", "n2"), out):
            made.setdefault(key, []).append(value)
        made.setdefault("gn2", []).extend(out[5:])

    def sides(at):
        return (made["hidden"], made["n2"]) if at == 0 else (made["active"], made["branch"])

    def step(name):
        kind, at = name.rstrip("0123456789"), name[len(name.rstrip("0123456789")) :]
        at = int(at) if at else 0
        if kind == "mlp":
            mlp(at)
        elif kind == "down":
            made["down"] = chain.run(down_rows, down_weight, down_b, made["active"])
        elif kind == "gs":
            sent[f"cb{at}"] = chain.run(functools.partial(grad_sent, 1), *sides(at))
        elif kind == "gk":
            unit(f"u{at}", at, *chain.run(functools.partial(grad_kept, ORDERS[at][0]), place, *sides(at), got[f"cb{at}"][0]))
        elif kind == "ob":
            made[f"ob{at}"] = chain.run(functools.partial(own_back, at), place, pieces, cotangent, middle, made["gn2"][at], got[f"G{at}"][0], vectors,
                                        qkv_own, logs_own, mixed, w_own, wo_own)
        elif kind in ("ao", "ak"):
            kinds = (0, 1) if at == 0 else (2, 3)
            owns = [made[f"ob{s}"] for s in range(seqs)]
            operands = ([o[1] for o in owns], [o[2] for o in owns], n1)
            if kind == "ao":
                sent[f"ca{at}"] = chain.run(functools.partial(attn_sent, kinds), *operands)
            else:
                unit(f"u{2 + at}", 2 + at, *chain.run(functools.partial(attn_kept, kinds, ORDERS[2 + at][0]), place, *operands, got[f"ca{at}"][0]))
        elif kind == "xb":
            own = made[f"ob{at}"]
            made[f"xb{at}"] = chain.run(functools.partial(other_back, at), place, pieces, block_input, own[0], own[2], own[3], vectors,
                                        qkv_oth, logs_oth, w_oth, wo_oth)
            sent[f"gc{at}"] = made[f"xb{at}"][:1]
        elif kind == "sums":
            made["small"], more = chain.run(functools.partial(small_sums, shard), [made[f"ob{s}"][4] for s in range(seqs)],
                                            [made[f"xb{s}"][1] for s in range(seqs)], made["sums"])
            sent["sc"] = [more]
        elif kind == "out":
            sent["oc"] = chain.run(output_rows, place, pieces, middle, vectors, made["down"][0], got["D0"][0])
        elif kind == "gin":
            made["input_grad"] = chain.run(both_cores, place, sum((list(sent[f"gc{s}"]) for s in range(seqs)), []), sum((list(got[f"gc{s}"]) for s in range(seqs)), []))
        elif kind == "bout":
            made["block_output"] = chain.run(both_cores, place, sent["oc"], got["oc"])
        elif kind == "u":
            take(f"u{at}")
        elif kind == "finish":
            name = f"u{at}"
            complete(name)
            u = units[name]
            if at == 0:
                out = chain.run(functools.partial(finish, finish_up_kernel, "finish_up", u.order[0], (d, ff)), place, u.keep, u.got)
            elif at == 1:
                out = chain.run(functools.partial(finish, finish_down_kernel, "finish_down", u.order[0], (ff, d)), place, u.keep, u.got)
            elif "late" not in made:
                made["late"] = True
                return
            else:
                a, b = units["u2"], units["u3"]
                out = chain.run(functools.partial(finish_attn, a.order[0], b.order[0], shard), place, a.keep, a.got, a.sums, b.keep, b.got)
                made["attn"], made["flat"] = out[:4], out[4:]
            made[name] = out

    def start(name):
        if name[0] == "u":
            return begin(name)
        if name[0] == "G":
            sent[name] = [made["gn2"][int(name[1:])]]
        elif name[0] == "D":
            sent[name] = made["down"]
        if name[0] in "GD":
            move = other_chip
        else:
            move = other_core
        sent[name] = chain.after(sent[name])
        with jax.named_scope(f"send_{name}"):
            got[name] = [move(value) for value in sent[name]]

    for name in SCHEDULE:
        if name[0] == "+":
            start(name[1:])
        elif name[0] == "-":
            chain.need(units[name[1:]].got if name[1] == "u" else got[name[1:]])
        else:
            step(name)
    totals, input_grad, block_output = made["flat"], made["input_grad"], made["block_output"]
    up_grad, down_grad, attn = made["u0"], made["u1"], made["attn"]
    return (
        block_output,
        input_grad,
        totals[0],
        totals[1],
        attn[0].T,
        totals[6],
        attn[1].T,
        attn[2].T,
        totals[7],
        attn[3],
        totals[2],
        totals[3],
        totals[4],
        up_grad,
        totals[8],
        down_grad,
        totals[5],
    )


def solution(mesh):
    rows, cols, col, copied = P("dp", None), P(None, "tp"), P("tp"), P()
    return jax.shard_map(
        functools.partial(on_device, mesh.shape["dp"], mesh.shape["tp"]),
        mesh=mesh,
        in_specs=(rows, rows, copied, copied, cols, col, cols, cols, col, P("tp", None), copied, copied, copied, cols, col, P("tp", None), copied, rows),
        out_specs=(rows, rows, copied, copied, cols, col, cols, cols, col, P("tp", None), copied, copied, copied, cols, col, P("tp", None), copied),
        check_vma=False,
    )
```
